32 devices in a mesh: tier: 4 (over y, x), tile: 8 (over z, core).
Axes of the slice: x: 2, y: 2, z: 4, core: 2. Of those that a mesh axis runs over, the one named last changes fastest.
Arguments:
- warming_above_ambient: float32 [4, 16, 256, 2048], P('tier', None, 'tile'), may hold values from -6 to 6
- substance_label: int32 [4, 16, 256, 2048], P('tier', None, 'tile'), may hold values from 0 to 15
- glue_zone_label: int32 [256, 2048], P('tile'), may hold values from 0 to 7
- patch_label_per_cell: int32 [4, 256, 2048], P('tier', 'tile'), may hold values from 0 to 127
- heat_conductance_per_substance: float32 [16], replicated, may hold values from 0.3 to 4
- dissipation_per_patch: float32 [4, 128], P('tier'), may hold values from 0.5 to 5
- glue_sheet_reciprocal_operators: float32 [8, 8, 8], replicated, may hold values from -0.3 to 1.3, as said below
Outputs:
- final_state: float32 [4, 16, 256, 2048], P('tier', None, 'tile')
The draws below stay inside these ranges and needn't reach their ends.
Inputs may be any that keep to these rules, and one draw needn't show every extreme that they name: `glue_sheet_reciprocal_operators`: each matrix has diagonal entries of 0.6 to 1.0 plus a perturbation, and perturbed entries elsewhere.
All inputs are finite; a program needn't handle non-finite values.
Results may differ from the reference program's by a relative error of at most 0.0001.
Values sent between devices are 32-bit elements; how exact they have to be, the bound alone decides.
No kernel may reach another device: no remote copies, remote signals or barrier semaphores. Data moves between devices by JAX's collectives and lax.ppermute only.
A program may use at most 128 MiB of HBM per device.

```python
import math
import jax
import jax.numpy as jnp
from jax import lax

DIE_NUMBER = 4
BLOCK = 8
SHEETS_PER_DIE = 16
GRID_WIDTH_CELLS = 2048
GRID_DEPTH_CELLS = 256
MATERIALS = 16
REGIONS = 8
POWER_TILES = 128
STEPS = 2


def draw_glue_sheet_reciprocal_operators(key, part):
    first, second = jax.random.split(key)
    diag = jax.random.uniform(first, (REGIONS, BLOCK), jnp.float32, 0.6, 1.0)
    other = jnp.clip(0.1 * jax.random.normal(second, (REGIONS, BLOCK, BLOCK), jnp.float32), -0.3, 0.3)
    eye = jnp.eye(BLOCK, dtype=jnp.float32)
    return eye * diag[:, :, None] + other


def place_ends(result, key, least, high):
    extent = result.shape
    index_at = [jax.random.randint(jax.random.fold_in(key, axis), (), 0, extent[axis]) for axis in range(len(extent))]
    result = result.at[tuple(index_at)].set(least)
    longest = extent.index(max(extent))
    index_at[longest] = (index_at[longest] + 1) % extent[longest]
    return result.at[tuple(index_at)].set(high)


def level_of(own_key, extent, pieces, least, largest):
    loudness = 1.0
    for position, blocks in pieces:
        steps = jax.random.uniform(jax.random.fold_in(jax.random.fold_in(own_key, 6), position), (blocks,), jnp.float32, least / len(pieces), largest / len(pieces))
        loudness = loudness * jnp.repeat(jnp.exp(steps), extent[position] // blocks).reshape((-1,) + (1,) * (len(extent) - 1 - position))
    return loudness


def normal_values(key, extent, spread, most, pieces=(), kind=jnp.bfloat16):
    loudness = level_of(key, extent, pieces, -0.22, 0.18) if pieces else 1.0
    drawn = jax.random.normal(key, extent, jnp.float32) * spread * loudness
    return jnp.minimum(jnp.maximum(drawn, -most), most).astype(kind)


def setup_inputs(seed: int = 0) -> dict:
    key_list = jax.random.split(jax.random.key(seed), 8)
    return {
        "warming_above_ambient": normal_values(key_list[0], (DIE_NUMBER, SHEETS_PER_DIE, GRID_DEPTH_CELLS, GRID_WIDTH_CELLS), 1.0, 6.0, ((0, 4), (2, 8)), jnp.float32),
        "substance_label": place_ends(jax.random.randint(key_list[1], (DIE_NUMBER, SHEETS_PER_DIE, GRID_DEPTH_CELLS, GRID_WIDTH_CELLS), 0, MATERIALS), jax.random.fold_in(key_list[1], 1), 0, MATERIALS - 1).astype(jnp.int32),
        "glue_zone_label": place_ends(jax.random.randint(key_list[2], (GRID_DEPTH_CELLS, GRID_WIDTH_CELLS), 0, REGIONS), jax.random.fold_in(key_list[2], 1), 0, REGIONS - 1).astype(jnp.int32),
        "patch_label_per_cell": place_ends(jax.random.randint(key_list[3], (DIE_NUMBER, GRID_DEPTH_CELLS, GRID_WIDTH_CELLS), 0, POWER_TILES), jax.random.fold_in(key_list[3], 1), 0, POWER_TILES - 1).astype(jnp.int32),
        "heat_conductance_per_substance": jnp.clip(jnp.exp(jax.random.uniform(key_list[4], (MATERIALS,), jnp.float32, math.log(0.3), math.log(4.0))), 0.3, 4.0),
        "dissipation_per_patch": jnp.clip(jnp.exp(math.log(5.0) - 2.3025851 * jax.random.uniform(key_list[5], (DIE_NUMBER, POWER_TILES), jnp.float32) ** level_of(key_list[5], (DIE_NUMBER, POWER_TILES), ((0, 4),), -0.2, 0.2)), 0.5, 5.0),
        "glue_sheet_reciprocal_operators": draw_glue_sheet_reciprocal_operators(jax.random.fold_in(key_list[7], 71), 0),
    }


step_dt = 0.04


def pad_axis(field, axis, low, high):
    widths = [(0, 0)] * field.ndim
    widths[axis] = (low, high)
    return jnp.pad(field, widths)


def conduct(padded_t, padded_k):
    centre = padded_t[..., 1:-1, :]
    kcell = padded_k[..., 1:-1, :]
    flux = 0.5 * (kcell + padded_k[..., 2:, :]) * (padded_t[..., 2:, :] - centre)
    flux = flux + 0.5 * (kcell + padded_k[..., :-2, :]) * (padded_t[..., :-2, :] - centre)
    side_t = pad_axis(centre, centre.ndim - 1, 1, 1)
    side_k = pad_axis(kcell, kcell.ndim - 1, 1, 1)
    flux = flux + 0.5 * (kcell + side_k[..., 2:]) * (side_t[..., 2:] - centre)
    flux = flux + 0.5 * (kcell + side_k[..., :-2]) * (side_t[..., :-2] - centre)
    face = 0.5 * (kcell[..., 1:, :, :] + kcell[..., :-1, :, :]) * (centre[..., 1:, :, :] - centre[..., :-1, :, :])
    axis = centre.ndim - 3
    return flux + pad_axis(face, axis, 0, 1) - pad_axis(face, axis, 1, 0)


def reference(warming_above_ambient, substance_label, glue_zone_label, patch_label_per_cell, heat_conductance_per_substance, dissipation_per_patch, glue_sheet_reciprocal_operators):
    kappa = heat_conductance_per_substance[substance_label]
    source = dissipation_per_patch[jnp.arange(DIE_NUMBER)[:, None, None], patch_label_per_cell]
    heating_snapshot = warming_above_ambient
    for step in range(STEPS):
        padded_t = pad_axis(heating_snapshot, 2, 1, 1)
        padded_k = pad_axis(kappa, 2, 1, 1)
        heating_snapshot = heating_snapshot + step_dt * conduct(padded_t, padded_k)
        heating_snapshot = heating_snapshot.at[:, 0].add(step_dt * source)
        planes = jnp.stack([heating_snapshot[:, 0], heating_snapshot[:, -1]], 1).reshape(2 * DIE_NUMBER, GRID_DEPTH_CELLS, GRID_WIDTH_CELLS)
        solved = jnp.zeros_like(planes)
        for which in range(REGIONS):
            mapped = jnp.einsum("ij,jxc->ixc", glue_sheet_reciprocal_operators[which], planes, precision=lax.Precision.HIGHEST)
            solved = solved + jnp.where(glue_zone_label == which, mapped, 0.0)
        solved = solved.reshape(DIE_NUMBER, 2, GRID_DEPTH_CELLS, GRID_WIDTH_CELLS)
        heating_snapshot = heating_snapshot.at[:, 0].set(solved[:, 0]).at[:, -1].set(solved[:, 1])
    return heating_snapshot
```

```python
import functools

import jax
import jax.numpy as jnp
from jax import lax
from jax.experimental import pallas as pl
from jax.experimental.pallas import tpu as pltpu
from jax.sharding import PartitionSpec as P

STEPS = 2
step_dt = 0.04
half_dt = 0.5 * step_dt
LANES = 128
ROWS = 8
MIB = 1 << 20

VMEM = pl.BlockSpec(memory_space=pltpu.VMEM)
SMEM = pl.BlockSpec(memory_space=pltpu.SMEM)
ANY = pl.BlockSpec(memory_space=pl.ANY)


def tile(r, c):
    return pl.ds(ROWS * r, ROWS), pl.ds(LANES * c, LANES)


def lane_ids():
    return lax.broadcasted_iota(jnp.int32, (ROWS, LANES), 1)


def row_ids():
    return lax.broadcasted_iota(jnp.int32, (ROWS, LANES), 0)


def choose(values, labels):
    values, bit = list(values), 1
    while len(values) > 1:
        odd = (labels & bit) != 0
        paired = [
            jnp.where(odd, values[i + 1], values[i]) if i + 1 < len(values) else values[i]
            for i in range(0, len(values), 2)
        ]
        values, bit = paired, 2 * bit
    return values[0]


def lookup(row, labels):
    table = jnp.broadcast_to(row, labels.shape)
    return jnp.take_along_axis(table, labels, axis=1, mode="promise_in_bounds")


def conductance(kap, labels):
    table = [kap[i] for i in range(kap.shape[0])]
    return half_dt * choose(table, labels)


def stencil(R, W, get_s, get_h, get_z, halo, put):
    C, S = W // LANES, R // ROWS
    lane, row = lane_ids(), row_ids()
    first, last = lane == 0, lane == LANES - 1
    top, bottom = row == 0, row == ROWS - 1
    before = None
    for c in range(C):
        s = [get_s(r, c) for r in range(S)]
        h = [get_h(r, c) for r in range(S)]
        rs = [pltpu.roll(v, 1, 1) for v in s]
        rh = [pltpu.roll(v, 1, 1) for v in h]
        us = [pltpu.roll(v, 1, 0) for v in s]
        uh = [pltpu.roll(v, 1, 0) for v in h]
        if halo is not None:
            sa, ha, sb, hb = halo(c)
        acc, back, down = [], [], []
        for r in range(S):
            if c == 0:
                sl, hl = jnp.where(first, 0.0, rs[r]), jnp.where(first, 0.0, rh[r])
            else:
                sl = jnp.where(first, before[0][r], rs[r])
                hl = jnp.where(first, before[1][r], rh[r])
            face = (h[r] + hl) * (sl - s[r])
            back.append(pltpu.roll(face, LANES - 1, 1))
            if r == 0:
                if halo is None:
                    su, hu = us[0], uh[0]
                else:
                    su, hu = jnp.where(top, sa, us[0]), jnp.where(top, ha, uh[0])
            else:
                su, hu = jnp.where(top, us[r - 1], us[r]), jnp.where(top, uh[r - 1], uh[r])
            upper = (h[r] + hu) * (su - s[r])
            down.append(pltpu.roll(upper, ROWS - 1, 0))
            acc.append((s[r] + get_z(r, c, s[r], h[r])) + (face + upper))
        for r in range(S):
            if r + 1 < S:
                lower = jnp.where(bottom, down[r + 1], down[r])
            elif halo is None:
                lower = down[r]
            else:
                lower = jnp.where(bottom, (h[r] + hb) * (s[r] - sb), down[r])
            acc[r] = acc[r] - lower
        if before is not None:
            for r in range(S):
                put(r, c - 1, before[3][r] - jnp.where(last, back[r], before[2][r]))
        before = (rs, rh, back, acc, s, h)
    for r in range(S):
        out = before[5][r] * before[4][r]
        put(r, C - 1, before[3][r] - jnp.where(last, out, before[2][r]))


def vertical(s, h, s_up, h_up, s_down, h_down):
    return (h + h_up) * (s_up - s) + (h + h_down) * (s_down - s)


def first_planes_kernel(s_any, lab_any, patch, kap, power, left, right, h_out, src, s_v, lab_v, sem):
    L, R, W = s_any.shape
    C = W // LANES
    starts = (0, L - 2)
    copies = []
    for p, a in enumerate(starts):
        copies.append(
            [
                pltpu.make_async_copy(s_any.at[pl.ds(a, 2)], s_v.at[p], sem.at[0, p]),
                pltpu.make_async_copy(lab_any.at[pl.ds(a, 2)], lab_v.at[p], sem.at[1, p]),
            ]
        )
    for group in copies:
        for copy in group:
            copy.start()
    for p, a in enumerate(starts):
        for copy in copies[p]:
            copy.wait()
        own, near = (0, 1) if p == 0 else (1, 0)

        def get_s(r, c):
            return s_v[(p, own) + tile(r, c)]

        def get_h(r, c):
            value = conductance(kap, lab_v[(p, own) + tile(r, c)])
            h_out[(a + own,) + tile(r, c)] = value
            return value

        def get_z(r, c, s, h):
            h_near = conductance(kap, lab_v[(p, near) + tile(r, c)])
            h_out[(a + near,) + tile(r, c)] = h_near
            flow = (h + h_near) * (s_v[(p, near) + tile(r, c)] - s)
            if p == 0:
                heat = step_dt * lookup(power[...], patch[tile(r, c)])
                src[tile(r, c)] = heat
                flow = flow + heat
            return flow

        def put(r, c, value):
            half = C // 2
            if c < half:
                left[(p,) + tile(r, c)] = value
            else:
                right[(p,) + tile(r, c - half)] = value

        stencil(R, W, get_s, get_h, get_z, None, put)


def first_planes(s, lab, patch, kap, power):
    L, R, W = s.shape
    f32 = jnp.float32
    return pl.pallas_call(
        first_planes_kernel,
        out_shape=(
            jax.ShapeDtypeStruct((2, R, W // 2), f32),
            jax.ShapeDtypeStruct((2, R, W // 2), f32),
            jax.ShapeDtypeStruct((L, R, W), f32),
            jax.ShapeDtypeStruct((R, W), f32),
        ),
        in_specs=[ANY, ANY, VMEM, SMEM, VMEM],
        out_specs=[VMEM] * 4,
        scratch_shapes=[
            pltpu.VMEM((2, 2, R, W), f32),
            pltpu.VMEM((2, 2, R, W), jnp.int32),
            pltpu.SemaphoreType.DMA((2, 2)),
        ],
        compiler_params=pltpu.CompilerParams(vmem_limit_bytes=16 * MIB),
        name="first_planes",
    )(s, lab, patch, kap, power)


def pack_kernel(s_lo, s_hi, l_lo, l_hi, p_lo, p_hi, g_lo, g_hi, kap, power, up, down):
    L, _, W = s_lo.shape

    def body(c, _):
        lanes = pl.ds(pl.multiple_of(c * LANES, LANES), LANES)
        for out, s, lab, patch, glue, rows in (
            (up, s_lo, l_lo, p_lo, g_lo, (0, 1)),
            (down, s_hi, l_hi, p_hi, g_hi, (ROWS - 2, ROWS - 1)),
        ):
            for k, row in enumerate(rows):
                out[pl.ds(k * L, L), lanes] = s[:, row, lanes]
                out[pl.ds((2 + k) * L, L), lanes] = conductance(kap, lab[:, row, lanes])
            edge = 0 if out is up else ROWS - 1
            heat = step_dt * lookup(power[...], patch[:, lanes])
            glued = glue[:, lanes].astype(jnp.float32)
            row = row_ids()
            pair = jnp.where(row == 0, heat[edge : edge + 1], glued[edge : edge + 1])
            out[pl.ds(4 * L, ROWS), lanes] = pair
        return 0

    lax.fori_loop(0, W // LANES, body, 0)


def pack(s, lab, patch, glue, kap, power):
    L, R, W = s.shape
    n = R // ROWS - 1
    lo3, hi3 = (pl.BlockSpec((L, ROWS, W), lambda i, k=k: (0, k, 0)) for k in (0, n))
    lo2, hi2 = (pl.BlockSpec((ROWS, W), lambda i, k=k: (k, 0)) for k in (0, n))
    rows = 4 * L + ROWS
    whole = pl.BlockSpec((rows, W), lambda i: (0, 0))
    return pl.pallas_call(
        pack_kernel,
        grid=(1,),
        out_shape=(jax.ShapeDtypeStruct((rows, W), jnp.float32),) * 2,
        in_specs=[lo3, hi3, lo3, hi3, lo2, hi2, lo2, hi2, SMEM, pl.BlockSpec(power.shape, lambda i: (0, 0))],
        out_specs=[whole, whole],
        compiler_params=pltpu.CompilerParams(vmem_limit_bytes=24 * MIB),
        name="pack",
    )(s, s, lab, lab, patch, patch, glue, glue, kap, power)


def edge_kernel(place, own_up, own_down, lo, hi, edges, beyond, aux):
    rows, W = own_up.shape
    L = (rows - ROWS) // 4
    col = lax.broadcasted_iota(jnp.int32, (L, W), 1)
    layer = lax.broadcasted_iota(jnp.int32, (L, W), 0)

    def part(ref, k):
        return ref[pl.ds(k * L, L), :]

    def step(s_a, h_a, s, h, s_b, h_b):
        def toward(s_n, h_n):
            return (h + h_n) * (s_n - s)

        def moved(shift, axis, gone):
            return jnp.where(gone, 0.0, pltpu.roll(s, shift, axis)), jnp.where(
                gone, 0.0, pltpu.roll(h, shift, axis)
            )

        total = s + toward(s_a, h_a) + toward(s_b, h_b)
        total = total + toward(*moved(1, 1, col == 0)) + toward(*moved(W - 1, 1, col == W - 1))
        under = jnp.where(layer == 0, 0.0, toward(pltpu.roll(s, 1, 0), pltpu.roll(h, 1, 0)))
        over = jnp.where(layer == L - 1, 0.0, toward(pltpu.roll(s, L - 1, 0), pltpu.roll(h, L - 1, 0)))
        return total + under + over

    for side, (other, own, there) in enumerate(((lo, own_up, place[0]), (hi, own_down, place[1]))):
        far, near = (0, 1) if side == 0 else (1, 0)
        exists = there != 0
        sf, sn = (jnp.where(exists, part(other, k), 0.0) for k in (far, near))
        hf, hn = (jnp.where(exists, part(other, 2 + k), 0.0) for k in (far, near))
        first, second = (0, 1) if side == 0 else (1, 0)
        s0, s1, h0, h1 = part(own, first), part(own, second), part(own, 2 + first), part(own, 2 + second)
        out = step(sf, hf, sn, hn, s0, h0)
        out = jnp.where(exists, out, 0.0)
        inner = step(sn, hn, s0, h0, s1, h1)
        beyond[side] = out
        heat_out = jnp.where(exists, other[pl.ds(4 * L, 1), :], 0.0)
        heat_in = own[pl.ds(4 * L, 1), :]
        k_out, k_in = (0, 1) if side == 0 else (3, 2)
        edges[pl.ds(k_out, 1), :] = out[0:1] + heat_out
        edges[pl.ds(k_in, 1), :] = inner[0:1] + heat_in
        edges[pl.ds(4 + k_out, 1), :] = out[L - 1 : L]
        edges[pl.ds(4 + k_in, 1), :] = inner[L - 1 : L]
        aux[pl.ds(2 * side, 1), :] = hn[0:1]
        aux[pl.ds(2 * side + 1, 1), :] = hn[L - 1 : L]
        zone_out = jnp.where(exists, other[pl.ds(4 * L + 1, 1), :], 0.0)
        aux[pl.ds(4 + k_out, 1), :] = zone_out
        aux[pl.ds(4 + k_in, 1), :] = own[pl.ds(4 * L + 1, 1), :]


def edge_rows(place, own_up, own_down, lo, hi):
    rows, W = own_up.shape
    L = (rows - ROWS) // 4
    f32 = jnp.float32
    return pl.pallas_call(
        edge_kernel,
        out_shape=(
            jax.ShapeDtypeStruct((ROWS, W), f32),
            jax.ShapeDtypeStruct((2, L, W), f32),
            jax.ShapeDtypeStruct((ROWS, W), f32),
        ),
        in_specs=[SMEM] + [VMEM] * 4,
        out_specs=[VMEM] * 3,
        compiler_params=pltpu.CompilerParams(vmem_limit_bytes=16 * MIB),
        name="edge_rows",
    )(place, own_up, own_down, lo, hi)


def pick(ref, base, l, lanes, row):
    at = base + (l // ROWS) * ROWS
    if not isinstance(l, int):
        at = pl.multiple_of(at, ROWS)
    return pltpu.roll(ref[pl.ds(at, ROWS), lanes], (row - l) % ROWS, 0)


def halo_rows(lo, hi, place, lanes, l, L):
    above, below = place[0] != 0, place[1] != 0
    end = ROWS - 1
    sa = jnp.where(above, pick(lo, L, l, lanes, 0), 0.0)
    ha = jnp.where(above, pick(lo, 3 * L, l, lanes, 0), 0.0)
    sb = jnp.where(below, pick(hi, 0, l, lanes, end), 0.0)
    hb = jnp.where(below, pick(hi, 2 * L, l, lanes, end), 0.0)
    return sa, ha, sb, hb


def first_layer(l, L, R, W, place, s_ref, lab, kap, lo, hi, h_ref, out, ready):
    def get_h(r, c):
        return h_ref[(l,) + tile(r, c)]

    def get_s(r, c):
        return s_ref[(l,) + tile(r, c)]

    def near(k, r, c):
        at = (l + k,) + tile(r, c)
        if k in ready:
            return h_ref[at]
        value = conductance(kap, lab[at])
        h_ref[at] = value
        return value

    def get_z(r, c, s, h):
        return vertical(
            s, h, s_ref[(l - 1,) + tile(r, c)], near(-1, r, c), s_ref[(l + 1,) + tile(r, c)], near(1, r, c)
        )

    def put(r, c, value):
        out[(l,) + tile(r, c)] = value

    def halo(c):
        return halo_rows(lo, hi, place, pl.ds(LANES * c, LANES), l, L)

    stencil(R, W, get_s, get_h, get_z, halo, put)


def outer_kernel(place, s_ref, lab, kap, lo, hi, h_in, h_ref, out):
    L, R, W = s_ref.shape
    first_layer(1, L, R, W, place, s_ref, lab, kap, lo, hi, h_ref, out, (-1, 0))
    first_layer(L - 2, L, R, W, place, s_ref, lab, kap, lo, hi, h_ref, out, (0, 1))


def outer_layers(place, s, lab, kap, lo, hi, h):
    return pl.pallas_call(
        outer_kernel,
        out_shape=(jax.ShapeDtypeStruct(s.shape, jnp.float32),) * 2,
        in_specs=[SMEM, VMEM, VMEM, SMEM, VMEM, VMEM, VMEM],
        out_specs=[VMEM, VMEM],
        input_output_aliases={6: 0},
        compiler_params=pltpu.CompilerParams(vmem_limit_bytes=24 * MIB),
        name="outer_layers",
    )(place, s, lab, kap, lo, hi, h)


def inner_kernel(place, s_ref, lab, kap, lo, hi, h_in, t_in, h_ref, out):
    L, R, W = s_ref.shape

    def body(l, _):
        first_layer(l, L, R, W, place, s_ref, lab, kap, lo, hi, h_ref, out, (-1, 0))
        return 0

    lax.fori_loop(2, L - 2, body, 0)


def inner_layers(place, s, lab, kap, lo, hi, h, t):
    return pl.pallas_call(
        inner_kernel,
        out_shape=(jax.ShapeDtypeStruct(s.shape, jnp.float32),) * 2,
        in_specs=[SMEM, VMEM, VMEM, SMEM, VMEM, VMEM, VMEM, VMEM],
        out_specs=[VMEM, VMEM],
        input_output_aliases={6: 0, 7: 1},
        compiler_params=pltpu.CompilerParams(vmem_limit_bytes=24 * MIB),
        name="inner_layers",
    )(place, s, lab, kap, lo, hi, h, t)


def last_kernel(place, t_ref, h_ref, lo, hi, beyond, out, buf, sem):
    L, R, W = t_ref.shape

    def send(l):
        return pltpu.make_async_copy(buf.at[l], out.at[l], sem.at[l])

    def body(l, _):
        def get_s(r, c):
            return t_ref[(l,) + tile(r, c)]

        def get_h(r, c):
            return h_ref[(l,) + tile(r, c)]

        def get_z(r, c, s, h):
            a, b = (l - 1,) + tile(r, c), (l + 1,) + tile(r, c)
            return vertical(s, h, t_ref[a], h_ref[a], t_ref[b], h_ref[b])

        def put(r, c, value):
            buf[(l,) + tile(r, c)] = value

        def halo(c):
            lanes = pl.ds(LANES * c, LANES)
            _, ha, _, hb = halo_rows(lo, hi, place, lanes, l, L)
            sa, sb = pick(beyond.at[0], 0, l, lanes, 0), pick(beyond.at[1], 0, l, lanes, ROWS - 1)
            return sa, ha, sb, hb

        stencil(R, W, get_s, get_h, get_z, halo, put)
        send(l).start()
        return 0

    lax.fori_loop(1, L - 1, body, 0)

    def drain(l, _):
        send(l).wait()
        return 0

    lax.fori_loop(1, L - 1, drain, 0)


def last_layers(place, t, h, lo, hi, beyond):
    L = t.shape[0]
    return pl.pallas_call(
        last_kernel,
        out_shape=jax.ShapeDtypeStruct(t.shape, jnp.float32),
        in_specs=[SMEM] + [VMEM] * 5,
        out_specs=ANY,
        scratch_shapes=[pltpu.VMEM(t.shape, jnp.float32), pltpu.SemaphoreType.DMA((L,))],
        compiler_params=pltpu.CompilerParams(vmem_limit_bytes=24 * MIB),
        name="last_layers",
    )(place, t, h, lo, hi, beyond)


def coefficient(ops, tiers, regions, region, i, j):
    return ops[(region * 2 * tiers + i) * 2 * tiers + j]


def mixed(ops, tiers, regions, zone, row, planes):
    total = None
    for index, value in planes:
        table = [coefficient(ops, tiers, regions, g, row, index) for g in range(regions)]
        term = choose(table, zone) * value
        total = term if total is None else total + term
    return total


def combine_kernel(tiers, regions, tier, ops, zone, left, left_x, right, right_y, to_y, to_x):
    _, R, half = left.shape
    me = tier[0]
    for out, own, other, near, target, base in (
        (to_y, left, left_x, tier[1], tier[2], 0),
        (to_x, right, right_y, tier[2], tier[1], half),
    ):

        def body(c, _, out=out, own=own, other=other, near=near, target=target, base=base):
            lanes = pl.ds(pl.multiple_of(c * LANES, LANES), LANES)
            zone_lanes = pl.ds(pl.multiple_of(base + c * LANES, LANES), LANES)
            for r in range(R // ROWS):
                rows = pl.ds(ROWS * r, ROWS)
                planes = [(2 * me + j, own[j, rows, lanes]) for j in range(2)]
                planes += [(2 * near + j, other[j, rows, lanes]) for j in range(2)]
                for i in range(2):
                    out[i, rows, lanes] = mixed(
                        ops, tiers, regions, zone[rows, zone_lanes], 2 * target + i, planes
                    )
            return 0

        lax.fori_loop(0, half // LANES, body, 0)


def combine(tiers, regions, tier, ops, zone, left, left_x, right, right_y):
    return pl.pallas_call(
        functools.partial(combine_kernel, tiers, regions),
        out_shape=(jax.ShapeDtypeStruct(left.shape, jnp.float32),) * 2,
        in_specs=[SMEM, SMEM] + [VMEM] * 5,
        out_specs=[VMEM, VMEM],
        compiler_params=pltpu.CompilerParams(vmem_limit_bytes=16 * MIB),
        name="combine",
    )(tier, ops, zone, left, left_x, right, right_y)


def solve_half(tiers, regions, me, ops, zone, R, half, base, raw, partial, put):
    def body(c, _):
        lanes = pl.ds(pl.multiple_of(c * LANES, LANES), LANES)
        whole = pl.ds(pl.multiple_of(base + c * LANES, LANES), LANES)
        for r in range(R // ROWS):
            rows = pl.ds(ROWS * r, ROWS)
            planes = [(2 * q + j, ref[k + j, rows, lanes]) for q, ref, k in raw for j in range(2)]
            for i in range(2):
                value = mixed(ops, tiers, regions, zone[rows, whole], 2 * me + i, planes)
                for ref in partial:
                    value = value + ref[i, rows, lanes]
                put(i, rows, whole, value)
        return 0

    lax.fori_loop(0, half // LANES, body, 0)


def sources(tiers, tier, refs, paired):
    if paired is not None:
        own, other, part = refs
        return [(tier[0], own, 0), (tier[paired], other, 0)], [part]
    (every,) = refs
    return [(q, every, 2 * q) for q in range(tiers)], []


def bond_kernel(tiers, regions, count, place, tier, ops, zone, aux, heat, h_ref, *refs):
    pairs = tiers == 4
    per = 3 if pairs else 1
    left, right, refs = refs[:per], refs[per : 2 * per], refs[2 * per :]
    edge_refs, refs = refs[: 4 if pairs else 1], refs[4 if pairs else 1 :]
    t_in, t_ref, out_left, out_right, rim = refs
    L, R, W = t_ref.shape
    half, C = W // 2, W // LANES
    me = tier[0]
    row = row_ids()

    def put(i, rows, lanes, value):
        t_ref[i * (L - 1), rows, lanes] = value

    for side, group in enumerate((left, right)):
        raw, partial = sources(tiers, tier, group, 1 + side if pairs else None)
        solve_half(tiers, regions, me, ops, zone, R, half, side * half, raw, partial, put)

    def edge_body(c, _):
        lanes = pl.ds(pl.multiple_of(c * LANES, LANES), LANES)
        if pairs:
            tiles = [(tier[q], ref[:, lanes]) for q, ref in enumerate(edge_refs)]
        else:
            tiles = [(q, edge_refs[0][q, :, lanes]) for q in range(tiers)]
        zones = aux[pl.ds(4, 4), lanes].astype(jnp.int32)
        zones = jnp.concatenate([zones, zones], axis=0)
        total = []
        for i in range(2):
            planes = []
            for q, value in tiles:
                swapped = pltpu.roll(value, 4, 0)
                planes += [(2 * q + i, value), (2 * q + 1 - i, swapped)]
            total.append(mixed(ops, tiers, regions, zones, 2 * me + i, planes))
        value = jnp.where(row < 4, total[0], total[1])
        gone = ((row % 4 == 0) & (place[0] == 0)) | ((row % 4 == 3) & (place[1] == 0))
        value = jnp.where(gone, 0.0, value)
        rim[:, lanes] = value
        for i in range(2):
            t_ref[i * (L - 1), pl.ds(0, 1), lanes] = value[4 * i + 1 : 4 * i + 2]
            t_ref[i * (L - 1), pl.ds(R - 1, 1), lanes] = value[4 * i + 2 : 4 * i + 3]
        return 0

    lax.fori_loop(0, C, edge_body, 0)

    for p in range(2):
        own, near = (0, 1) if p == 0 else (L - 1, L - 2)

        def get_s(r, c):
            return t_ref[(own,) + tile(r, c)]

        def get_h(r, c):
            return h_ref[(own,) + tile(r, c)]

        def get_z(r, c, s, h):
            at = (near,) + tile(r, c)
            flow = (h + h_ref[at]) * (t_ref[at] - s)
            return flow + heat[tile(r, c)] if p == 0 else flow

        def halo(c):
            lanes = pl.ds(LANES * c, LANES)
            return (
                rim[pl.ds(4 * p, 1), lanes],
                aux[pl.ds(p, 1), lanes],
                rim[pl.ds(4 * p + 3, 1), lanes],
                aux[pl.ds(2 + p, 1), lanes],
            )

        def put_out(r, c, value):
            if c < C // 2:
                out_left[(p,) + tile(r, c)] = value
            else:
                out_right[(p,) + tile(r, c - C // 2)] = value

        stencil(R, W, get_s, get_h, get_z, halo, put_out)


def bond(tiers, regions, place, tier, ops, zone, aux, heat, h, left, right, edges, t):
    L, R, W = t.shape
    args = (place, tier, ops, zone, aux, heat, h, *left, *right, *edges, t)
    f32 = jnp.float32
    return pl.pallas_call(
        functools.partial(bond_kernel, tiers, regions, len(left)),
        out_shape=(
            jax.ShapeDtypeStruct(t.shape, f32),
            jax.ShapeDtypeStruct((2, R, W // 2), f32),
            jax.ShapeDtypeStruct((2, R, W // 2), f32),
        ),
        in_specs=[SMEM] * 3 + [VMEM] * (len(args) - 3),
        out_specs=[VMEM] * 3,
        scratch_shapes=[pltpu.VMEM((ROWS, W), f32)],
        input_output_aliases={len(args) - 1: 0},
        compiler_params=pltpu.CompilerParams(vmem_limit_bytes=24 * MIB),
        name="bond",
    )(*args)


def final_kernel(tiers, regions, tier, ops, zone, *refs):
    per = 3 if tiers == 4 else 1
    left, right = refs[:per], refs[per : 2 * per]
    _, out, buf, sem = refs[2 * per :]
    L, R, W = out.shape
    half = W // 2
    copies = []
    for side, group in enumerate((left, right)):
        raw, partial = sources(tiers, tier, group, 1 + side if tiers == 4 else None)

        def put(i, rows, lanes, value):
            buf[i, rows, lanes] = value

        solve_half(tiers, regions, tier[0], ops, zone, R, half, side * half, raw, partial, put)
        lanes = pl.ds(side * half, half)
        for i in range(2):
            copies.append(
                pltpu.make_async_copy(
                    buf.at[i, :, lanes], out.at[i * (L - 1), :, lanes], sem.at[2 * side + i]
                )
            )
            copies[-1].start()
    for copy in copies:
        copy.wait()


def final_planes(tiers, regions, tier, ops, zone, left, right, out):
    args = (tier, ops, zone, *left, *right, out)
    _, R, W = out.shape
    return pl.pallas_call(
        functools.partial(final_kernel, tiers, regions),
        out_shape=jax.ShapeDtypeStruct(out.shape, jnp.float32),
        in_specs=[SMEM, SMEM] + [VMEM] * (len(args) - 3) + [ANY],
        out_specs=ANY,
        scratch_shapes=[pltpu.VMEM((2, R, W), jnp.float32), pltpu.SemaphoreType.DMA((4,))],
        input_output_aliases={len(args) - 1: 0},
        compiler_params=pltpu.CompilerParams(vmem_limit_bytes=16 * MIB),
        name="final_planes",
    )(*args)


def across(value, bits, tiers):
    return lax.ppermute(value, "tier", [(i, i ^ bits) for i in range(tiers)])


def every(value, tiers):
    gathered = lax.all_gather(value, "tier", axis=0, tiled=False)
    return gathered.reshape((tiers * value.shape[0],) + value.shape[1:]) if value.ndim == 3 else gathered


def exchange(tiers, regions, tier, ops, zone, left, right):
    if tiers != 4:
        return (every(left, tiers),), (every(right, tiers),)
    left_x, right_y = across(left, 1, tiers), across(right, 2, tiers)
    to_y, to_x = combine(tiers, regions, tier, ops, zone, left, left_x, right, right_y)
    return (left, left_x, across(to_y, 2, tiers)), (right, right_y, across(to_x, 1, tiers))


def local(warming, substance, zone, patch, kap, power, ops):
    tiers, tiles = lax.axis_size("tier"), lax.axis_size("tile")
    regions = ops.shape[0]
    ops = ops.reshape(-1)
    s, lab, patch = warming[0], substance[0], patch[0]
    me, at = lax.axis_index("tier"), lax.axis_index("tile")
    tier = jnp.stack([me, me ^ 1, me ^ 2, me ^ 3]).astype(jnp.int32)
    place = jnp.stack([at > 0, at < tiles - 1]).astype(jnp.int32)

    left, right, h, heat = first_planes(s, lab, patch, kap, power)
    up, down = pack(s, lab, patch, zone, kap, power)
    lo = lax.ppermute(down, "tile", [(i, (i + 1) % tiles) for i in range(tiles)])
    hi = lax.ppermute(up, "tile", [((i + 1) % tiles, i) for i in range(tiles)])
    left, right = exchange(tiers, regions, tier, ops, zone, left, right)
    edges, beyond, aux = edge_rows(place, up, down, lo, hi)
    if tiers == 4:
        edges = (edges, across(edges, 1, tiers), across(edges, 2, tiers), across(edges, 3, tiers))
    else:
        edges = (every(edges, tiers),)
    h, t = outer_layers(place, s, lab, kap, lo, hi, h)
    t, left, right = bond(tiers, regions, place, tier, ops, zone, aux, heat, h, left, right, edges, t)
    left, right = exchange(tiers, regions, tier, ops, zone, left, right)
    h, t = inner_layers(place, s, lab, kap, lo, hi, h, t)
    out = last_layers(place, t, h, lo, hi, beyond)
    out = final_planes(tiers, regions, tier, ops, zone, left, right, out)
    return out[None]


def solution(mesh):
    in_specs = (
        P("tier", None, "tile", None),
        P("tier", None, "tile", None),
        P("tile", None),
        P("tier", "tile", None),
        P(),
        P("tier", None),
        P(),
    )
    out_specs = P("tier", None, "tile", None)
    return jax.shard_map(local, mesh=mesh, in_specs=in_specs, out_specs=out_specs, check_vma=False)
```

```python
import functools
import math

import jax
import jax.numpy as jnp
from jax import lax
from jax.experimental import pallas as pl
from jax.experimental.pallas import tpu as pltpu
from jax.sharding import PartitionSpec as P

STEPS = 2
step_dt = 0.04
half_dt = 0.5 * step_dt
LANES = 128
ROWS = 8
MIB = 1 << 20

VMEM = pl.BlockSpec(memory_space=pltpu.VMEM)
SMEM = pl.BlockSpec(memory_space=pltpu.SMEM)
ANY = pl.BlockSpec(memory_space=pl.ANY)
HBM = pl.BlockSpec(memory_space=pltpu.HBM)


def tile(r, c):
    return pl.ds(ROWS * r, ROWS), pl.ds(LANES * c, LANES)


def lasts(us):
    return pl.CostEstimate(flops=0, bytes_accessed=int(us * 3.3e6), transcendentals=0)


def lane_ids():
    return lax.broadcasted_iota(jnp.int32, (ROWS, LANES), 1)


def row_ids():
    return lax.broadcasted_iota(jnp.int32, (ROWS, LANES), 0)


def choose(values, labels):
    values, bit = list(values), 1
    while len(values) > 1:
        odd = (labels & bit) != 0
        paired = [
            jnp.where(odd, values[i + 1], values[i]) if i + 1 < len(values) else values[i]
            for i in range(0, len(values), 2)
        ]
        values, bit = paired, 2 * bit
    return values[0]


def lookup(row, labels):
    return jnp.take_along_axis(row, labels, axis=1, mode="promise_in_bounds")


def splats(kap):
    return [jnp.full((ROWS, LANES), half_dt * kap[i], jnp.float32) for i in range(kap.shape[0])]


def stencil(R, W, get_s, get_h, get_z, halo, put, get_g=None, put_g=None):
    C, S = W // LANES, R // ROWS
    lane, row = lane_ids(), row_ids()
    first, last = lane == 0, lane == LANES - 1
    top, bottom = row == 0, row == ROWS - 1
    before = None
    for c in range(C):
        s = [get_s(r, c) for r in range(S)]
        h = [get_h(r, c) for r in range(S)]
        rs = [pltpu.roll(v, 1, 1) for v in s]
        rh = [pltpu.roll(v, 1, 1) for v in h] if get_g is None else None
        us = [pltpu.roll(v, 1, 0) for v in s]
        uh = [pltpu.roll(v, 1, 0) for v in h]
        if halo is not None:
            sa, ha, sb, hb = halo(c)
        acc, back, down = [], [], []
        for r in range(S):
            sl = jnp.where(first, 0.0 if c == 0 else before[0][r], rs[r])
            if get_g is None:
                g = h[r] + jnp.where(first, 0.0 if c == 0 else before[1][r], rh[r])
                if put_g is not None:
                    put_g(r, c, g)
            else:
                g = get_g(r, c)
            face = g * (sl - s[r])
            back.append(pltpu.roll(face, LANES - 1, 1))
            if r == 0:
                if halo is None:
                    su, hu = us[0], uh[0]
                else:
                    su, hu = jnp.where(top, sa, us[0]), jnp.where(top, ha, uh[0])
            else:
                su, hu = jnp.where(top, us[r - 1], us[r]), jnp.where(top, uh[r - 1], uh[r])
            upper = (h[r] + hu) * (su - s[r])
            down.append(pltpu.roll(upper, ROWS - 1, 0))
            acc.append((s[r] + get_z(r, c, s[r], h[r])) + (face + upper))
        for r in range(S):
            if r + 1 < S:
                lower = jnp.where(bottom, down[r + 1], down[r])
            elif halo is None:
                lower = down[r]
            else:
                lower = jnp.where(bottom, (h[r] + hb) * (s[r] - sb), down[r])
            acc[r] = acc[r] - lower
        if before is not None:
            for r in range(S):
                put(r, c - 1, before[3][r] - jnp.where(last, back[r], before[2][r]))
        before = (rs, rh, back, acc, s, h)
    for r in range(S):
        out = before[5][r] * before[4][r]
        put(r, C - 1, before[3][r] - jnp.where(last, out, before[2][r]))


def vertical(s, h, s_up, h_up, s_down, h_down):
    return (h + h_up) * (s_up - s) + (h + h_down) * (s_down - s)


def begin_kernel(
    s_hbm, lab_hbm, patch_hbm, zone_hbm, kap_hbm, power_hbm,
    left, right, heat, swap_a, swap_b, s_v, lab_v,
    patch, zone_v, kap, power, sem,
):
    L, R, W = s_hbm.shape
    C, half = W // LANES, W // 2
    starts = (0, R - ROWS)
    small = [
        pltpu.make_async_copy(kap_hbm, kap, sem.at[0]),
        pltpu.make_async_copy(power_hbm, power, sem.at[1]),
        pltpu.make_async_copy(patch_hbm, patch, sem.at[2]),
    ]
    groups = [(0, 2), (L - 2, 2), (2, L - 4)]
    layers = [
        [
            pltpu.make_async_copy(s_hbm.at[pl.ds(l, n)], s_v.at[pl.ds(l, n)], sem.at[3 + 2 * k]),
            pltpu.make_async_copy(lab_hbm.at[pl.ds(l, n)], lab_v.at[pl.ds(l, n)], sem.at[4 + 2 * k]),
        ]
        for k, (l, n) in enumerate(groups)
    ]
    layers[2] += [
        pltpu.make_async_copy(zone_hbm.at[pl.ds(start, ROWS)], zone_v.at[k], sem.at[9 + k])
        for k, start in enumerate(starts)
    ]
    for copy in small + layers[0] + layers[1] + layers[2]:
        copy.start()
    for copy in small:
        copy.wait()
    values = splats(kap)
    heats = step_dt * jnp.broadcast_to(power[...], (ROWS, LANES))
    for p in range(2):
        for copy in layers[p]:
            copy.wait()
        own, near = (0, 1) if p == 0 else (L - 1, L - 2)

        def get_s(r, c):
            return s_v[(own,) + tile(r, c)]

        def get_h(r, c):
            return choose(values, lab_v[(own,) + tile(r, c)])

        def get_z(r, c, s, h):
            h_near = choose(values, lab_v[(near,) + tile(r, c)])
            flow = (h + h_near) * (s_v[(near,) + tile(r, c)] - s)
            if p == 0:
                value = lookup(heats, patch[tile(r, c)])
                heat[tile(r, c)] = value
                flow = flow + value
            return flow

        def put(r, c, value):
            out = left if c < C // 2 else right
            out[(p,) + tile(r, c % (C // 2))] = value

        stencil(R, W, get_s, get_h, get_z, None, put)
    row = row_ids()
    for copy in layers[2]:
        copy.wait()

    def pack(k, out):
        rows = ((0, 1), (ROWS - 2, ROWS - 1))[k]

        def body(c, _):
            lanes = pl.ds(pl.multiple_of(c * LANES, LANES), LANES)
            edge = pl.ds(starts[k], ROWS)
            for base in range(0, L, ROWS):
                for ref, at in ((s_v, 0), (lab_v, 2 * L)):
                    tiles = [ref[base + q, edge, lanes] for q in range(ROWS)]
                    for j, source in enumerate(rows):
                        packed = tiles[source]
                        for q in range(ROWS):
                            if q != source:
                                packed = jnp.where(row == q, pltpu.roll(tiles[q], (q - source) % ROWS, 0), packed)
                        if ref is lab_v:
                            packed = choose(values, packed)
                        out[pl.ds(at + j * L + base, ROWS), lanes] = packed
            last = rows[0] if k == 0 else rows[1]
            warm = heat[edge, lanes]
            zones = zone_v[k, :, lanes].astype(jnp.float32)
            pair = jnp.where(row == 0, pltpu.roll(warm, -last % ROWS, 0), pltpu.roll(zones, (1 - last) % ROWS, 0))
            out[pl.ds(4 * L, ROWS), lanes] = pair
            return 0

        lax.fori_loop(0, W // LANES, body, 0)

    odd = lax.axis_index("tile") % 2 == 1

    @pl.when(odd)
    def _():
        pack(0, swap_a)
        pack(1, swap_b)

    @pl.when(jnp.logical_not(odd))
    def _():
        pack(1, swap_a)
        pack(0, swap_b)


def begin(s, lab, patch, zone, kap, power):
    L, R, W = s.shape
    f32, i32 = jnp.float32, jnp.int32
    packed = pltpu.VMEM((4 * L + ROWS, W), f32)
    plane = pltpu.VMEM((2, R, W // 2), f32)
    args = [pltpu.with_memory_space_constraint(x, pltpu.HBM) for x in (s, lab, patch, zone, kap, power)]
    return pl.pallas_call(
        begin_kernel,
        out_shape=(
            plane, plane, pltpu.VMEM((R, W), f32), packed, packed, pltpu.VMEM(s.shape, f32), pltpu.VMEM(lab.shape, i32)
        ),
        in_specs=[HBM] * 6,
        out_specs=[VMEM] * 7,
        scratch_shapes=[
            pltpu.VMEM((R, W), i32),
            pltpu.VMEM((2, ROWS, W), i32),
            pltpu.SMEM(kap.shape, f32),
            pltpu.VMEM(power.shape, f32),
            pltpu.SemaphoreType.DMA((11,)),
        ],
        compiler_params=pltpu.CompilerParams(vmem_limit_bytes=16 * MIB),
        name="begin",
    )(*args)


def above_exists():
    return lax.axis_index("tile") > 0


def below_exists():
    return lax.axis_index("tile") < lax.axis_size("tile") - 1


def edge_kernel(own_a, own_b, got_a, got_b, edges, rims, aux):
    rows, W = own_a.shape
    L = (rows - ROWS) // 4
    col = lax.broadcasted_iota(jnp.int32, (L, W), 1)
    layer = lax.broadcasted_iota(jnp.int32, (L, W), 0)
    odd = lax.axis_index("tile") % 2 == 1

    def step(s_a, h_a, s, h, s_b, h_b):
        def toward(s_n, h_n):
            return (h + h_n) * (s_n - s)

        def moved(shift, axis, gone):
            return jnp.where(gone, 0.0, pltpu.roll(s, shift, axis)), jnp.where(
                gone, 0.0, pltpu.roll(h, shift, axis)
            )

        total = s + toward(s_a, h_a) + toward(s_b, h_b)
        total = total + toward(*moved(1, 1, col == 0)) + toward(*moved(W - 1, 1, col == W - 1))
        under = jnp.where(layer == 0, 0.0, toward(pltpu.roll(s, 1, 0), pltpu.roll(h, 1, 0)))
        over = jnp.where(layer == L - 1, 0.0, toward(pltpu.roll(s, L - 1, 0), pltpu.roll(h, L - 1, 0)))
        return total + under + over

    for side, exists in enumerate((above_exists(), below_exists())):
        first_swap = odd if side == 0 else jnp.logical_not(odd)

        def other(at, n):
            at = pl.ds(at, n)
            return jnp.where(exists, jnp.where(first_swap, got_a[at, :], got_b[at, :]), 0.0)

        def own(at, n):
            at = pl.ds(at, n)
            return jnp.where(first_swap, own_a[at, :], own_b[at, :])

        far, near = (0, 1) if side == 0 else (1, 0)
        sf, sn, hf, hn = (other(k * L, L) for k in (far, near, 2 + far, 2 + near))
        s0, s1, h0, h1 = (own(k * L, L) for k in (1 - near, near, 3 - near, 2 + near))
        out = jnp.where(exists, step(sf, hf, sn, hn, s0, h0), 0.0)
        inner = step(sn, hn, s0, h0, s1, h1)
        rims[2 * side] = sn
        rims[2 * side + 1] = hn
        rims[4 + side] = out
        k_out, k_in = (0, 1) if side == 0 else (3, 2)
        edges[pl.ds(k_out, 1), :] = out[0:1] + other(4 * L, 1)
        edges[pl.ds(k_in, 1), :] = inner[0:1] + own(4 * L, 1)
        edges[pl.ds(4 + k_out, 1), :] = out[L - 1 : L]
        edges[pl.ds(4 + k_in, 1), :] = inner[L - 1 : L]
        aux[pl.ds(2 * side, 1), :] = hn[0:1]
        aux[pl.ds(2 * side + 1, 1), :] = hn[L - 1 : L]
        aux[pl.ds(4 + k_out, 1), :] = other(4 * L + 1, 1)
        aux[pl.ds(4 + k_in, 1), :] = own(4 * L + 1, 1)


def edge_rows(own_a, own_b, got_a, got_b):
    rows, W = own_a.shape
    L = (rows - ROWS) // 4
    f32 = jnp.float32
    return pl.pallas_call(
        edge_kernel,
        out_shape=(
            jax.ShapeDtypeStruct((ROWS, W), f32),
            jax.ShapeDtypeStruct((6, L, W), f32),
            jax.ShapeDtypeStruct((ROWS, W), f32),
        ),
        in_specs=[VMEM] * 4,
        out_specs=[VMEM] * 3,
        compiler_params=pltpu.CompilerParams(vmem_limit_bytes=16 * MIB),
        cost_estimate=lasts(1.0),
        name="edge_rows",
    )(own_a, own_b, got_a, got_b)


def pick(ref, base, l, lanes, row):
    at = base + (l // ROWS) * ROWS
    if not isinstance(l, int):
        at = pl.multiple_of(at, ROWS)
    return pltpu.roll(ref[pl.ds(at, ROWS), lanes], (row - l) % ROWS, 0)


def halo_rows(rims, state, lanes, l):
    end = ROWS - 1
    where = ((state[0], 0), (1, 0), (state[1], end), (3, end))
    return tuple(pick(rims.at[k], 0, l, lanes, row) for k, row in where)


def fill_faces(first, end, lab, values, h_out, g_out):
    _, R, W = lab.shape
    edge = lane_ids() == 0

    def body(l, _):
        for r in range(R // ROWS):
            before = 0.0
            for c in range(W // LANES):
                at = (l,) + tile(r, c)
                h = choose(values, lab[at])
                moved = pltpu.roll(h, 1, 1)
                h_out[at] = h
                g_out[at] = h + jnp.where(edge, before, moved)
                before = moved
        return 0

    lax.fori_loop(first, end, body, 0)


def faces_kernel(lab, kap, _, __, h_out, g_out):
    L = lab.shape[0]
    values = splats(kap)
    fill_faces(0, 3, lab, values, h_out, g_out)
    fill_faces(L - 3, L, lab, values, h_out, g_out)


def faces(lab, kap, first, second):
    return pl.pallas_call(
        faces_kernel,
        out_shape=(jax.ShapeDtypeStruct(lab.shape, jnp.float32),) * 2,
        in_specs=[VMEM, SMEM, ANY, ANY],
        out_specs=[VMEM] * 2,
        compiler_params=pltpu.CompilerParams(vmem_limit_bytes=20 * MIB),
        name="faces",
    )(lab, kap, first, second)


def layer_step(l, s_ref, h_ref, g_ref, halo, put):
    _, R, W = s_ref.shape

    def get_s(r, c):
        return s_ref[(l,) + tile(r, c)]

    def get_h(r, c):
        return h_ref[(l,) + tile(r, c)]

    def get_g(r, c):
        return g_ref[(l,) + tile(r, c)]

    def get_z(r, c, s, h):
        a, b = (l - 1,) + tile(r, c), (l + 1,) + tile(r, c)
        return vertical(s, h, s_ref[a], h_ref[a], s_ref[b], h_ref[b])

    stencil(R, W, get_s, get_h, get_z, halo, put, get_g=get_g)


def first_step(l, s_ref, h_ref, g_ref, rims, t):
    def put(r, c, value):
        t[(l,) + tile(r, c)] = value

    def halo(c):
        return halo_rows(rims, (0, 2), pl.ds(LANES * c, LANES), l)

    layer_step(l, s_ref, h_ref, g_ref, halo, put)


def outer_kernel(s_ref, h_ref, g_ref, rims, t):
    L = s_ref.shape[0]

    def body(k, _):
        first_step(1 + k * (L - 3), s_ref, h_ref, g_ref, rims, t)
        return 0

    lax.fori_loop(0, 2, body, 0)


def outer(s, h, g, rims):
    return pl.pallas_call(
        outer_kernel,
        out_shape=jax.ShapeDtypeStruct(s.shape, jnp.float32),
        in_specs=[VMEM] * 4,
        out_specs=VMEM,
        compiler_params=pltpu.CompilerParams(vmem_limit_bytes=20 * MIB),
        cost_estimate=lasts(0.8),
        name="outer",
    )(s, h, g, rims)


def inside_kernel(s_ref, lab, kap, rims, h_in, g_in, t_in, _, h_ref, g_ref, t):
    L = s_ref.shape[0]
    fill_faces(3, L - 3, lab, splats(kap), h_ref, g_ref)

    def body(l, _):
        first_step(l, s_ref, h_ref, g_ref, rims, t)
        return 0

    lax.fori_loop(2, L - 2, body, 0)


def inside(s, lab, kap, rims, h, g, t, after):
    return pl.pallas_call(
        inside_kernel,
        out_shape=(jax.ShapeDtypeStruct(s.shape, jnp.float32),) * 3,
        in_specs=[VMEM, VMEM, SMEM] + [VMEM] * 4 + [ANY],
        out_specs=[VMEM] * 3,
        input_output_aliases={4: 0, 5: 1, 6: 2},
        compiler_params=pltpu.CompilerParams(vmem_limit_bytes=28 * MIB),
        name="inside",
    )(s, lab, kap, rims, h, g, t, after)


def last_kernel(t_ref, h_ref, g_ref, rims, out, buf, sem):
    L, R, W = t_ref.shape

    def send(l):
        return pltpu.make_async_copy(buf.at[l], out.at[l], sem.at[l])

    def body(l, _):
        def put(r, c, value):
            buf[(l,) + tile(r, c)] = value

        def halo(c):
            return halo_rows(rims, (4, 5), pl.ds(LANES * c, LANES), l)

        layer_step(l, t_ref, h_ref, g_ref, halo, put)
        send(l).start()
        return 0

    lax.fori_loop(1, L - 1, body, 0)

    def drain(l, _):
        send(l).wait()
        return 0

    lax.fori_loop(1, L - 1, drain, 0)


def last_layers(t, h, g, rims):
    L = t.shape[0]
    return pl.pallas_call(
        last_kernel,
        out_shape=jax.ShapeDtypeStruct(t.shape, jnp.float32),
        in_specs=[VMEM] * 4,
        out_specs=HBM,
        scratch_shapes=[pltpu.VMEM(t.shape, jnp.float32), pltpu.SemaphoreType.DMA((L,))],
        compiler_params=pltpu.CompilerParams(vmem_limit_bytes=24 * MIB),
        cost_estimate=lasts(5.5),
        name="last_layers",
    )(t, h, g, rims)


def near_of(side):
    me = lax.axis_index("tier")
    return (me ^ 1, me ^ 2) if side == 0 else (me ^ 2, me ^ 1)


def entries(tiers):
    me = lax.axis_index("tier")
    if tiers != 4:
        return [(2 * me + i, j) for i in range(2) for j in range(2 * tiers)]
    listed = []
    for side in range(2):
        near, target = near_of(side)
        columns = [2 * me, 2 * me + 1, 2 * near, 2 * near + 1]
        for who in (target, me):
            listed += [(2 * who + i, j) for i in range(2) for j in columns]
    return listed


def table_kernel(tiers, ops, table, rim_table):
    regions = ops.shape[0]
    me = lax.axis_index("tier")
    for k, (i, j) in enumerate(entries(tiers)):
        for g in range(regions):
            table[k, g] = jnp.full((ROWS, LANES), ops[g, i, j], jnp.float32)
    lane, upper = lane_ids(), row_ids() < 4
    for q in range(tiers):
        source = me ^ q if tiers == 4 else q
        for k in range(2):
            value = jnp.zeros((ROWS, LANES), jnp.float32)
            for g in range(regions):
                a, b = ops[g, 2 * me, 2 * source + k], ops[g, 2 * me + 1, 2 * source + 1 - k]
                value = jnp.where(lane == g, jnp.where(upper, a, b), value)
            rim_table[2 * q + k] = value


def make_tables(tiers, ops):
    regions = ops.shape[0]
    count = 32 if tiers == 4 else 4 * tiers
    return pl.pallas_call(
        functools.partial(table_kernel, tiers),
        out_shape=(
            jax.ShapeDtypeStruct((count, regions, ROWS, LANES), jnp.float32),
            jax.ShapeDtypeStruct((2 * tiers, ROWS, LANES), jnp.float32),
        ),
        in_specs=[SMEM],
        out_specs=[VMEM, VMEM],
        compiler_params=pltpu.CompilerParams(vmem_limit_bytes=16 * MIB),
        cost_estimate=lasts(1.4),
        name="make_tables",
    )(ops)


def product(table, at, zone, refs, partial, base, c, S, put):
    regions = table.shape[1]
    lanes = pl.ds(pl.multiple_of(c * LANES, LANES), LANES)
    whole = pl.ds(pl.multiple_of(base + c * LANES, LANES), LANES)
    for r0 in range(0, S, 2):
        rows = [pl.ds(ROWS * r, ROWS) for r in range(r0, min(S, r0 + 2))]
        zones = [zone[x, whole] for x in rows]
        for i in range(2):
            totals = [None] * len(rows)
            for j, (ref, index) in enumerate(refs):
                values = [table[at + i * len(refs) + j, g] for g in range(regions)]
                for k, x in enumerate(rows):
                    term = choose(values, zones[k]) * ref[index, x, lanes]
                    totals[k] = term if totals[k] is None else totals[k] + term
            for k, x in enumerate(rows):
                for ref in partial:
                    totals[k] = totals[k] + ref[i, x, lanes]
                put(i, x, lanes, whole, totals[k])


def combine_kernel(table, zone, left, left_x, right, right_y, _, to_y, to_x):
    _, R, half = left.shape

    def body(c, _):
        for side, (out, own, other) in enumerate(((to_y, left, left_x), (to_x, right, right_y))):

            def put(i, rows, lanes, whole, value, out=out):
                out[i, rows, lanes] = value

            refs = [(own, 0), (own, 1), (other, 0), (other, 1)]
            product(table, 16 * side, zone, refs, [], side * half, c, R // ROWS, put)
        return 0

    lax.fori_loop(0, half // LANES, body, 0)


def combine(table, zone, left, left_x, right, right_y, after):
    return pl.pallas_call(
        combine_kernel,
        out_shape=(jax.ShapeDtypeStruct(left.shape, jnp.float32),) * 2,
        in_specs=[VMEM] * 6 + [ANY],
        out_specs=[VMEM, VMEM],
        compiler_params=pltpu.CompilerParams(vmem_limit_bytes=16 * MIB),
        cost_estimate=lasts(0.75),
        name="combine",
    )(table, zone, left, left_x, right, right_y, after)


def solve(tiers, table, zone, groups, R, half, put, after=None):
    for side, group in enumerate(groups):
        if tiers == 4:
            own, other, part = group
            refs, partial, at = [(own, 0), (own, 1), (other, 0), (other, 1)], [part], 16 * side + 8
        else:
            refs, partial, at = [(group[0], k) for k in range(2 * tiers)], [], 0

        def body(c, _):
            product(table, at, zone, refs, partial, side * half, c, R // ROWS, put)
            return 0

        lax.fori_loop(0, half // LANES, body, 0)
        if after is not None:
            after(side)


def bond_kernel(tiers, zone, table, rim_table, aux, heat, h_ref, t_in, *refs):
    pairs = tiers == 4
    per = 3 if pairs else 1
    groups, refs = (refs[:per], refs[per : 2 * per]), refs[2 * per :]
    edge_refs, (t, out_left, out_right, rim) = refs[:-4], refs[-4:]
    L, R, W = t.shape
    half, C = W // 2, W // LANES
    row = row_ids()

    def put(i, rows, lanes, whole, value):
        t[i * (L - 1), rows, whole] = value

    solve(tiers, table, zone, groups, R, half, put)
    gone = ((row % 4 == 0) & jnp.logical_not(above_exists())) | ((row % 4 == 3) & jnp.logical_not(below_exists()))

    for c in range(C):
        lanes = pl.ds(c * LANES, LANES)
        if pairs:
            tiles = [ref[:, lanes] for ref in edge_refs]
        else:
            tiles = [edge_refs[0][q, :, lanes] for q in range(tiers)]
        zones = aux[:, lanes].astype(jnp.int32)
        zones = jnp.where(row < 4, pltpu.roll(zones, 4, 0), zones)
        value = None
        for q, mine in enumerate(tiles):
            for k, x in enumerate((mine, pltpu.roll(mine, 4, 0))):
                entry = jnp.take_along_axis(rim_table[2 * q + k], zones, axis=1, mode="promise_in_bounds")
                value = entry * x if value is None else value + entry * x
        value = jnp.where(gone, 0.0, value)
        rim[:, lanes] = value
        for i in range(2):
            t[i * (L - 1), pl.ds(0, 1), lanes] = value[4 * i + 1 : 4 * i + 2]
            t[i * (L - 1), pl.ds(R - 1, 1), lanes] = value[4 * i + 2 : 4 * i + 3]

    for p in range(2):
        own, near = (0, 1) if p == 0 else (L - 1, L - 2)

        def get_s(r, c):
            return t[(p * (L - 1),) + tile(r, c)]

        def get_h(r, c):
            return h_ref[(own,) + tile(r, c)]

        def get_z(r, c, s, h):
            at = (near,) + tile(r, c)
            flow = (h + h_ref[at]) * (t[at] - s)
            return flow + heat[tile(r, c)] if p == 0 else flow

        def halo(c):
            lanes = pl.ds(LANES * c, LANES)
            sides, walls = rim[:, lanes], aux[:, lanes]
            return (
                pltpu.roll(sides, -4 * p % ROWS, 0),
                pltpu.roll(walls, -p % ROWS, 0),
                pltpu.roll(sides, ROWS - 1 - (4 * p + 3), 0),
                pltpu.roll(walls, ROWS - 1 - (2 + p), 0),
            )

        def put_out(r, c, value):
            if c < C // 2:
                out_left[(p,) + tile(r, c)] = value
            else:
                out_right[(p,) + tile(r, c - C // 2)] = value

        stencil(R, W, get_s, get_h, get_z, halo, put_out)


def bond(tiers, zone, tables, aux, heat, h, t, left, right, edges):
    R, W = zone.shape
    args = (zone, *tables, aux, heat, h, t, *left, *right, *edges)
    f32 = jnp.float32
    return pl.pallas_call(
        functools.partial(bond_kernel, tiers),
        out_shape=(
            jax.ShapeDtypeStruct(t.shape, f32),
            jax.ShapeDtypeStruct((2, R, W // 2), f32),
            jax.ShapeDtypeStruct((2, R, W // 2), f32),
        ),
        in_specs=[VMEM] * len(args),
        out_specs=[VMEM] * 3,
        input_output_aliases={6: 0},
        scratch_shapes=[pltpu.VMEM((ROWS, W), f32)],
        compiler_params=pltpu.CompilerParams(vmem_limit_bytes=20 * MIB),
        cost_estimate=lasts(3.3),
        name="bond",
    )(*args)


def final_kernel(tiers, zone, table, *refs):
    per = 3 if tiers == 4 else 1
    groups = refs[:per], refs[per : 2 * per]
    _, out, buf, sem = refs[2 * per :]
    L, R, W = out.shape
    half = W // 2
    copies = []

    def put(i, rows, lanes, whole, value):
        buf[i, rows, whole] = value

    def after(side):
        lanes = pl.ds(side * half, half)
        for i in range(2):
            copies.append(
                pltpu.make_async_copy(
                    buf.at[i, :, lanes], out.at[i * (L - 1), :, lanes], sem.at[2 * side + i]
                )
            )
            copies[-1].start()

    solve(tiers, table, zone, groups, R, half, put, after)
    for copy in copies:
        copy.wait()


def final_planes(tiers, zone, table, left, right, out):
    args = (zone, table, *left, *right, out)
    _, R, W = out.shape
    return pl.pallas_call(
        functools.partial(final_kernel, tiers),
        out_shape=jax.ShapeDtypeStruct(out.shape, jnp.float32),
        in_specs=[VMEM] * (len(args) - 1) + [HBM],
        out_specs=HBM,
        scratch_shapes=[pltpu.VMEM((2, R, W), jnp.float32), pltpu.SemaphoreType.DMA((4,))],
        input_output_aliases={len(args) - 1: 0},
        compiler_params=pltpu.CompilerParams(vmem_limit_bytes=16 * MIB),
        cost_estimate=lasts(1.6),
        name="final_planes",
    )(*args)


def across(value, bits, tiers):
    return lax.ppermute(value, "tier", [(i, i ^ bits) for i in range(tiers)])


def every(value, tiers):
    gathered = lax.all_gather(value, "tier", axis=0, tiled=False)
    return gathered.reshape((tiers * value.shape[0],) + value.shape[1:]) if value.ndim == 3 else gathered


def exchange(tiers, table, zone, left, right, after):
    if tiers != 4:
        return (every(left, tiers),), (every(right, tiers),), left
    left_x, right_y = across(left, 1, tiers), across(right, 2, tiers)
    to_y, to_x = combine(table, zone, left, left_x, right, right_y, after)
    return (left, left_x, across(to_y, 2, tiers)), (right, right_y, across(to_x, 1, tiers)), to_y


def local(warming, substance, zone, patch, kap, power, ops):
    tiers, tiles = lax.axis_size("tier"), lax.axis_size("tile")
    s, lab, patch = warming[0], substance[0], patch[0]

    left, right, heat, swap_a, swap_b, s, lab = begin(s, lab, patch, zone, kap, power)
    pairs = [(i, i ^ 1) for i in range(tiles) if i ^ 1 < tiles]
    got_a = lax.ppermute(swap_a, "tile", pairs)
    pairs = [(i, ((i - 1) ^ 1) + 1) for i in range(1, tiles - 1 + tiles % 2)]
    got_b = lax.ppermute(swap_b, "tile", pairs)
    tables = make_tables(tiers, ops)
    left, right, sent = exchange(tiers, tables[0], zone, left, right, heat)
    edges, rims, aux = edge_rows(swap_a, swap_b, got_a, got_b)
    h, g = faces(lab, kap, edges, sent)
    if tiers == 4:
        edges = (edges, across(edges, 1, tiers), across(edges, 2, tiers), across(edges, 3, tiers))
    else:
        edges = (every(edges, tiers),)
    t = outer(s, h, g, rims)
    t, left, right = bond(tiers, zone, tables, aux, heat, h, t, left, right, edges)
    h, g, t = inside(s, lab, kap, rims, h, g, t, left)
    left, right, _ = exchange(tiers, tables[0], zone, left, right, t)
    out = last_layers(t, h, g, rims)
    out = final_planes(tiers, zone, tables[0], left, right, out)
    return out[None]


def solution(mesh):
    in_specs = (
        P("tier", None, "tile", None),
        P("tier", None, "tile", None),
        P("tile", None),
        P("tier", "tile", None),
        P(),
        P("tier", None),
        P(),
    )
    out_specs = P("tier", None, "tile", None)
    return jax.shard_map(local, mesh=mesh, in_specs=in_specs, out_specs=out_specs, check_vma=False)
```

```python
import functools
import math

import jax
import jax.numpy as jnp
from jax import lax
from jax.experimental import pallas as pl
from jax.experimental.pallas import tpu as pltpu
from jax.sharding import PartitionSpec as P

STEPS = 2
step_dt = 0.04
half_dt = 0.5 * step_dt
LANES = 128
ROWS = 8
MIB = 1 << 20

VMEM = pl.BlockSpec(memory_space=pltpu.VMEM)
SMEM = pl.BlockSpec(memory_space=pltpu.SMEM)
ANY = pl.BlockSpec(memory_space=pl.ANY)
HBM = pl.BlockSpec(memory_space=pltpu.HBM)


def tile(r, c):
    return pl.ds(ROWS * r, ROWS), pl.ds(LANES * c, LANES)


def lane_ids():
    return lax.broadcasted_iota(jnp.int32, (ROWS, LANES), 1)


def row_ids():
    return lax.broadcasted_iota(jnp.int32, (ROWS, LANES), 0)


def choose(values, labels):
    values, bit = list(values), 1
    while len(values) > 1:
        odd = (labels & bit) != 0
        paired = [
            jnp.where(odd, values[i + 1], values[i]) if i + 1 < len(values) else values[i]
            for i in range(0, len(values), 2)
        ]
        values, bit = paired, 2 * bit
    return values[0]


def lookup(row, labels):
    return jnp.take_along_axis(row, labels, axis=1, mode="promise_in_bounds")


def splats(kap):
    return [jnp.full((ROWS, LANES), half_dt * kap[i], jnp.float32) for i in range(kap.shape[0])]


def stencil(R, W, get_s, get_h, get_z, halo, put, get_g=None, put_g=None):
    C, S = W // LANES, R // ROWS
    lane, row = lane_ids(), row_ids()
    first, last = lane == 0, lane == LANES - 1
    top, bottom = row == 0, row == ROWS - 1
    before = None
    for c in range(C):
        s = [get_s(r, c) for r in range(S)]
        h = [get_h(r, c) for r in range(S)]
        rs = [pltpu.roll(v, 1, 1) for v in s]
        rh = [pltpu.roll(v, 1, 1) for v in h] if get_g is None else None
        us = [pltpu.roll(v, 1, 0) for v in s]
        uh = [pltpu.roll(v, 1, 0) for v in h]
        if halo is not None:
            sa, ha, sb, hb = halo(c)
        acc, back, down = [], [], []
        for r in range(S):
            sl = jnp.where(first, 0.0 if c == 0 else before[0][r], rs[r])
            if get_g is None:
                g = h[r] + jnp.where(first, 0.0 if c == 0 else before[1][r], rh[r])
                if put_g is not None:
                    put_g(r, c, g)
            else:
                g = get_g(r, c)
            face = g * (sl - s[r])
            back.append(pltpu.roll(face, LANES - 1, 1))
            if r == 0:
                if halo is None:
                    su, hu = us[0], uh[0]
                else:
                    su, hu = jnp.where(top, sa, us[0]), jnp.where(top, ha, uh[0])
            else:
                su, hu = jnp.where(top, us[r - 1], us[r]), jnp.where(top, uh[r - 1], uh[r])
            upper = (h[r] + hu) * (su - s[r])
            down.append(pltpu.roll(upper, ROWS - 1, 0))
            acc.append((s[r] + get_z(r, c, s[r], h[r])) + (face + upper))
        for r in range(S):
            if r + 1 < S:
                lower = jnp.where(bottom, down[r + 1], down[r])
            elif halo is None:
                lower = down[r]
            else:
                lower = jnp.where(bottom, (h[r] + hb) * (s[r] - sb), down[r])
            acc[r] = acc[r] - lower
        if before is not None:
            for r in range(S):
                put(r, c - 1, before[3][r] - jnp.where(last, back[r], before[2][r]))
        before = (rs, rh, back, acc, s, h)
    for r in range(S):
        out = before[5][r] * before[4][r]
        put(r, C - 1, before[3][r] - jnp.where(last, out, before[2][r]))


def vertical(s, h, s_up, h_up, s_down, h_down):
    return (h + h_up) * (s_up - s) + (h + h_down) * (s_down - s)


def begin_kernel(
    s_hbm, lab_hbm, patch_hbm, zone_hbm, kap_hbm, power_hbm,
    planes, heat, swap_a, swap_b, s_v, lab_v,
    patch, zone_v, kap, power, sem,
):
    L, R, W = s_hbm.shape
    C = W // LANES
    starts = (0, R - ROWS)
    small = [
        pltpu.make_async_copy(kap_hbm, kap, sem.at[0]),
        pltpu.make_async_copy(power_hbm, power, sem.at[1]),
        pltpu.make_async_copy(patch_hbm, patch, sem.at[2]),
    ]
    groups = [(0, 2), (L - 2, 2), (2, L - 4)]
    layers = [
        [
            pltpu.make_async_copy(s_hbm.at[pl.ds(l, n)], s_v.at[pl.ds(l, n)], sem.at[3 + 2 * k]),
            pltpu.make_async_copy(lab_hbm.at[pl.ds(l, n)], lab_v.at[pl.ds(l, n)], sem.at[4 + 2 * k]),
        ]
        for k, (l, n) in enumerate(groups)
    ]
    layers[2] += [
        pltpu.make_async_copy(zone_hbm.at[pl.ds(start, ROWS)], zone_v.at[k], sem.at[9 + k])
        for k, start in enumerate(starts)
    ]
    for copy in small + layers[0] + layers[1] + layers[2]:
        copy.start()
    for copy in small:
        copy.wait()
    values = splats(kap)
    heats = step_dt * jnp.broadcast_to(power[...], (ROWS, LANES))
    for p in range(2):
        for copy in layers[p]:
            copy.wait()
        own, near = (0, 1) if p == 0 else (L - 1, L - 2)

        def get_s(r, c):
            return s_v[(own,) + tile(r, c)]

        def get_h(r, c):
            return choose(values, lab_v[(own,) + tile(r, c)])

        def get_z(r, c, s, h):
            h_near = choose(values, lab_v[(near,) + tile(r, c)])
            flow = (h + h_near) * (s_v[(near,) + tile(r, c)] - s)
            if p == 0:
                value = lookup(heats, patch[tile(r, c)])
                heat[tile(r, c)] = value
                flow = flow + value
            return flow

        def put(r, c, value):
            planes[(p,) + tile(r, c)] = value

        stencil(R, W, get_s, get_h, get_z, None, put)
    row = row_ids()
    for copy in layers[2]:
        copy.wait()

    def pack(k, out):
        rows = ((0, 1), (ROWS - 2, ROWS - 1))[k]

        def body(c, _):
            lanes = pl.ds(pl.multiple_of(c * LANES, LANES), LANES)
            edge = pl.ds(starts[k], ROWS)
            for base in range(0, L, ROWS):
                for ref, at in ((s_v, 0), (lab_v, 2 * L)):
                    tiles = [ref[base + q, edge, lanes] for q in range(ROWS)]
                    for j, source in enumerate(rows):
                        packed = tiles[source]
                        for q in range(ROWS):
                            if q != source:
                                packed = jnp.where(row == q, pltpu.roll(tiles[q], (q - source) % ROWS, 0), packed)
                        if ref is lab_v:
                            packed = choose(values, packed)
                        out[pl.ds(at + j * L + base, ROWS), lanes] = packed
            last = rows[0] if k == 0 else rows[1]
            warm = heat[edge, lanes]
            zones = zone_v[k, :, lanes].astype(jnp.float32)
            pair = jnp.where(row == 0, pltpu.roll(warm, -last % ROWS, 0), pltpu.roll(zones, (1 - last) % ROWS, 0))
            out[pl.ds(4 * L, ROWS), lanes] = pair
            return 0

        lax.fori_loop(0, W // LANES, body, 0)

    odd = lax.axis_index("tile") % 2 == 1

    @pl.when(odd)
    def _():
        pack(0, swap_a)
        pack(1, swap_b)

    @pl.when(jnp.logical_not(odd))
    def _():
        pack(1, swap_a)
        pack(0, swap_b)


def begin(s, lab, patch, zone, kap, power):
    L, R, W = s.shape
    f32, i32 = jnp.float32, jnp.int32
    packed = pltpu.VMEM((4 * L + ROWS, W), f32)
    args = [pltpu.with_memory_space_constraint(x, pltpu.HBM) for x in (s, lab, patch, zone, kap, power)]
    return pl.pallas_call(
        begin_kernel,
        out_shape=(
            pltpu.VMEM((2, R, W), f32), pltpu.VMEM((R, W), f32), packed, packed, pltpu.VMEM(s.shape, f32), pltpu.VMEM(lab.shape, i32)
        ),
        in_specs=[HBM] * 6,
        out_specs=[VMEM] * 6,
        scratch_shapes=[
            pltpu.VMEM((R, W), i32),
            pltpu.VMEM((2, ROWS, W), i32),
            pltpu.SMEM(kap.shape, f32),
            pltpu.VMEM(power.shape, f32),
            pltpu.SemaphoreType.DMA((11,)),
        ],
        compiler_params=pltpu.CompilerParams(vmem_limit_bytes=16 * MIB),
        name="begin",
    )(*args)


def above_exists():
    return lax.axis_index("tile") > 0


def below_exists():
    return lax.axis_index("tile") < lax.axis_size("tile") - 1


def edge_kernel(own_a, own_b, got_a, got_b, edges, rims, aux):
    rows, W = own_a.shape
    L = (rows - ROWS) // 4
    col = lax.broadcasted_iota(jnp.int32, (L, W), 1)
    layer = lax.broadcasted_iota(jnp.int32, (L, W), 0)
    odd = lax.axis_index("tile") % 2 == 1

    def step(s_a, h_a, s, h, s_b, h_b):
        def toward(s_n, h_n):
            return (h + h_n) * (s_n - s)

        def moved(shift, axis, gone):
            return jnp.where(gone, 0.0, pltpu.roll(s, shift, axis)), jnp.where(
                gone, 0.0, pltpu.roll(h, shift, axis)
            )

        total = s + toward(s_a, h_a) + toward(s_b, h_b)
        total = total + toward(*moved(1, 1, col == 0)) + toward(*moved(W - 1, 1, col == W - 1))
        under = jnp.where(layer == 0, 0.0, toward(pltpu.roll(s, 1, 0), pltpu.roll(h, 1, 0)))
        over = jnp.where(layer == L - 1, 0.0, toward(pltpu.roll(s, L - 1, 0), pltpu.roll(h, L - 1, 0)))
        return total + under + over

    for side, exists in enumerate((above_exists(), below_exists())):
        first_swap = odd if side == 0 else jnp.logical_not(odd)

        def other(at, n):
            at = pl.ds(at, n)
            return jnp.where(exists, jnp.where(first_swap, got_a[at, :], got_b[at, :]), 0.0)

        def own(at, n):
            at = pl.ds(at, n)
            return jnp.where(first_swap, own_a[at, :], own_b[at, :])

        far, near = (0, 1) if side == 0 else (1, 0)
        sf, sn, hf, hn = (other(k * L, L) for k in (far, near, 2 + far, 2 + near))
        s0, s1, h0, h1 = (own(k * L, L) for k in (1 - near, near, 3 - near, 2 + near))
        out = jnp.where(exists, step(sf, hf, sn, hn, s0, h0), 0.0)
        inner = step(sn, hn, s0, h0, s1, h1)
        rims[2 * side] = sn
        rims[2 * side + 1] = hn
        rims[4 + side] = out
        k_out, k_in = (0, 1) if side == 0 else (3, 2)
        edges[pl.ds(k_out, 1), :] = out[0:1] + other(4 * L, 1)
        edges[pl.ds(k_in, 1), :] = inner[0:1] + own(4 * L, 1)
        edges[pl.ds(4 + k_out, 1), :] = out[L - 1 : L]
        edges[pl.ds(4 + k_in, 1), :] = inner[L - 1 : L]
        aux[pl.ds(2 * side, 1), :] = hn[0:1]
        aux[pl.ds(2 * side + 1, 1), :] = hn[L - 1 : L]
        aux[pl.ds(4 + k_out, 1), :] = other(4 * L + 1, 1)
        aux[pl.ds(4 + k_in, 1), :] = own(4 * L + 1, 1)


def edge_rows(own_a, own_b, got_a, got_b):
    rows, W = own_a.shape
    L = (rows - ROWS) // 4
    f32 = jnp.float32
    return pl.pallas_call(
        edge_kernel,
        out_shape=(
            jax.ShapeDtypeStruct((ROWS, W), f32),
            jax.ShapeDtypeStruct((6, L, W), f32),
            jax.ShapeDtypeStruct((ROWS, W), f32),
        ),
        in_specs=[VMEM] * 4,
        out_specs=[VMEM] * 3,
        compiler_params=pltpu.CompilerParams(vmem_limit_bytes=16 * MIB),
        name="edge_rows",
    )(own_a, own_b, got_a, got_b)


def pick(ref, base, l, lanes, row):
    at = base + (l // ROWS) * ROWS
    if not isinstance(l, int):
        at = pl.multiple_of(at, ROWS)
    return pltpu.roll(ref[pl.ds(at, ROWS), lanes], (row - l) % ROWS, 0)


def halo_rows(rims, state, lanes, l):
    end = ROWS - 1
    where = ((state[0], 0), (1, 0), (state[1], end), (3, end))
    return tuple(pick(rims.at[k], 0, l, lanes, row) for k, row in where)


def fill_faces(first, end, lab, values, h_out, g_out):
    _, R, W = lab.shape
    edge = lane_ids() == 0

    def body(l, _):
        for r in range(R // ROWS):
            before = 0.0
            for c in range(W // LANES):
                at = (l,) + tile(r, c)
                h = choose(values, lab[at])
                moved = pltpu.roll(h, 1, 1)
                h_out[at] = h
                g_out[at] = h + jnp.where(edge, before, moved)
                before = moved
        return 0

    lax.fori_loop(first, end, body, 0)


def faces_kernel(lab, kap, h_out, g_out):
    fill_faces(0, lab.shape[0], lab, splats(kap), h_out, g_out)


def faces(lab, kap):
    return pl.pallas_call(
        faces_kernel,
        out_shape=(jax.ShapeDtypeStruct(lab.shape, jnp.float32),) * 2,
        in_specs=[VMEM, SMEM],
        out_specs=[VMEM] * 2,
        compiler_params=pltpu.CompilerParams(vmem_limit_bytes=20 * MIB),
        name="faces",
    )(lab, kap)


def layer_step(l, s_ref, h_ref, g_ref, halo, put):
    _, R, W = s_ref.shape

    def get_s(r, c):
        return s_ref[(l,) + tile(r, c)]

    def get_h(r, c):
        return h_ref[(l,) + tile(r, c)]

    def get_g(r, c):
        return g_ref[(l,) + tile(r, c)]

    def get_z(r, c, s, h):
        a, b = (l - 1,) + tile(r, c), (l + 1,) + tile(r, c)
        return vertical(s, h, s_ref[a], h_ref[a], s_ref[b], h_ref[b])

    stencil(R, W, get_s, get_h, get_z, halo, put, get_g=get_g)


def first_step(l, s_ref, h_ref, g_ref, rims, t):
    def put(r, c, value):
        t[(l,) + tile(r, c)] = value

    def halo(c):
        return halo_rows(rims, (0, 2), pl.ds(LANES * c, LANES), l)

    layer_step(l, s_ref, h_ref, g_ref, halo, put)


def outer_kernel(s_ref, h_ref, g_ref, rims, t):
    L = s_ref.shape[0]

    def body(k, _):
        first_step(1 + k * (L - 3), s_ref, h_ref, g_ref, rims, t)
        return 0

    lax.fori_loop(0, 2, body, 0)


def outer(s, h, g, rims):
    return pl.pallas_call(
        outer_kernel,
        out_shape=jax.ShapeDtypeStruct(s.shape, jnp.float32),
        in_specs=[VMEM] * 4,
        out_specs=VMEM,
        compiler_params=pltpu.CompilerParams(vmem_limit_bytes=20 * MIB),
        name="outer",
    )(s, h, g, rims)


def inside_kernel(s_ref, h_ref, g_ref, rims, t_in, _, t):
    L = s_ref.shape[0]

    def body(l, _):
        first_step(l, s_ref, h_ref, g_ref, rims, t)
        return 0

    lax.fori_loop(2, L - 2, body, 0)


def inside(s, h, g, rims, t, after):
    return pl.pallas_call(
        inside_kernel,
        out_shape=jax.ShapeDtypeStruct(s.shape, jnp.float32),
        in_specs=[VMEM] * 5 + [ANY],
        out_specs=VMEM,
        input_output_aliases={4: 0},
        compiler_params=pltpu.CompilerParams(vmem_limit_bytes=24 * MIB),
        name="inside",
    )(s, h, g, rims, t, after)


def last_kernel(t_ref, h_ref, g_ref, rims, out, buf, sem):
    L, R, W = t_ref.shape

    def send(l):
        return pltpu.make_async_copy(buf.at[l], out.at[l], sem.at[l])

    def body(l, _):
        def put(r, c, value):
            buf[(l,) + tile(r, c)] = value

        def halo(c):
            return halo_rows(rims, (4, 5), pl.ds(LANES * c, LANES), l)

        layer_step(l, t_ref, h_ref, g_ref, halo, put)
        send(l).start()
        return 0

    lax.fori_loop(1, L - 1, body, 0)

    def drain(l, _):
        send(l).wait()
        return 0

    lax.fori_loop(1, L - 1, drain, 0)


def last_layers(t, h, g, rims):
    L = t.shape[0]
    return pl.pallas_call(
        last_kernel,
        out_shape=jax.ShapeDtypeStruct(t.shape, jnp.float32),
        in_specs=[VMEM] * 4,
        out_specs=HBM,
        scratch_shapes=[pltpu.VMEM(t.shape, jnp.float32), pltpu.SemaphoreType.DMA((L,))],
        compiler_params=pltpu.CompilerParams(vmem_limit_bytes=24 * MIB),
        name="last_layers",
    )(t, h, g, rims)


def near_of(side):
    me = lax.axis_index("tier")
    return (me ^ 1, me ^ 2) if side == 0 else (me ^ 2, me ^ 1)


def routes(tier, tile):
    odd = tile % 2
    return tier ^ (1 + odd), tier ^ (2 - odd)


def entries(tiers):
    me = lax.axis_index("tier")
    if tiers != 4:
        return [(2 * me + i, j) for i in range(2) for j in range(2 * tiers)]
    listed = []
    for side in range(2):
        near, target = near_of(side)
        columns = [2 * me, 2 * me + 1, 2 * near, 2 * near + 1]
        for who in (target, me):
            listed += [(2 * who + i, j) for i in range(2) for j in columns]
    return listed


def rim_entries(tiers):
    me = lax.axis_index("tier")
    if tiers != 4:
        return [(me, q) for q in range(tiers)]
    near, target = routes(me, lax.axis_index("tile"))
    return [(who, source) for who in (target, me) for source in (me, near)]


def table_kernel(tiers, ops, table, rim_table):
    regions = ops.shape[0]
    for k, (i, j) in enumerate(entries(tiers)):
        for g in range(regions):
            table[k, g] = jnp.full((ROWS, LANES), ops[g, i, j], jnp.float32)
    lane, upper = lane_ids(), row_ids() < 4
    for q, (who, source) in enumerate(rim_entries(tiers)):
        for k in range(2):
            value = jnp.zeros((ROWS, LANES), jnp.float32)
            for g in range(regions):
                a, b = ops[g, 2 * who, 2 * source + k], ops[g, 2 * who + 1, 2 * source + 1 - k]
                value = jnp.where(lane == g, jnp.where(upper, a, b), value)
            rim_table[2 * q + k] = value


def make_tables(tiers, ops):
    regions = ops.shape[0]
    f32 = jnp.float32
    count, rims = (32, 8) if tiers == 4 else (4 * tiers, 2 * tiers)
    return pl.pallas_call(
        functools.partial(table_kernel, tiers),
        out_shape=(pltpu.VMEM((count, regions, ROWS, LANES), f32), pltpu.VMEM((rims, ROWS, LANES), f32)),
        in_specs=[SMEM],
        out_specs=[VMEM, VMEM],
        compiler_params=pltpu.CompilerParams(vmem_limit_bytes=16 * MIB),
        name="make_tables",
    )(ops)


def product(table, at, zone, refs, partial, base, put):
    regions = table.shape[1]
    R, W = refs[0][0].shape[1:]
    S = R // ROWS

    def body(c, _):
        lanes = pl.ds(pl.multiple_of(c * LANES, LANES), LANES)
        whole = pl.ds(pl.multiple_of(base + c * LANES, LANES), LANES)
        for r0 in range(0, S, 2):
            rows = [pl.ds(ROWS * r, ROWS) for r in range(r0, min(S, r0 + 2))]
            zones = [zone[x, whole] for x in rows]
            for i in range(2):
                totals = [None] * len(rows)
                for j, (ref, index) in enumerate(refs):
                    values = [table[at + i * len(refs) + j, g] for g in range(regions)]
                    for k, x in enumerate(rows):
                        term = choose(values, zones[k]) * ref[index, x, lanes]
                        totals[k] = term if totals[k] is None else totals[k] + term
                for k, x in enumerate(rows):
                    for ref in partial:
                        totals[k] = totals[k] + ref[i, x, lanes]
                    put(i, x, lanes, whole, totals[k])
        return 0

    lax.fori_loop(0, W // LANES, body, 0)


def both(own, near):
    return [(own, 0), (own, 1), (near, 0), (near, 1)]


def put_in(out):
    def put(i, rows, lanes, whole, value):
        out[i, rows, lanes] = value

    return put


def way_of_tile():
    return lax.axis_index("tile") % 2


def combine_kernel(table, zone, own, near, _, out):
    product(table, 16 * way_of_tile(), zone, both(own, near), [], 0, put_in(out))


def combine(table, zone, own, near, after):
    return pl.pallas_call(
        combine_kernel,
        out_shape=pltpu.VMEM(own.shape, jnp.float32),
        in_specs=[VMEM] * 4 + [ANY],
        out_specs=VMEM,
        compiler_params=pltpu.CompilerParams(vmem_limit_bytes=16 * MIB),
        name="combine",
    )(table, zone, own, near, after)


def combine_halves_kernel(table, zone, left, left_x, right, right_y, _, to_y, to_x):
    product(table, 0, zone, both(left, left_x), [], 0, put_in(to_y))
    product(table, 16, zone, both(right, right_y), [], left.shape[2], put_in(to_x))


def combine_halves(table, zone, left, left_x, right, right_y, after):
    return pl.pallas_call(
        combine_halves_kernel,
        out_shape=(pltpu.VMEM(left.shape, jnp.float32),) * 2,
        in_specs=[VMEM] * 6 + [ANY],
        out_specs=[VMEM, VMEM],
        compiler_params=pltpu.CompilerParams(vmem_limit_bytes=16 * MIB),
        name="combine_halves",
    )(table, zone, left, left_x, right, right_y, after)


def rim_product(rim_table, pairs, aux, lanes):
    zones = aux[:, lanes].astype(jnp.int32)
    zones = jnp.where(row_ids() < 4, pltpu.roll(zones, 4, 0), zones)
    value = None
    for at, planes in pairs:
        for k, x in enumerate((planes, pltpu.roll(planes, 4, 0))):
            term = lookup(rim_table[at + k], zones) * x
            value = term if value is None else value + term
    return value


def combine_rim_kernel(rim_table, aux, own, near, out):
    for c in range(own.shape[1] // LANES):
        lanes = pl.ds(c * LANES, LANES)
        out[:, lanes] = rim_product(rim_table, [(0, own[:, lanes]), (2, near[:, lanes])], aux, lanes)


def combine_rim(rim_table, aux, own, near):
    return pl.pallas_call(
        combine_rim_kernel,
        out_shape=pltpu.VMEM(own.shape, jnp.float32),
        in_specs=[VMEM] * 4,
        out_specs=VMEM,
        compiler_params=pltpu.CompilerParams(vmem_limit_bytes=16 * MIB),
        name="combine_rim",
    )(rim_table, aux, own, near)


def bond_kernel(tiers, zone, table, rim_table, aux, heat, h_ref, g_ref, t_in, *refs):
    pairs = tiers == 4
    per = 3 if pairs else 1
    arrays, edges, (t, left, right, rim) = refs[:per], refs[per : 2 * per], refs[2 * per :]
    L, R, W = t.shape
    C = W // LANES
    row = row_ids()

    def put(i, rows, lanes, whole, value):
        t[i * (L - 1), rows, lanes] = value

    if pairs:
        own, near, part = arrays
        product(table, 16 * way_of_tile() + 8, zone, both(own, near), [part], 0, put)
    else:
        product(table, 0, zone, [(arrays[0], k) for k in range(2 * tiers)], [], 0, put)
    gone = ((row % 4 == 0) & jnp.logical_not(above_exists())) | ((row % 4 == 3) & jnp.logical_not(below_exists()))

    for c in range(C):
        lanes = pl.ds(c * LANES, LANES)
        if pairs:
            tiles = [(4, edges[0][:, lanes]), (6, edges[1][:, lanes])]
            value = rim_product(rim_table, tiles, aux, lanes) + edges[2][:, lanes]
        else:
            value = rim_product(rim_table, [(2 * q, edges[0][q, :, lanes]) for q in range(tiers)], aux, lanes)
        value = jnp.where(gone, 0.0, value)
        rim[:, lanes] = value
        for i in range(2):
            t[i * (L - 1), pl.ds(0, 1), lanes] = value[4 * i + 1 : 4 * i + 2]
            t[i * (L - 1), pl.ds(R - 1, 1), lanes] = value[4 * i + 2 : 4 * i + 3]

    for p in range(2):
        own, near = (0, 1) if p == 0 else (L - 1, L - 2)

        def get_s(r, c):
            return t[(p * (L - 1),) + tile(r, c)]

        def get_h(r, c):
            return h_ref[(own,) + tile(r, c)]

        def get_g(r, c):
            return g_ref[(own,) + tile(r, c)]

        def get_z(r, c, s, h):
            at = (near,) + tile(r, c)
            flow = (h + h_ref[at]) * (t[at] - s)
            return flow + heat[tile(r, c)] if p == 0 else flow

        def halo(c):
            lanes = pl.ds(LANES * c, LANES)
            sides, walls = rim[:, lanes], aux[:, lanes]
            return (
                pltpu.roll(sides, -4 * p % ROWS, 0),
                pltpu.roll(walls, -p % ROWS, 0),
                pltpu.roll(sides, ROWS - 1 - (4 * p + 3), 0),
                pltpu.roll(walls, ROWS - 1 - (2 + p), 0),
            )

        def put_out(r, c, value):
            out, c = (left, c) if c < C // 2 else (right, c - C // 2)
            out[(p,) + tile(r, c)] = value

        stencil(R, W, get_s, get_h, get_z, halo, put_out, get_g=get_g)


def bond(tiers, zone, tables, aux, heat, h, g, t, arrays, edges):
    _, R, W = t.shape
    args = (zone, *tables, aux, heat, h, g, t, *arrays, *edges)
    f32 = jnp.float32
    return pl.pallas_call(
        functools.partial(bond_kernel, tiers),
        out_shape=(
            jax.ShapeDtypeStruct(t.shape, f32),
            jax.ShapeDtypeStruct((2, R, W // 2), f32),
            jax.ShapeDtypeStruct((2, R, W // 2), f32),
        ),
        in_specs=[VMEM] * len(args),
        out_specs=[VMEM] * 3,
        scratch_shapes=[pltpu.VMEM((ROWS, W), f32)],
        input_output_aliases={7: 0},
        compiler_params=pltpu.CompilerParams(vmem_limit_bytes=24 * MIB),
        name="bond",
    )(*args)


def final_kernel(tiers, zone, table, *refs):
    per = 3 if tiers == 4 else 1
    groups = refs[:per], refs[per : 2 * per]
    _, out, buf, sem = refs[2 * per :]
    L, R, W = out.shape
    half = W // 2

    def put(i, rows, lanes, whole, value):
        buf[i, rows, whole] = value

    copies = []
    for side, group in enumerate(groups):
        if tiers == 4:
            product(table, 16 * side + 8, zone, both(group[0], group[1]), [group[2]], side * half, put)
        else:
            product(table, 0, zone, [(group[0], k) for k in range(2 * tiers)], [], side * half, put)
        lanes = pl.ds(side * half, half)
        for i in range(2):
            copy = pltpu.make_async_copy(
                buf.at[i, :, lanes], out.at[i * (L - 1), :, lanes], sem.at[2 * side + i]
            )
            copy.start()
            copies.append(copy)
    for copy in copies:
        copy.wait()


def final_planes(tiers, zone, table, left, right, out):
    args = (zone, table, *left, *right, out)
    _, R, W = out.shape
    return pl.pallas_call(
        functools.partial(final_kernel, tiers),
        out_shape=jax.ShapeDtypeStruct(out.shape, jnp.float32),
        in_specs=[VMEM] * (len(args) - 1) + [HBM],
        out_specs=HBM,
        scratch_shapes=[pltpu.VMEM((2, R, W), jnp.float32), pltpu.SemaphoreType.DMA((4,))],
        input_output_aliases={len(args) - 1: 0},
        compiler_params=pltpu.CompilerParams(vmem_limit_bytes=16 * MIB),
        name="final_planes",
    )(*args)


def across(value, bits, tiers):
    return lax.ppermute(value, "tier", [(i, i ^ bits) for i in range(tiers)])


def every(value, tiers):
    gathered = lax.all_gather(value, "tier", axis=0, tiled=False)
    return gathered.reshape((tiers * value.shape[0],) + value.shape[1:]) if value.ndim == 3 else gathered


def along(value, way, tiers, tiles):
    places = [(tier, tile) for tier in range(tiers) for tile in range(tiles)]
    pairs = [(tier * tiles + tile, routes(tier, tile)[way] * tiles + tile) for tier, tile in places]
    return lax.ppermute(value, ("tier", "tile"), pairs)


def exchange(tiers, tiles, table, zone, planes, after):
    if tiers != 4:
        return (every(planes, tiers),)
    near = along(planes, 0, tiers, tiles)
    return planes, near, along(combine(table, zone, planes, near, after), 1, tiers, tiles)


def exchange_rim(tiers, tiles, rim_table, aux, edges):
    if tiers != 4:
        return (every(edges, tiers),)
    near = along(edges, 0, tiers, tiles)
    return edges, near, along(combine_rim(rim_table, aux, edges, near), 1, tiers, tiles)


def exchange_halves(tiers, table, zone, left, right, after):
    if tiers != 4:
        return (every(left, tiers),), (every(right, tiers),)
    left_x, right_y = across(left, 1, tiers), across(right, 2, tiers)
    to_y, to_x = combine_halves(table, zone, left, left_x, right, right_y, after)
    return (left, left_x, across(to_y, 2, tiers)), (right, right_y, across(to_x, 1, tiers))


def local(warming, substance, zone, patch, kap, power, ops):
    tiers, tiles = lax.axis_size("tier"), lax.axis_size("tile")
    s, lab, patch = warming[0], substance[0], patch[0]

    planes, heat, swap_a, swap_b, s, lab = begin(s, lab, patch, zone, kap, power)
    pairs = [(i, i ^ 1) for i in range(tiles) if i ^ 1 < tiles]
    got_a = lax.ppermute(swap_a, "tile", pairs)
    pairs = [(i, ((i - 1) ^ 1) + 1) for i in range(1, tiles - 1 + tiles % 2)]
    got_b = lax.ppermute(swap_b, "tile", pairs)
    tables = make_tables(tiers, ops)
    h, g = faces(lab, kap)
    arrays = exchange(tiers, tiles, tables[0], zone, planes, h)
    edges, rims, aux = edge_rows(swap_a, swap_b, got_a, got_b)
    edges = exchange_rim(tiers, tiles, tables[1], aux, edges)
    t = outer(s, h, g, rims)
    t, left, right = bond(tiers, zone, tables, aux, heat, h, g, t, arrays, edges)
    t = inside(s, h, g, rims, t, left)
    left, right = exchange_halves(tiers, tables[0], zone, left, right, t)
    out = last_layers(t, h, g, rims)
    out = final_planes(tiers, zone, tables[0], left, right, out)
    return out[None]


def solution(mesh):
    in_specs = (
        P("tier", None, "tile", None),
        P("tier", None, "tile", None),
        P("tile", None),
        P("tier", "tile", None),
        P(),
        P("tier", None),
        P(),
    )
    out_specs = P("tier", None, "tile", None)
    return jax.shard_map(local, mesh=mesh, in_specs=in_specs, out_specs=out_specs, check_vma=False)
```

```python
import functools
import math

import jax
import jax.numpy as jnp
from jax import lax
from jax.experimental import pallas as pl
from jax.experimental.pallas import tpu as pltpu
from jax.sharding import PartitionSpec as P

STEPS = 2
step_dt = 0.04
half_dt = 0.5 * step_dt
LANES = 128
ROWS = 8
MIB = 1 << 20

VMEM = pl.BlockSpec(memory_space=pltpu.VMEM)
SMEM = pl.BlockSpec(memory_space=pltpu.SMEM)
ANY = pl.BlockSpec(memory_space=pl.ANY)
HBM = pl.BlockSpec(memory_space=pltpu.HBM)


def tile(r, c):
    return pl.ds(ROWS * r, ROWS), pl.ds(LANES * c, LANES)


def lane_ids():
    return lax.broadcasted_iota(jnp.int32, (ROWS, LANES), 1)


def row_ids():
    return lax.broadcasted_iota(jnp.int32, (ROWS, LANES), 0)


def choose(values, labels):
    values, bit = list(values), 1
    while len(values) > 1:
        odd = (labels & bit) != 0
        paired = [
            jnp.where(odd, values[i + 1], values[i]) if i + 1 < len(values) else values[i]
            for i in range(0, len(values), 2)
        ]
        values, bit = paired, 2 * bit
    return values[0]


def lookup(row, labels):
    return jnp.take_along_axis(row, labels, axis=1, mode="promise_in_bounds")


def splats(kap):
    return [jnp.full((ROWS, LANES), half_dt * kap[i], jnp.float32) for i in range(kap.shape[0])]


def stencil(R, W, get_s, get_h, get_z, halo, put, get_g=None, put_g=None):
    C, S = W // LANES, R // ROWS
    lane, row = lane_ids(), row_ids()
    first, last = lane == 0, lane == LANES - 1
    top, bottom = row == 0, row == ROWS - 1
    before = None
    for c in range(C):
        s = [get_s(r, c) for r in range(S)]
        h = [get_h(r, c) for r in range(S)]
        rs = [pltpu.roll(v, 1, 1) for v in s]
        rh = [pltpu.roll(v, 1, 1) for v in h] if get_g is None else None
        us = [pltpu.roll(v, 1, 0) for v in s]
        uh = [pltpu.roll(v, 1, 0) for v in h]
        if halo is not None:
            sa, ha, sb, hb = halo(c)
        acc, back, down = [], [], []
        for r in range(S):
            sl = jnp.where(first, 0.0 if c == 0 else before[0][r], rs[r])
            if get_g is None:
                g = h[r] + jnp.where(first, 0.0 if c == 0 else before[1][r], rh[r])
                if put_g is not None:
                    put_g(r, c, g)
            else:
                g = get_g(r, c)
            face = g * (sl - s[r])
            back.append(pltpu.roll(face, LANES - 1, 1))
            if r == 0:
                if halo is None:
                    su, hu = us[0], uh[0]
                else:
                    su, hu = jnp.where(top, sa, us[0]), jnp.where(top, ha, uh[0])
            else:
                su, hu = jnp.where(top, us[r - 1], us[r]), jnp.where(top, uh[r - 1], uh[r])
            upper = (h[r] + hu) * (su - s[r])
            down.append(pltpu.roll(upper, ROWS - 1, 0))
            acc.append((s[r] + get_z(r, c, s[r], h[r])) + (face + upper))
        for r in range(S):
            if r + 1 < S:
                lower = jnp.where(bottom, down[r + 1], down[r])
            elif halo is None:
                lower = down[r]
            else:
                lower = jnp.where(bottom, (h[r] + hb) * (s[r] - sb), down[r])
            acc[r] = acc[r] - lower
        if before is not None:
            for r in range(S):
                put(r, c - 1, before[3][r] - jnp.where(last, back[r], before[2][r]))
        before = (rs, rh, back, acc, s, h)
    for r in range(S):
        out = before[5][r] * before[4][r]
        put(r, C - 1, before[3][r] - jnp.where(last, out, before[2][r]))


def vertical(s, h, s_up, h_up, s_down, h_down):
    return (h + h_up) * (s_up - s) + (h + h_down) * (s_down - s)


def collect(row, pieces):
    value = None
    for q, (source_tile, source) in enumerate(pieces):
        moved = source_tile if q == source else pltpu.roll(source_tile, (q - source) % ROWS, 0)
        value = moved if value is None else jnp.where(row == q, moved, value)
    return value


def begin_kernel(
    s_hbm, lab_hbm, patch_hbm, zone_hbm, kap_hbm, power_hbm,
    planes, heat, swap_a, swap_b, s_v, lab_v,
    patch, zone_v, kap, power, sem,
):
    L, R, W = s_hbm.shape
    C = W // LANES
    starts = (0, R - ROWS)
    small = [
        pltpu.make_async_copy(kap_hbm, kap, sem.at[0]),
        pltpu.make_async_copy(power_hbm, power, sem.at[1]),
        pltpu.make_async_copy(patch_hbm, patch, sem.at[2]),
    ]
    groups = [(0, 2), (L - 2, 2), (2, L - 4)]
    layers = [
        [
            pltpu.make_async_copy(s_hbm.at[pl.ds(l, n)], s_v.at[pl.ds(l, n)], sem.at[3 + 2 * k]),
            pltpu.make_async_copy(lab_hbm.at[pl.ds(l, n)], lab_v.at[pl.ds(l, n)], sem.at[4 + 2 * k]),
        ]
        for k, (l, n) in enumerate(groups)
    ]
    layers[2] += [
        pltpu.make_async_copy(zone_hbm.at[pl.ds(start, ROWS)], zone_v.at[k], sem.at[9 + k])
        for k, start in enumerate(starts)
    ]
    for copy in small + layers[0] + layers[1] + layers[2]:
        copy.start()
    for copy in small:
        copy.wait()
    values = splats(kap)
    heats = step_dt * jnp.broadcast_to(power[...], (ROWS, LANES))

    def warm(c, _):
        lanes = pl.ds(pl.multiple_of(c * LANES, LANES), LANES)
        for r in range(R // ROWS):
            at = (pl.ds(ROWS * r, ROWS), lanes)
            heat[at] = lookup(heats, patch[at])
        return 0

    lax.fori_loop(0, C, warm, 0)
    for copy in layers[0] + layers[1]:
        copy.wait()

    def plane(p, _):
        own, near = p * (L - 1), 1 + p * (L - 3)
        heated = jnp.where(p == 0, 1.0, 0.0)

        def get_s(r, c):
            return s_v[(own,) + tile(r, c)]

        def get_h(r, c):
            return choose(values, lab_v[(own,) + tile(r, c)])

        def get_z(r, c, s, h):
            h_near = choose(values, lab_v[(near,) + tile(r, c)])
            return (h + h_near) * (s_v[(near,) + tile(r, c)] - s) + heated * heat[tile(r, c)]

        def put(r, c, value):
            planes[(p,) + tile(r, c)] = value

        stencil(R, W, get_s, get_h, get_z, None, put)
        return 0

    lax.fori_loop(0, 2, plane, 0)
    row = row_ids()
    for copy in layers[2]:
        copy.wait()

    def pack(k, out):
        rows = ((0, 1), (ROWS - 2, ROWS - 1))[k]

        def body(c, _):
            lanes = pl.ds(pl.multiple_of(c * LANES, LANES), LANES)
            edge = pl.ds(starts[k], ROWS)
            for base in range(0, L, ROWS):
                for ref, at in ((s_v, 0), (lab_v, 2 * L)):
                    tiles = [ref[base + q, edge, lanes] for q in range(ROWS)]
                    for j, source in enumerate(rows):
                        packed = collect(row, [(x, source) for x in tiles])
                        if ref is lab_v:
                            packed = choose(values, packed)
                        out[pl.ds(at + j * L + base, ROWS), lanes] = packed
            zones = zone_v[k, :, lanes].astype(jnp.float32)
            out[pl.ds(4 * L, ROWS), lanes] = collect(row, [(heat[edge, lanes], rows[k]), (zones, rows[k])])
            return 0

        lax.fori_loop(0, W // LANES, body, 0)

    odd = lax.axis_index("tile") % 2 == 1

    @pl.when(odd)
    def _():
        pack(0, swap_a)
        pack(1, swap_b)

    @pl.when(jnp.logical_not(odd))
    def _():
        pack(1, swap_a)
        pack(0, swap_b)


def begin(s, lab, patch, zone, kap, power):
    L, R, W = s.shape
    f32, i32 = jnp.float32, jnp.int32
    packed = pltpu.VMEM((4 * L + ROWS, W), f32)
    args = [pltpu.with_memory_space_constraint(x, pltpu.HBM) for x in (s, lab, patch, zone, kap, power)]
    return pl.pallas_call(
        begin_kernel,
        out_shape=(
            pltpu.VMEM((2, R, W), f32), pltpu.VMEM((R, W), f32), packed, packed, pltpu.VMEM(s.shape, f32), pltpu.VMEM(lab.shape, i32)
        ),
        in_specs=[HBM] * 6,
        out_specs=[VMEM] * 6,
        scratch_shapes=[
            pltpu.VMEM((R, W), i32),
            pltpu.VMEM((2, ROWS, W), i32),
            pltpu.SMEM(kap.shape, f32),
            pltpu.VMEM(power.shape, f32),
            pltpu.SemaphoreType.DMA((11,)),
        ],
        compiler_params=pltpu.CompilerParams(vmem_limit_bytes=16 * MIB),
        name="begin",
    )(*args)


def above_exists():
    return lax.axis_index("tile") > 0


def below_exists():
    return lax.axis_index("tile") < lax.axis_size("tile") - 1


def near_edge_kernel(own_a, own_b, got_a, got_b, edges, aux):
    rows, W = own_a.shape
    L = (rows - ROWS) // 4
    col = lax.broadcasted_iota(jnp.int32, (ROWS, W), 1)
    row = lax.broadcasted_iota(jnp.int32, (ROWS, W), 0)
    odd = lax.axis_index("tile") % 2 == 1
    above, below = above_exists(), below_exists()

    def four_sides(at):
        at = pl.ds(at, ROWS)
        up = jnp.where(odd, own_a[at, :], own_b[at, :])
        down = jnp.where(odd, own_b[at, :], own_a[at, :])
        lo = jnp.where(above, jnp.where(odd, got_a[at, :], got_b[at, :]), 0.0)
        hi = jnp.where(below, jnp.where(odd, got_b[at, :], got_a[at, :]), 0.0)
        return lo, up, down, hi

    def part(k):
        first, second = 2 * k * L, 2 * k * L + L
        a0, a1, b0, b1 = (four_sides(at) for at in (first, first + L - ROWS, second, second + L - ROWS))
        end = ROWS - 1
        return [
            collect(
                row,
                [(a0[x], 0), (b0[x], 0), (a0[x], 1), (b0[x], 1)]
                + [(a1[x], end), (b1[x], end), (a1[x], end - 1), (b1[x], end - 1)],
            )
            for x in range(4)
        ]

    def four(*pieces):
        value = None
        for k, (x, source) in enumerate(pieces):
            moved = x if k == source else pltpu.roll(x, (k - source) % ROWS, 0)
            value = moved if value is None else jnp.where(row % 4 == k, moved, value)
        return value

    def arrange(lo, up, down, hi):
        centre = four((lo, 1), (up, 0), (down, 1), (hi, 0))
        upper = four((lo, 0), (lo, 1), (down, 0), (down, 1))
        lower = four((up, 0), (up, 1), (hi, 0), (hi, 1))
        inward = four((lo, 3), (up, 2), (down, 3), (hi, 2))
        return centre, upper, lower, inward

    s, s_up, s_down, s_in = arrange(*part(0))
    h, h_up, h_down, h_in = arrange(*part(1))

    def toward(s_n, h_n):
        return (h + h_n) * (s_n - s)

    def moved(shift, gone):
        return jnp.where(gone, 0.0, pltpu.roll(s, shift, 1)), jnp.where(gone, 0.0, pltpu.roll(h, shift, 1))

    total = s + toward(s_up, h_up) + toward(s_down, h_down) + toward(s_in, h_in)
    total = total + toward(*moved(1, col == 0)) + toward(*moved(W - 1, col == W - 1))
    extra = four_sides(4 * L)
    heat = four(*((x, 0) for x in extra))
    total = total + jnp.where(row < 4, heat, 0.0)
    gone = ((row % 4 == 0) & jnp.logical_not(above)) | ((row % 4 == 3) & jnp.logical_not(below))
    edges[...] = jnp.where(gone, 0.0, total)
    zones = four(*((x, 1) for x in extra))
    aux[pl.ds(0, ROWS), :] = h
    aux[pl.ds(ROWS, ROWS), :] = jnp.where(row < 4, zones, pltpu.roll(zones, 4, 0))
    aux[pl.ds(2 * ROWS, ROWS), :] = s_in
    aux[pl.ds(3 * ROWS, ROWS), :] = h_in


def near_edges(own_a, own_b, got_a, got_b):
    W = own_a.shape[1]
    return pl.pallas_call(
        near_edge_kernel,
        out_shape=(pltpu.VMEM((ROWS, W), jnp.float32), pltpu.VMEM((4 * ROWS, W), jnp.float32)),
        in_specs=[VMEM] * 4,
        out_specs=[VMEM] * 2,
        compiler_params=pltpu.CompilerParams(vmem_limit_bytes=16 * MIB),
        name="near_edges",
    )(own_a, own_b, got_a, got_b)


def edge_kernel(own_a, own_b, got_a, got_b, _, rims):
    rows, W = own_a.shape
    L = (rows - ROWS) // 4
    col = lax.broadcasted_iota(jnp.int32, (L, W), 1)
    layer = lax.broadcasted_iota(jnp.int32, (L, W), 0)
    odd = lax.axis_index("tile") % 2 == 1

    def step(s_a, h_a, s, h, s_b, h_b):
        def toward(s_n, h_n):
            return (h + h_n) * (s_n - s)

        def moved(shift, axis, gone):
            return jnp.where(gone, 0.0, pltpu.roll(s, shift, axis)), jnp.where(
                gone, 0.0, pltpu.roll(h, shift, axis)
            )

        total = s + toward(s_a, h_a) + toward(s_b, h_b)
        total = total + toward(*moved(1, 1, col == 0)) + toward(*moved(W - 1, 1, col == W - 1))
        under = jnp.where(layer == 0, 0.0, toward(pltpu.roll(s, 1, 0), pltpu.roll(h, 1, 0)))
        over = jnp.where(layer == L - 1, 0.0, toward(pltpu.roll(s, L - 1, 0), pltpu.roll(h, L - 1, 0)))
        return total + under + over

    for side, exists in enumerate((above_exists(), below_exists())):
        first_swap = odd if side == 0 else jnp.logical_not(odd)

        def other(at, n):
            at = pl.ds(at, n)
            return jnp.where(exists, jnp.where(first_swap, got_a[at, :], got_b[at, :]), 0.0)

        def own(at, n):
            at = pl.ds(at, n)
            return jnp.where(first_swap, own_a[at, :], own_b[at, :])

        far, near = (0, 1) if side == 0 else (1, 0)
        sf, sn, hf, hn = (other(k * L, L) for k in (far, near, 2 + far, 2 + near))
        s0, h0 = own((1 - near) * L, L), own((3 - near) * L, L)
        rims[2 * side] = sn
        rims[2 * side + 1] = hn
        rims[4 + side] = jnp.where(exists, step(sf, hf, sn, hn, s0, h0), 0.0)


def edge_rows(own_a, own_b, got_a, got_b, after):
    rows, W = own_a.shape
    return pl.pallas_call(
        edge_kernel,
        out_shape=pltpu.VMEM((6, (rows - ROWS) // 4, W), jnp.float32),
        in_specs=[VMEM] * 4 + [ANY],
        out_specs=VMEM,
        compiler_params=pltpu.CompilerParams(vmem_limit_bytes=16 * MIB),
        name="edge_rows",
    )(own_a, own_b, got_a, got_b, after)


def pick(ref, base, l, lanes, row):
    at = base + (l // ROWS) * ROWS
    if not isinstance(l, int):
        at = pl.multiple_of(at, ROWS)
    return pltpu.roll(ref[pl.ds(at, ROWS), lanes], (row - l) % ROWS, 0)


def halo_rows(rims, state, lanes, l):
    end = ROWS - 1
    where = ((state[0], 0), (1, 0), (state[1], end), (3, end))
    return tuple(pick(rims.at[k], 0, l, lanes, row) for k, row in where)


def fill_faces(first, end, lab, values, h_out, g_out):
    _, R, W = lab.shape
    edge = lane_ids() == 0

    def body(l, _):
        for r in range(R // ROWS):
            before = 0.0
            for c in range(W // LANES):
                at = (l,) + tile(r, c)
                h = choose(values, lab[at])
                moved = pltpu.roll(h, 1, 1)
                h_out[at] = h
                g_out[at] = h + jnp.where(edge, before, moved)
                before = moved
        return 0

    lax.fori_loop(first, end, body, 0)


def faces_kernel(lab, kap, h_out, g_out):
    L = lab.shape[0]
    values = splats(kap)
    fill_faces(0, 3, lab, values, h_out, g_out)
    fill_faces(L - 3, L, lab, values, h_out, g_out)


def faces(lab, kap):
    return pl.pallas_call(
        faces_kernel,
        out_shape=(jax.ShapeDtypeStruct(lab.shape, jnp.float32),) * 2,
        in_specs=[VMEM, SMEM],
        out_specs=[VMEM] * 2,
        compiler_params=pltpu.CompilerParams(vmem_limit_bytes=20 * MIB),
        name="faces",
    )(lab, kap)


def more_faces_kernel(lab, kap, h_in, g_in, _, h_out, g_out):
    fill_faces(3, lab.shape[0] - 3, lab, splats(kap), h_out, g_out)


def more_faces(lab, kap, h, g, after):
    return pl.pallas_call(
        more_faces_kernel,
        out_shape=(jax.ShapeDtypeStruct(lab.shape, jnp.float32),) * 2,
        in_specs=[VMEM, SMEM, VMEM, VMEM, ANY],
        out_specs=[VMEM] * 2,
        input_output_aliases={2: 0, 3: 1},
        compiler_params=pltpu.CompilerParams(vmem_limit_bytes=24 * MIB),
        name="more_faces",
    )(lab, kap, h, g, after)


def layer_step(l, s_ref, h_ref, g_ref, halo, put):
    _, R, W = s_ref.shape

    def get_s(r, c):
        return s_ref[(l,) + tile(r, c)]

    def get_h(r, c):
        return h_ref[(l,) + tile(r, c)]

    def get_g(r, c):
        return g_ref[(l,) + tile(r, c)]

    def get_z(r, c, s, h):
        a, b = (l - 1,) + tile(r, c), (l + 1,) + tile(r, c)
        return vertical(s, h, s_ref[a], h_ref[a], s_ref[b], h_ref[b])

    stencil(R, W, get_s, get_h, get_z, halo, put, get_g=get_g)


def first_step(l, s_ref, h_ref, g_ref, halo, t):
    def put(r, c, value):
        t[(l,) + tile(r, c)] = value

    layer_step(l, s_ref, h_ref, g_ref, halo, put)


def wall(aux, k, p, lanes):
    rows = aux[pl.ds(k * ROWS, ROWS), lanes]
    return pltpu.roll(rows, (2 - p) * 4 % ROWS, 0), pltpu.roll(rows, 4 - 4 * p, 0)


def outer_kernel(s_ref, h_ref, g_ref, aux, t):
    L = s_ref.shape[0]

    def body(p, _):
        def halo(c):
            lanes = pl.ds(LANES * c, LANES)
            (sa, sb), (ha, hb) = wall(aux, 2, p, lanes), wall(aux, 3, p, lanes)
            return sa, ha, sb, hb

        first_step(1 + p * (L - 3), s_ref, h_ref, g_ref, halo, t)
        return 0

    lax.fori_loop(0, 2, body, 0)


def outer(s, h, g, aux):
    return pl.pallas_call(
        outer_kernel,
        out_shape=pltpu.VMEM(s.shape, jnp.float32),
        in_specs=[VMEM] * 4,
        out_specs=VMEM,
        compiler_params=pltpu.CompilerParams(vmem_limit_bytes=20 * MIB),
        name="outer",
    )(s, h, g, aux)


def inside_kernel(s_ref, h_ref, g_ref, rims, t_in, _, t):
    L = s_ref.shape[0]

    def body(l, _):
        def halo(c):
            return halo_rows(rims, (0, 2), pl.ds(LANES * c, LANES), l)

        first_step(l, s_ref, h_ref, g_ref, halo, t)
        return 0

    lax.fori_loop(2, L - 2, body, 0)


def inside(s, h, g, rims, t, after):
    return pl.pallas_call(
        inside_kernel,
        out_shape=jax.ShapeDtypeStruct(s.shape, jnp.float32),
        in_specs=[VMEM] * 5 + [ANY],
        out_specs=VMEM,
        input_output_aliases={4: 0},
        compiler_params=pltpu.CompilerParams(vmem_limit_bytes=24 * MIB),
        name="inside",
    )(s, h, g, rims, t, after)


def last_kernel(t_ref, h_ref, g_ref, rims, out, buf, sem):
    L, R, W = t_ref.shape

    def send(l):
        return pltpu.make_async_copy(buf.at[l], out.at[l], sem.at[l])

    def body(l, _):
        def put(r, c, value):
            buf[(l,) + tile(r, c)] = value

        def halo(c):
            return halo_rows(rims, (4, 5), pl.ds(LANES * c, LANES), l)

        layer_step(l, t_ref, h_ref, g_ref, halo, put)
        send(l).start()
        return 0

    lax.fori_loop(1, L - 1, body, 0)

    def drain(l, _):
        send(l).wait()
        return 0

    lax.fori_loop(1, L - 1, drain, 0)


def last_layers(t, h, g, rims):
    L = t.shape[0]
    return pl.pallas_call(
        last_kernel,
        out_shape=jax.ShapeDtypeStruct(t.shape, jnp.float32),
        in_specs=[VMEM] * 4,
        out_specs=HBM,
        scratch_shapes=[pltpu.VMEM(t.shape, jnp.float32), pltpu.SemaphoreType.DMA((L,))],
        compiler_params=pltpu.CompilerParams(vmem_limit_bytes=24 * MIB),
        name="last_layers",
    )(t, h, g, rims)


def near_of(side):
    me = lax.axis_index("tier")
    return (me ^ 1, me ^ 2) if side == 0 else (me ^ 2, me ^ 1)


def routes(tier, tile):
    odd = tile % 2
    return tier ^ (1 + odd), tier ^ (2 - odd)


def entries(tiers):
    me = lax.axis_index("tier")
    if tiers != 4:
        return [(2 * me + i, j) for i in range(2) for j in range(2 * tiers)]
    listed = []
    for side in range(2):
        near, target = near_of(side)
        columns = [2 * me, 2 * me + 1, 2 * near, 2 * near + 1]
        for who in (target, me):
            listed += [(2 * who + i, j) for i in range(2) for j in columns]
    return listed


def rim_entries(tiers):
    me = lax.axis_index("tier")
    if tiers != 4:
        return [(me, q) for q in range(tiers)]
    near, target = routes(me, lax.axis_index("tile"))
    return [(who, source) for who in (target, me) for source in (me, near)]


def table_kernel(tiers, ops, table, rim_table):
    regions = ops.shape[0]
    for k, (i, j) in enumerate(entries(tiers)):
        for g in range(regions):
            table[k, g] = jnp.full((ROWS, LANES), ops[g, i, j], jnp.float32)
    lane, upper = lane_ids(), row_ids() < 4
    for q, (who, source) in enumerate(rim_entries(tiers)):
        for k in range(2):
            value = jnp.zeros((ROWS, LANES), jnp.float32)
            for g in range(regions):
                a, b = ops[g, 2 * who, 2 * source + k], ops[g, 2 * who + 1, 2 * source + 1 - k]
                value = jnp.where(lane == g, jnp.where(upper, a, b), value)
            rim_table[2 * q + k] = value


def make_tables(tiers, ops):
    regions = ops.shape[0]
    f32 = jnp.float32
    count, rims = (32, 8) if tiers == 4 else (4 * tiers, 2 * tiers)
    return pl.pallas_call(
        functools.partial(table_kernel, tiers),
        out_shape=(pltpu.VMEM((count, regions, ROWS, LANES), f32), pltpu.VMEM((rims, ROWS, LANES), f32)),
        in_specs=[SMEM],
        out_specs=[VMEM, VMEM],
        compiler_params=pltpu.CompilerParams(vmem_limit_bytes=16 * MIB),
        name="make_tables",
    )(ops)


def product(table, at, zone, refs, partial, base, put):
    regions = table.shape[1]
    R, W = refs[0][0].shape[1:]
    S = R // ROWS

    def body(c, _):
        lanes = pl.ds(pl.multiple_of(c * LANES, LANES), LANES)
        whole = pl.ds(pl.multiple_of(base + c * LANES, LANES), LANES)
        for r0 in range(0, S, 2):
            rows = [pl.ds(ROWS * r, ROWS) for r in range(r0, min(S, r0 + 2))]
            zones = [zone[x, whole] for x in rows]
            for i in range(2):
                totals = [None] * len(rows)
                for j, (ref, index) in enumerate(refs):
                    values = [table[at + i * len(refs) + j, g] for g in range(regions)]
                    for k, x in enumerate(rows):
                        term = choose(values, zones[k]) * ref[index, x, lanes]
                        totals[k] = term if totals[k] is None else totals[k] + term
                for k, x in enumerate(rows):
                    for ref in partial:
                        totals[k] = totals[k] + ref[i, x, lanes]
                    put(i, x, lanes, whole, totals[k])
        return 0

    lax.fori_loop(0, W // LANES, body, 0)


def both(own, near):
    return [(own, 0), (own, 1), (near, 0), (near, 1)]


def put_in(out):
    def put(i, rows, lanes, whole, value):
        out[i, rows, lanes] = value

    return put


def way_of_tile():
    return lax.axis_index("tile") % 2


def combine_kernel(table, zone, own, near, _, out):
    product(table, 16 * way_of_tile(), zone, both(own, near), [], 0, put_in(out))


def combine(table, zone, own, near, after):
    return pl.pallas_call(
        combine_kernel,
        out_shape=pltpu.VMEM(own.shape, jnp.float32),
        in_specs=[VMEM] * 4 + [ANY],
        out_specs=VMEM,
        compiler_params=pltpu.CompilerParams(vmem_limit_bytes=16 * MIB),
        name="combine",
    )(table, zone, own, near, after)


def combine_halves_kernel(table, zone, left, left_x, right, right_y, _, to_y, to_x):
    product(table, 0, zone, both(left, left_x), [], 0, put_in(to_y))
    product(table, 16, zone, both(right, right_y), [], left.shape[2], put_in(to_x))


def combine_halves(table, zone, left, left_x, right, right_y, after):
    return pl.pallas_call(
        combine_halves_kernel,
        out_shape=(pltpu.VMEM(left.shape, jnp.float32),) * 2,
        in_specs=[VMEM] * 6 + [ANY],
        out_specs=[VMEM, VMEM],
        compiler_params=pltpu.CompilerParams(vmem_limit_bytes=16 * MIB),
        name="combine_halves",
    )(table, zone, left, left_x, right, right_y, after)


def rim_product(rim_table, pairs, aux, lanes):
    zones = aux[pl.ds(ROWS, ROWS), lanes].astype(jnp.int32)
    value = None
    for at, planes in pairs:
        for k, x in enumerate((planes, pltpu.roll(planes, 4, 0))):
            term = lookup(rim_table[at + k], zones) * x
            value = term if value is None else value + term
    return value


def combine_rim_kernel(rim_table, aux, own, near, _, out):
    for c in range(own.shape[1] // LANES):
        lanes = pl.ds(c * LANES, LANES)
        out[:, lanes] = rim_product(rim_table, [(0, own[:, lanes]), (2, near[:, lanes])], aux, lanes)


def combine_rim(rim_table, aux, own, near, after):
    return pl.pallas_call(
        combine_rim_kernel,
        out_shape=pltpu.VMEM(own.shape, jnp.float32),
        in_specs=[VMEM] * 4 + [ANY],
        out_specs=VMEM,
        compiler_params=pltpu.CompilerParams(vmem_limit_bytes=16 * MIB),
        name="combine_rim",
    )(rim_table, aux, own, near, after)


def own_kernel(table, rim_table, aux, zone, own, near, edges, edges_near, _, base, rim_base):
    for c in range(edges.shape[1] // LANES):
        lanes = pl.ds(c * LANES, LANES)
        rim_base[:, lanes] = rim_product(rim_table, [(4, edges[:, lanes]), (6, edges_near[:, lanes])], aux, lanes)
    product(table, 16 * way_of_tile() + 8, zone, both(own, near), [], 0, put_in(base))


def own_part(tables, aux, zone, own, near, edges, edges_near, after):
    return pl.pallas_call(
        own_kernel,
        out_shape=(pltpu.VMEM(own.shape, jnp.float32), pltpu.VMEM(edges.shape, jnp.float32)),
        in_specs=[VMEM] * 8 + [ANY],
        out_specs=[VMEM] * 2,
        compiler_params=pltpu.CompilerParams(vmem_limit_bytes=16 * MIB),
        name="own_part",
    )(*tables, aux, zone, own, near, edges, edges_near, after)


def own_halves_kernel(table, zone, left, left_x, right, right_y, _, base):
    half = left.shape[2]

    def put(i, rows, lanes, whole, value):
        base[i, rows, whole] = value

    product(table, 8, zone, both(left, left_x), [], 0, put)
    product(table, 24, zone, both(right, right_y), [], half, put)


def own_halves(table, zone, left, left_x, right, right_y, after):
    return pl.pallas_call(
        own_halves_kernel,
        out_shape=pltpu.VMEM((2,) + zone.shape, jnp.float32),
        in_specs=[VMEM] * 6 + [ANY],
        out_specs=VMEM,
        compiler_params=pltpu.CompilerParams(vmem_limit_bytes=16 * MIB),
        name="own_halves",
    )(table, zone, left, left_x, right, right_y, after)


def bond_kernel(tiers, zone, table, rim_table, aux, heat, h_ref, g_ref, t_in, *refs):
    pairs = tiers == 4
    arrays, (t, left, right, rim) = refs[:-4], refs[-4:]
    L, R, W = t.shape
    C = W // LANES
    row = row_ids()
    if pairs:
        base, part, rim_base, rim_part = arrays

        def add(c, _):
            lanes = pl.ds(pl.multiple_of(c * LANES, LANES), LANES)
            for r in range(R // ROWS):
                rows = pl.ds(ROWS * r, ROWS)
                for i in range(2):
                    t[i * (L - 1), rows, lanes] = base[i, rows, lanes] + part[i, rows, lanes]
            return 0

        lax.fori_loop(0, C, add, 0)
    else:
        planes, edges = arrays

        def put(i, rows, lanes, whole, value):
            t[i * (L - 1), rows, lanes] = value

        product(table, 0, zone, [(planes, k) for k in range(2 * tiers)], [], 0, put)
    gone = ((row % 4 == 0) & jnp.logical_not(above_exists())) | ((row % 4 == 3) & jnp.logical_not(below_exists()))

    for c in range(C):
        lanes = pl.ds(c * LANES, LANES)
        if pairs:
            value = rim_base[:, lanes] + rim_part[:, lanes]
        else:
            value = rim_product(rim_table, [(2 * q, edges[q, :, lanes]) for q in range(tiers)], aux, lanes)
        value = jnp.where(gone, 0.0, value)
        rim[:, lanes] = value
        for i in range(2):
            t[i * (L - 1), pl.ds(0, 1), lanes] = value[4 * i + 1 : 4 * i + 2]
            t[i * (L - 1), pl.ds(R - 1, 1), lanes] = value[4 * i + 2 : 4 * i + 3]

    def plane(p, _):
        own, near = p * (L - 1), 1 + p * (L - 3)
        heated = jnp.where(p == 0, 1.0, 0.0)

        def get_s(r, c):
            return t[(own,) + tile(r, c)]

        def get_h(r, c):
            return h_ref[(own,) + tile(r, c)]

        def get_g(r, c):
            return g_ref[(own,) + tile(r, c)]

        def get_z(r, c, s, h):
            at = (near,) + tile(r, c)
            return (h + h_ref[at]) * (t[at] - s) + heated * heat[tile(r, c)]

        def halo(c):
            lanes = pl.ds(LANES * c, LANES)
            (sa, sb), (ha, hb) = wall(rim, 0, p, lanes), wall(aux, 0, p, lanes)
            return sa, ha, sb, hb

        def put_out(r, c, value):
            out, c = (left, c) if c < C // 2 else (right, c - C // 2)
            out[(p,) + tile(r, c)] = value

        stencil(R, W, get_s, get_h, get_z, halo, put_out, get_g=get_g)
        return 0

    lax.fori_loop(0, 2, plane, 0)


def bond(tiers, zone, tables, aux, heat, h, g, t, arrays):
    _, R, W = t.shape
    args = (zone, *tables, aux, heat, h, g, t, *arrays)
    f32 = jnp.float32
    return pl.pallas_call(
        functools.partial(bond_kernel, tiers),
        out_shape=(
            jax.ShapeDtypeStruct(t.shape, f32),
            jax.ShapeDtypeStruct((2, R, W // 2), f32),
            jax.ShapeDtypeStruct((2, R, W // 2), f32),
        ),
        in_specs=[VMEM] * len(args),
        out_specs=[VMEM] * 3,
        scratch_shapes=[pltpu.VMEM((ROWS, W), f32)],
        input_output_aliases={7: 0},
        compiler_params=pltpu.CompilerParams(vmem_limit_bytes=24 * MIB),
        name="bond",
    )(*args)


def final_kernel(tiers, zone, table, *refs):
    arrays, (_, out, buf, sem) = refs[:-4], refs[-4:]
    L, R, W = out.shape
    half = W // 2
    copies = []
    for side in range(2):
        first = side * half

        def put(i, rows, lanes, whole, value):
            buf[i, rows, whole] = value

        if tiers == 4:
            base, part = arrays[0], arrays[1 + side]

            def add(c, _):
                lanes = pl.ds(pl.multiple_of(c * LANES, LANES), LANES)
                whole = pl.ds(pl.multiple_of(first + c * LANES, LANES), LANES)
                for r in range(R // ROWS):
                    rows = pl.ds(ROWS * r, ROWS)
                    for i in range(2):
                        buf[i, rows, whole] = base[i, rows, whole] + part[i, rows, lanes]
                return 0

            lax.fori_loop(0, half // LANES, add, 0)
        else:
            product(table, 0, zone, [(arrays[side], k) for k in range(2 * tiers)], [], first, put)
        lanes = pl.ds(first, half)
        for i in range(2):
            copy = pltpu.make_async_copy(
                buf.at[i, :, lanes], out.at[i * (L - 1), :, lanes], sem.at[2 * side + i]
            )
            copy.start()
            copies.append(copy)
    for copy in copies:
        copy.wait()


def final_planes(tiers, zone, table, arrays, out):
    args = (zone, table, *arrays, out)
    _, R, W = out.shape
    return pl.pallas_call(
        functools.partial(final_kernel, tiers),
        out_shape=jax.ShapeDtypeStruct(out.shape, jnp.float32),
        in_specs=[VMEM] * (len(args) - 1) + [HBM],
        out_specs=HBM,
        scratch_shapes=[pltpu.VMEM((2, R, W), jnp.float32), pltpu.SemaphoreType.DMA((4,))],
        input_output_aliases={len(args) - 1: 0},
        compiler_params=pltpu.CompilerParams(vmem_limit_bytes=16 * MIB),
        name="final_planes",
    )(*args)


def across(value, bits, tiers):
    return lax.ppermute(value, "tier", [(i, i ^ bits) for i in range(tiers)])


def every(value, tiers):
    gathered = lax.all_gather(value, "tier", axis=0, tiled=False)
    return gathered.reshape((tiers * value.shape[0],) + value.shape[1:]) if value.ndim == 3 else gathered


def along(value, way, tiers, tiles):
    places = [(tier, tile) for tier in range(tiers) for tile in range(tiles)]
    pairs = [(tier * tiles + tile, routes(tier, tile)[way] * tiles + tile) for tier, tile in places]
    return lax.ppermute(value, ("tier", "tile"), pairs)


def exchange(tiers, tiles, tables, zone, planes, after):
    near = along(planes, 0, tiers, tiles)
    total = combine(tables[0], zone, planes, near, after)
    return near, along(total, 1, tiers, tiles)


def exchange_rim(tiers, tiles, tables, aux, edges, after):
    near = along(edges, 0, tiers, tiles)
    total = combine_rim(tables[1], aux, edges, near, after)
    return near, total, along(total, 1, tiers, tiles)


def exchange_halves(tiers, table, zone, left, right, after):
    if tiers != 4:
        return every(left, tiers), every(right, tiers)
    left_x, right_y = across(left, 1, tiers), across(right, 2, tiers)
    to_y, to_x = combine_halves(table, zone, left, left_x, right, right_y, after)
    parts = across(to_y, 2, tiers), across(to_x, 1, tiers)
    return own_halves(table, zone, left, left_x, right, right_y, to_y), *parts


def local(warming, substance, zone, patch, kap, power, ops):
    tiers, tiles = lax.axis_size("tier"), lax.axis_size("tile")
    s, lab, patch = warming[0], substance[0], patch[0]

    planes, heat, swap_a, swap_b, s, lab = begin(s, lab, patch, zone, kap, power)
    pairs = [(i, i ^ 1) for i in range(tiles) if i ^ 1 < tiles]
    got_a = lax.ppermute(swap_a, "tile", pairs)
    pairs = [(i, ((i - 1) ^ 1) + 1) for i in range(1, tiles - 1 + tiles % 2)]
    got_b = lax.ppermute(swap_b, "tile", pairs)
    tables = make_tables(tiers, ops)
    h, g = faces(lab, kap)
    if tiers == 4:
        near, part = exchange(tiers, tiles, tables, zone, planes, h)
    edges, aux = near_edges(swap_a, swap_b, got_a, got_b)
    h, g = more_faces(lab, kap, h, g, aux)
    if tiers == 4:
        edges_near, sent, rim_part = exchange_rim(tiers, tiles, tables, aux, edges, h)
        base, rim_base = own_part(tables, aux, zone, planes, near, edges, edges_near, sent)
        arrays = base, part, rim_base, rim_part
    else:
        arrays = every(planes, tiers), every(edges, tiers)
    t = outer(s, h, g, aux)
    t, left, right = bond(tiers, zone, tables, aux, heat, h, g, t, arrays)
    rims = edge_rows(swap_a, swap_b, got_a, got_b, left)
    t = inside(s, h, g, rims, t, left)
    arrays = exchange_halves(tiers, tables[0], zone, left, right, t)
    out = last_layers(t, h, g, rims)
    out = final_planes(tiers, zone, tables[0], arrays, out)
    return out[None]


def solution(mesh):
    in_specs = (
        P("tier", None, "tile", None),
        P("tier", None, "tile", None),
        P("tile", None),
        P("tier", "tile", None),
        P(),
        P("tier", None),
        P(),
    )
    out_specs = P("tier", None, "tile", None)
    return jax.shard_map(local, mesh=mesh, in_specs=in_specs, out_specs=out_specs, check_vma=False)
```

```python
import functools
import math

import jax
import jax.numpy as jnp
from jax import lax
from jax.experimental import pallas as pl
from jax.experimental.pallas import tpu as pltpu
from jax.sharding import PartitionSpec as P

STEPS = 2
step_dt = 0.04
half_dt = 0.5 * step_dt
LANES = 128
ROWS = 8
MIB = 1 << 20

VMEM = pl.BlockSpec(memory_space=pltpu.VMEM)
SMEM = pl.BlockSpec(memory_space=pltpu.SMEM)
ANY = pl.BlockSpec(memory_space=pl.ANY)
HBM = pl.BlockSpec(memory_space=pltpu.HBM)


def tile(r, c):
    return pl.ds(ROWS * r, ROWS), pl.ds(LANES * c, LANES)


def lane_ids():
    return lax.broadcasted_iota(jnp.int32, (ROWS, LANES), 1)


def row_ids():
    return lax.broadcasted_iota(jnp.int32, (ROWS, LANES), 0)


def choose(values, labels):
    values, bit = list(values), 1
    while len(values) > 1:
        odd = (labels & bit) != 0
        paired = [
            jnp.where(odd, values[i + 1], values[i]) if i + 1 < len(values) else values[i]
            for i in range(0, len(values), 2)
        ]
        values, bit = paired, 2 * bit
    return values[0]


def lookup(row, labels):
    return jnp.take_along_axis(row, labels, axis=1, mode="promise_in_bounds")


def splats(kap):
    return [jnp.full((ROWS, LANES), half_dt * kap[i], jnp.float32) for i in range(kap.shape[0])]


def stencil(R, W, get_s, get_h, get_z, halo, put, get_g=None, put_g=None):
    C, S = W // LANES, R // ROWS
    lane, row = lane_ids(), row_ids()
    first, last = lane == 0, lane == LANES - 1
    top, bottom = row == 0, row == ROWS - 1
    before = None
    for c in range(C):
        s = [get_s(r, c) for r in range(S)]
        h = [get_h(r, c) for r in range(S)]
        rs = [pltpu.roll(v, 1, 1) for v in s]
        rh = [pltpu.roll(v, 1, 1) for v in h] if get_g is None else None
        us = [pltpu.roll(v, 1, 0) for v in s]
        uh = [pltpu.roll(v, 1, 0) for v in h]
        if halo is not None:
            sa, ha, sb, hb = halo(c)
        acc, back, down = [], [], []
        for r in range(S):
            sl = jnp.where(first, 0.0 if c == 0 else before[0][r], rs[r])
            if get_g is None:
                g = h[r] + jnp.where(first, 0.0 if c == 0 else before[1][r], rh[r])
                if put_g is not None:
                    put_g(r, c, g)
            else:
                g = get_g(r, c)
            face = g * (sl - s[r])
            back.append(pltpu.roll(face, LANES - 1, 1))
            if r == 0:
                if halo is None:
                    su, hu = us[0], uh[0]
                else:
                    su, hu = jnp.where(top, sa, us[0]), jnp.where(top, ha, uh[0])
            else:
                su, hu = jnp.where(top, us[r - 1], us[r]), jnp.where(top, uh[r - 1], uh[r])
            upper = (h[r] + hu) * (su - s[r])
            down.append(pltpu.roll(upper, ROWS - 1, 0))
            acc.append((s[r] + get_z(r, c, s[r], h[r])) + (face + upper))
        for r in range(S):
            if r + 1 < S:
                lower = jnp.where(bottom, down[r + 1], down[r])
            elif halo is None:
                lower = down[r]
            else:
                lower = jnp.where(bottom, (h[r] + hb) * (s[r] - sb), down[r])
            acc[r] = acc[r] - lower
        if before is not None:
            for r in range(S):
                put(r, c - 1, before[3][r] - jnp.where(last, back[r], before[2][r]))
        before = (rs, rh, back, acc, s, h)
    for r in range(S):
        out = before[5][r] * before[4][r]
        put(r, C - 1, before[3][r] - jnp.where(last, out, before[2][r]))


def vertical(s, h, s_up, h_up, s_down, h_down):
    return (h + h_up) * (s_up - s) + (h + h_down) * (s_down - s)


def collect(row, pieces):
    value = None
    for q, (source_tile, source) in enumerate(pieces):
        moved = source_tile if q == source else pltpu.roll(source_tile, (q - source) % ROWS, 0)
        value = moved if value is None else jnp.where(row == q, moved, value)
    return value


def begin_kernel(
    s_hbm, lab_hbm, patch_hbm, kap_hbm, power_hbm,
    planes, heat, s_v, lab_v, h_out,
    patch, kap, power, sem,
):
    L, R, W = s_hbm.shape
    C = W // LANES
    small = [
        pltpu.make_async_copy(kap_hbm, kap, sem.at[0]),
        pltpu.make_async_copy(power_hbm, power, sem.at[1]),
        pltpu.make_async_copy(patch_hbm, patch, sem.at[2]),
    ]
    groups = [(0, 2), (L - 2, 2), (2, L - 4)]
    layers = [
        [
            pltpu.make_async_copy(s_hbm.at[pl.ds(l, n)], s_v.at[pl.ds(l, n)], sem.at[3 + 2 * k]),
            pltpu.make_async_copy(lab_hbm.at[pl.ds(l, n)], lab_v.at[pl.ds(l, n)], sem.at[4 + 2 * k]),
        ]
        for k, (l, n) in enumerate(groups)
    ]
    for copy in small + layers[0] + layers[1] + layers[2]:
        copy.start()
    for copy in small:
        copy.wait()
    values = splats(kap)
    heats = step_dt * jnp.broadcast_to(power[...], (ROWS, LANES))

    for c in range(C):
        for r in range(R // ROWS):
            heat[tile(r, c)] = lookup(heats, patch[tile(r, c)])
    for copy in layers[0] + layers[1]:
        copy.wait()

    def plane(p, _):
        own, near = p * (L - 1), 1 + p * (L - 3)
        heated = jnp.where(p == 0, 1.0, 0.0)

        def get_s(r, c):
            return s_v[(own,) + tile(r, c)]

        def get_h(r, c):
            value = choose(values, lab_v[(own,) + tile(r, c)])
            h_out[(own,) + tile(r, c)] = value
            return value

        def get_z(r, c, s, h):
            h_near = choose(values, lab_v[(near,) + tile(r, c)])
            h_out[(near,) + tile(r, c)] = h_near
            return (h + h_near) * (s_v[(near,) + tile(r, c)] - s) + heated * heat[tile(r, c)]

        def put(r, c, value):
            planes[(p,) + tile(r, c)] = value

        stencil(R, W, get_s, get_h, get_z, None, put)
        return 0

    lax.fori_loop(0, 2, plane, 0)
    for copy in layers[2]:
        copy.wait()


def begin(s, lab, patch, kap, power):
    _, R, W = s.shape
    f32, i32 = jnp.float32, jnp.int32
    args = [pltpu.with_memory_space_constraint(x, pltpu.HBM) for x in (s, lab, patch, kap, power)]
    return pl.pallas_call(
        begin_kernel,
        out_shape=(
            pltpu.VMEM((2, R, W), f32), pltpu.VMEM((R, W), f32), pltpu.VMEM(s.shape, f32), pltpu.VMEM(lab.shape, i32),
            pltpu.VMEM(s.shape, f32),
        ),
        in_specs=[HBM] * 5,
        out_specs=[VMEM] * 5,
        scratch_shapes=[
            pltpu.VMEM((R, W), i32),
            pltpu.SMEM(kap.shape, f32),
            pltpu.VMEM(power.shape, f32),
            pltpu.SemaphoreType.DMA((9,)),
        ],
        compiler_params=pltpu.CompilerParams(vmem_limit_bytes=16 * MIB),
        name="begin",
    )(*args)


def above_exists():
    return lax.axis_index("tile") > 0


def below_exists():
    return lax.axis_index("tile") < lax.axis_size("tile") - 1


def pack_kernel(s, lab, heat, zone, kap, swap_a, swap_b, rows_v, next_v):
    L, R, W = s.shape
    C = W // LANES
    row = row_ids()
    values = splats(kap)
    group = math.gcd(C, 4)

    def body(first, _):
        for c in (group * first + n for n in range(group)):
            lanes = pl.ds(pl.multiple_of(c * LANES, LANES), LANES)
            for k, (start, at_edge, inwards) in enumerate(((0, 0, 1), (R - ROWS, ROWS - 1, ROWS - 2))):
                edge = pl.ds(start, ROWS)
                for base in range(0, L, ROWS):
                    for ref, at in ((s, 0), (lab, L)):
                        tiles = [ref[base + q, edge, lanes] for q in range(ROWS)]
                        for out, source in ((rows_v, at_edge), (next_v, inwards)):
                            packed = collect(row, [(x, source) for x in tiles])
                            if ref is lab:
                                packed = choose(values, packed)
                            out[k, pl.ds(at + base, ROWS), lanes] = packed
                zones = zone[edge, lanes].astype(jnp.float32)
                rows_v[k, pl.ds(3 * L, ROWS), lanes] = collect(row, [(zones, at_edge), (heat[edge, lanes], at_edge)])
        return 0

    lax.fori_loop(0, C // group, body, 0)

    def side(k, _):
        def at(base, r, c):
            return k, pl.ds(base + ROWS * r, ROWS), pl.ds(LANES * c, LANES)

        def get_s(r, c):
            return rows_v[at(0, r, c)]

        def get_h(r, c):
            return rows_v[at(L, r, c)]

        def get_z(r, c, s, h):
            flow = (h + next_v[at(L, r, c)]) * (next_v[at(0, r, c)] - s)
            if r == 0:
                flow = flow + jnp.where(row == 0, pltpu.roll(rows_v[at(3 * L, 0, c)], ROWS - 1, 0), 0.0)
            return flow

        def ends(c):
            last = L // ROWS - 1
            return get_s(0, c), get_h(0, c), get_s(last, c), get_h(last, c)

        def put(r, c, value):
            rows_v[at(2 * L, r, c)] = value

        stencil(L, W, get_s, get_h, get_z, ends, put)
        return 0

    lax.fori_loop(0, 2, side, 0)
    odd = lax.axis_index("tile") % 2

    for r in range(swap_a.shape[0] // ROWS):
        for c in range(C):
            swap_a[tile(r, c)] = rows_v[(1 - odd,) + tile(r, c)]
            swap_b[tile(r, c)] = rows_v[(odd,) + tile(r, c)]


def pack_rows(s, lab, heat, zone, kap):
    L, _, W = s.shape
    f32 = jnp.float32
    rows = 3 * L + ROWS
    return pl.pallas_call(
        pack_kernel,
        out_shape=(pltpu.VMEM((rows, W), f32),) * 2,
        in_specs=[VMEM] * 4 + [SMEM],
        out_specs=[VMEM] * 2,
        scratch_shapes=[pltpu.VMEM((2, rows, W), f32), pltpu.VMEM((2, 2 * L, W), f32)],
        compiler_params=pltpu.CompilerParams(vmem_limit_bytes=20 * MIB),
        name="pack_rows",
    )(s, lab, heat, zone, kap)


def edge_kernel(own_a, own_b, got_a, got_b, edges, zones, rims):
    rows, W = own_a.shape
    L = (rows - ROWS) // 3
    odd = lax.axis_index("tile") % 2 == 1
    for side, exists in enumerate((above_exists(), below_exists())):
        first_swap = odd if side == 0 else jnp.logical_not(odd)
        k_out, k_in = (0, 1) if side == 0 else (3, 2)

        def both_sides(at, n):
            at = pl.ds(at, n)
            other = jnp.where(exists, jnp.where(first_swap, got_a[at, :], got_b[at, :]), 0.0)
            return other, jnp.where(first_swap, own_a[at, :], own_b[at, :])

        for base in range(0, L, ROWS):
            part = pl.ds(base, ROWS)
            s_out, s_in = both_sides(base, ROWS)
            h_out, h_in = both_sides(L + base, ROWS)
            u_out, u_in = both_sides(2 * L + base, ROWS)
            face = (h_in + h_out) * (s_out - s_in)
            t_out, t_in = jnp.where(exists, u_out - face, 0.0), u_in + face
            rims[2 * side, part, :] = s_out
            rims[2 * side + 1, part, :] = h_out
            rims[4 + side, part, :] = t_out
            for i, l in ((0, 0), (1, L - 1)):
                if base <= l < base + ROWS:
                    edges[pl.ds(4 * i + k_out, 1), :] = t_out[l - base : l - base + 1]
                    edges[pl.ds(4 * i + k_in, 1), :] = t_in[l - base : l - base + 1]
        z_out, z_in = both_sides(3 * L, 1)
        for i in range(2):
            zones[pl.ds(4 * i + k_out, 1), :] = z_out
            zones[pl.ds(4 * i + k_in, 1), :] = z_in


def edge_rows(own_a, own_b, got_a, got_b):
    rows, W = own_a.shape
    f32 = jnp.float32
    return pl.pallas_call(
        edge_kernel,
        out_shape=(pltpu.VMEM((ROWS, W), f32), pltpu.VMEM((ROWS, W), f32), pltpu.VMEM((6, (rows - ROWS) // 3, W), f32)),
        in_specs=[VMEM] * 4,
        out_specs=[VMEM] * 3,
        compiler_params=pltpu.CompilerParams(vmem_limit_bytes=16 * MIB),
        name="edge_rows",
    )(own_a, own_b, got_a, got_b)


def pick(ref, base, l, lanes, row):
    at = base + (l // ROWS) * ROWS
    if not isinstance(l, int):
        at = pl.multiple_of(at, ROWS)
    return pltpu.roll(ref[pl.ds(at, ROWS), lanes], (row - l) % ROWS, 0)


def halo_rows(rims, state, lanes, l):
    end = ROWS - 1
    where = ((state[0], 0), (1, 0), (state[1], end), (3, end))
    return tuple(pick(rims.at[k], 0, l, lanes, row) for k, row in where)


def fill_faces(first, end, h_at, h_out, g_out):
    _, R, W = h_out.shape
    edge = lane_ids() == 0

    def body(l, _):
        before = [0.0] * (R // ROWS)
        for c in range(W // LANES):
            for r in range(R // ROWS):
                at = (l,) + tile(r, c)
                h = h_at(at, c)
                moved = pltpu.roll(h, 1, 1)
                h_out[at] = h
                g_out[at] = h + jnp.where(edge, before[r], moved)
                before[r] = moved
        return 0

    lax.fori_loop(first, end, body, 0)


def from_labels(lab, kap):
    values = splats(kap)
    table, lane = jnp.zeros((ROWS, LANES), jnp.float32), lane_ids()
    for k, value in enumerate(values):
        table = jnp.where(lane == k, value, table)
    return lambda at, c: lookup(table, lab[at]) if c % 4 == 0 else choose(values, lab[at])


def faces_kernel(lab, kap, h_in, h_out, g_out):
    L = lab.shape[0]

    def held(at, c):
        return h_out[at]

    getter = from_labels(lab, kap)
    for first, end in ((0, 2), (L - 2, L)):
        fill_faces(first, end, held, h_out, g_out)
    for l in (2, L - 3):
        fill_faces(l, l + 1, getter, h_out, g_out)


def faces(lab, kap, h):
    return pl.pallas_call(
        faces_kernel,
        out_shape=(jax.ShapeDtypeStruct(lab.shape, jnp.float32),) * 2,
        in_specs=[VMEM, SMEM, VMEM],
        out_specs=[VMEM] * 2,
        input_output_aliases={2: 0},
        compiler_params=pltpu.CompilerParams(vmem_limit_bytes=20 * MIB),
        name="faces",
    )(lab, kap, h)


def more_faces_kernel(lab, kap, h_in, g_in, _, h_out, g_out):
    fill_faces(3, lab.shape[0] - 3, from_labels(lab, kap), h_out, g_out)


def more_faces(lab, kap, h, g, after):
    return pl.pallas_call(
        more_faces_kernel,
        out_shape=(jax.ShapeDtypeStruct(lab.shape, jnp.float32),) * 2,
        in_specs=[VMEM, SMEM, VMEM, VMEM, ANY],
        out_specs=[VMEM] * 2,
        input_output_aliases={2: 0, 3: 1},
        compiler_params=pltpu.CompilerParams(vmem_limit_bytes=24 * MIB),
        name="more_faces",
    )(lab, kap, h, g, after)


def layer_step(l, s_ref, h_ref, g_ref, halo, put):
    _, R, W = s_ref.shape

    def get_s(r, c):
        return s_ref[(l,) + tile(r, c)]

    def get_h(r, c):
        return h_ref[(l,) + tile(r, c)]

    def get_g(r, c):
        return g_ref[(l,) + tile(r, c)]

    def get_z(r, c, s, h):
        a, b = (l - 1,) + tile(r, c), (l + 1,) + tile(r, c)
        return vertical(s, h, s_ref[a], h_ref[a], s_ref[b], h_ref[b])

    stencil(R, W, get_s, get_h, get_z, halo, put, get_g=get_g)


def first_step(l, s_ref, h_ref, g_ref, halo, t):
    def put(r, c, value):
        t[(l,) + tile(r, c)] = value

    layer_step(l, s_ref, h_ref, g_ref, halo, put)


def outer_kernel(s_ref, h_ref, g_ref, rims, t):
    L = s_ref.shape[0]

    def body(p, _):
        l = 1 + p * (L - 3)

        def halo(c):
            return halo_rows(rims, (0, 2), pl.ds(LANES * c, LANES), l)

        first_step(l, s_ref, h_ref, g_ref, halo, t)
        return 0

    lax.fori_loop(0, 2, body, 0)


def outer(s, h, g, rims):
    return pl.pallas_call(
        outer_kernel,
        out_shape=pltpu.VMEM(s.shape, jnp.float32),
        in_specs=[VMEM] * 4,
        out_specs=VMEM,
        compiler_params=pltpu.CompilerParams(vmem_limit_bytes=20 * MIB),
        name="outer",
    )(s, h, g, rims)


def inside_kernel(s_ref, h_ref, g_ref, rims, t_in, _, t):
    L = s_ref.shape[0]

    def body(l, _):
        def halo(c):
            return halo_rows(rims, (0, 2), pl.ds(LANES * c, LANES), l)

        first_step(l, s_ref, h_ref, g_ref, halo, t)
        return 0

    lax.fori_loop(2, L - 2, body, 0)


def inside(s, h, g, rims, t, after):
    return pl.pallas_call(
        inside_kernel,
        out_shape=jax.ShapeDtypeStruct(s.shape, jnp.float32),
        in_specs=[VMEM] * 5 + [ANY],
        out_specs=VMEM,
        input_output_aliases={4: 0},
        compiler_params=pltpu.CompilerParams(vmem_limit_bytes=24 * MIB),
        name="inside",
    )(s, h, g, rims, t, after)


def last_kernel(t_ref, h_ref, g_ref, rims, out, buf, sem):
    L, R, W = t_ref.shape

    def send(l):
        return pltpu.make_async_copy(buf.at[l], out.at[l], sem.at[l])

    def body(l, _):
        def put(r, c, value):
            buf[(l,) + tile(r, c)] = value

        def halo(c):
            return halo_rows(rims, (4, 5), pl.ds(LANES * c, LANES), l)

        layer_step(l, t_ref, h_ref, g_ref, halo, put)
        send(l).start()
        return 0

    lax.fori_loop(1, L - 1, body, 0)

    def drain(l, _):
        send(l).wait()
        return 0

    lax.fori_loop(1, L - 1, drain, 0)


def last_layers(t, h, g, rims):
    L = t.shape[0]
    return pl.pallas_call(
        last_kernel,
        out_shape=jax.ShapeDtypeStruct(t.shape, jnp.float32),
        in_specs=[VMEM] * 4,
        out_specs=HBM,
        scratch_shapes=[pltpu.VMEM(t.shape, jnp.float32), pltpu.SemaphoreType.DMA((L,))],
        compiler_params=pltpu.CompilerParams(vmem_limit_bytes=24 * MIB),
        name="last_layers",
    )(t, h, g, rims)


def near_of(side):
    me = lax.axis_index("tier")
    return (me ^ 1, me ^ 2) if side == 0 else (me ^ 2, me ^ 1)


def routes(tier, tile):
    odd = tile % 2
    return tier ^ (1 + odd), tier ^ (2 - odd)


def entries(tiers):
    me = lax.axis_index("tier")
    if tiers != 4:
        return [(2 * me + i, j) for i in range(2) for j in range(2 * tiers)]
    listed = []
    for side in range(2):
        near, target = near_of(side)
        columns = [2 * me, 2 * me + 1, 2 * near, 2 * near + 1]
        for who in (target, me):
            listed += [(2 * who + i, j) for i in range(2) for j in columns]
    return listed


def rim_entries(tiers):
    me = lax.axis_index("tier")
    return [me ^ q if tiers == 4 else q for q in range(tiers)]


def table_kernel(tiers, ops, table, rim_table):
    regions = ops.shape[0]
    for k, (i, j) in enumerate(entries(tiers)):
        for g in range(regions):
            table[k, g] = jnp.full((ROWS, LANES), ops[g, i, j], jnp.float32)
    lane, upper = lane_ids(), row_ids() < 4
    me = lax.axis_index("tier")
    for q, source in enumerate(rim_entries(tiers)):
        for k in range(2):
            value = jnp.zeros((ROWS, LANES), jnp.float32)
            for g in range(regions):
                a, b = ops[g, 2 * me, 2 * source + k], ops[g, 2 * me + 1, 2 * source + 1 - k]
                value = jnp.where(lane == g, jnp.where(upper, a, b), value)
            rim_table[2 * q + k] = value


def make_tables(tiers, ops):
    regions = ops.shape[0]
    f32 = jnp.float32
    count, rims = 32 if tiers == 4 else 4 * tiers, 2 * tiers
    return pl.pallas_call(
        functools.partial(table_kernel, tiers),
        out_shape=(pltpu.VMEM((count, regions, ROWS, LANES), f32), pltpu.VMEM((rims, ROWS, LANES), f32)),
        in_specs=[SMEM],
        out_specs=[VMEM, VMEM],
        compiler_params=pltpu.CompilerParams(vmem_limit_bytes=16 * MIB),
        name="make_tables",
    )(ops)


def product(table, at, zone, refs, partial, base, put):
    regions = table.shape[1]
    R, W = refs[0][0].shape[1:]
    S = R // ROWS

    def body(c, _):
        lanes = pl.ds(pl.multiple_of(c * LANES, LANES), LANES)
        whole = pl.ds(pl.multiple_of(base + c * LANES, LANES), LANES)
        for r0 in range(0, S, 2):
            rows = [pl.ds(ROWS * r, ROWS) for r in range(r0, min(S, r0 + 2))]
            zones = [zone[x, whole] for x in rows]
            for i in range(2):
                totals = [None] * len(rows)
                for j, (ref, index) in enumerate(refs):
                    values = [table[at + i * len(refs) + j, g] for g in range(regions)]
                    for k, x in enumerate(rows):
                        term = choose(values, zones[k]) * ref[index, x, lanes]
                        totals[k] = term if totals[k] is None else totals[k] + term
                for k, x in enumerate(rows):
                    for ref in partial:
                        totals[k] = totals[k] + ref[i, x, lanes]
                    put(i, x, lanes, whole, totals[k])
        return 0

    lax.fori_loop(0, W // LANES, body, 0)


def both(own, near):
    return [(own, 0), (own, 1), (near, 0), (near, 1)]


def put_in(out):
    def put(i, rows, lanes, whole, value):
        out[i, rows, lanes] = value

    return put


def way_of_tile():
    return lax.axis_index("tile") % 2


def combine_kernel(table, zone, own, near, _, out):
    product(table, 16 * way_of_tile(), zone, both(own, near), [], 0, put_in(out))


def combine(table, zone, own, near, after):
    return pl.pallas_call(
        combine_kernel,
        out_shape=pltpu.VMEM(own.shape, jnp.float32),
        in_specs=[VMEM] * 4 + [ANY],
        out_specs=VMEM,
        compiler_params=pltpu.CompilerParams(vmem_limit_bytes=16 * MIB),
        name="combine",
    )(table, zone, own, near, after)


def rim_product(rim_table, pairs, zones, lanes):
    zones = zones[:, lanes].astype(jnp.int32)
    value = None
    for at, planes in pairs:
        for k, x in enumerate((planes, pltpu.roll(planes, 4, 0))):
            term = lookup(rim_table[at + k], zones) * x
            value = term if value is None else value + term
    return value


def own_kernel(table, zone, own, near, _, base):
    product(table, 16 * way_of_tile() + 8, zone, both(own, near), [], 0, put_in(base))


def own_part(table, zone, own, near, after):
    return pl.pallas_call(
        own_kernel,
        out_shape=pltpu.VMEM(own.shape, jnp.float32),
        in_specs=[VMEM] * 4 + [ANY],
        out_specs=VMEM,
        compiler_params=pltpu.CompilerParams(vmem_limit_bytes=16 * MIB),
        name="own_part",
    )(table, zone, own, near, after)


def bond_kernel(tiers, zone, table, rim_table, rims, heat, h_ref, g_ref, t_in, *refs):
    pairs = tiers == 4
    (edge_zones, *arrays), (t, out, rim) = refs[:-3], refs[-3:]
    L, R, W = t.shape
    C = W // LANES
    row = row_ids()
    if pairs:
        base, part, *edges = arrays

        for i in range(2):
            for r in range(R // ROWS):
                for c in range(C):
                    t[(i * (L - 1),) + tile(r, c)] = base[(i,) + tile(r, c)] + part[(i,) + tile(r, c)]
    else:
        planes, edges = arrays

        def put(i, rows, lanes, whole, value):
            t[i * (L - 1), rows, lanes] = value

        product(table, 0, zone, [(planes, k) for k in range(2 * tiers)], [], 0, put)
    gone = ((row % 4 == 0) & jnp.logical_not(above_exists())) | ((row % 4 == 3) & jnp.logical_not(below_exists()))

    for c in range(C):
        lanes = pl.ds(c * LANES, LANES)
        tiles = [edges[q][:, lanes] if pairs else edges[q, :, lanes] for q in range(tiers)]
        value = rim_product(rim_table, [(2 * q, x) for q, x in enumerate(tiles)], edge_zones, lanes)
        value = jnp.where(gone, 0.0, value)
        rim[:, lanes] = value
        for i in range(2):
            t[i * (L - 1), pl.ds(0, 1), lanes] = value[4 * i + 1 : 4 * i + 2]
            t[i * (L - 1), pl.ds(R - 1, 1), lanes] = value[4 * i + 2 : 4 * i + 3]

    def plane(p, _):
        own, near = p * (L - 1), 1 + p * (L - 3)
        heated = jnp.where(p == 0, 1.0, 0.0)

        def get_s(r, c):
            return t[(own,) + tile(r, c)]

        def get_h(r, c):
            return h_ref[(own,) + tile(r, c)]

        def get_g(r, c):
            return g_ref[(own,) + tile(r, c)]

        def get_z(r, c, s, h):
            at = (near,) + tile(r, c)
            return (h + h_ref[at]) * (t[at] - s) + heated * heat[tile(r, c)]

        def halo(c):
            lanes = pl.ds(LANES * c, LANES)
            ha, hb = pick(rims.at[1], 0, own, lanes, 0), pick(rims.at[3], 0, own, lanes, ROWS - 1)
            return pltpu.roll(rim[:, lanes], (2 - p) * 4 % ROWS, 0), ha, pltpu.roll(rim[:, lanes], 4 - 4 * p, 0), hb

        def put_out(r, c, value):
            out[(p,) + tile(r, c)] = value

        stencil(R, W, get_s, get_h, get_z, halo, put_out, get_g=get_g)
        return 0

    lax.fori_loop(0, 2, plane, 0)


def bond(tiers, zone, tables, rims, heat, h, g, t, edge_zones, arrays):
    _, R, W = t.shape
    args = (zone, *tables, rims, heat, h, g, t, edge_zones, *arrays)
    f32 = jnp.float32
    return pl.pallas_call(
        functools.partial(bond_kernel, tiers),
        out_shape=(
            jax.ShapeDtypeStruct(t.shape, f32),
            jax.ShapeDtypeStruct((2, R, W), f32),
        ),
        in_specs=[VMEM] * len(args),
        out_specs=[VMEM] * 2,
        scratch_shapes=[pltpu.VMEM((ROWS, W), f32)],
        input_output_aliases={7: 0},
        compiler_params=pltpu.CompilerParams(vmem_limit_bytes=24 * MIB),
        name="bond",
    )(*args)


def final_kernel(tiers, zone, table, *refs):
    arrays, (_, out, buf, sem) = refs[:-4], refs[-4:]
    L, R, W = out.shape

    def put(i, rows, lanes, whole, value):
        buf[i, rows, lanes] = value

    if tiers != 4:
        product(table, 0, zone, [(arrays[0], k) for k in range(2 * tiers)], [], 0, put)
    copies = []
    for i in range(2):
        if tiers == 4:
            base, part = arrays
            for r in range(R // ROWS):
                for c in range(W // LANES):
                    buf[(i,) + tile(r, c)] = base[(i,) + tile(r, c)] + part[(i,) + tile(r, c)]
        copies.append(pltpu.make_async_copy(buf.at[i], out.at[i * (L - 1)], sem.at[i]))
        copies[i].start()
    for copy in copies:
        copy.wait()


def final_planes(tiers, zone, table, arrays, out):
    args = (zone, table, *arrays, out)
    _, R, W = out.shape
    return pl.pallas_call(
        functools.partial(final_kernel, tiers),
        out_shape=jax.ShapeDtypeStruct(out.shape, jnp.float32),
        in_specs=[VMEM] * (len(args) - 1) + [HBM],
        out_specs=HBM,
        scratch_shapes=[pltpu.VMEM((2, R, W), jnp.float32), pltpu.SemaphoreType.DMA((2,))],
        input_output_aliases={len(args) - 1: 0},
        compiler_params=pltpu.CompilerParams(vmem_limit_bytes=16 * MIB),
        name="final_planes",
    )(*args)


def across(value, bits, tiers):
    return lax.ppermute(value, "tier", [(i, i ^ bits) for i in range(tiers)])


def every(value, tiers):
    gathered = lax.all_gather(value, "tier", axis=0, tiled=False)
    return gathered.reshape((tiers * value.shape[0],) + value.shape[1:]) if value.ndim == 3 else gathered


def along(value, way, tiers, tiles):
    places = [(tier, tile) for tier in range(tiers) for tile in range(tiles)]
    pairs = [(tier * tiles + tile, routes(tier, tile)[way] * tiles + tile) for tier, tile in places]
    return lax.ppermute(value, ("tier", "tile"), pairs)


def exchange(tiers, tiles, table, zone, planes, after):
    if tiers != 4:
        return (every(planes, tiers),)
    near = along(planes, 0, tiers, tiles)
    total = combine(table, zone, planes, near, after)
    return own_part(table, zone, planes, near, total), along(total, 1, tiers, tiles)


def local(warming, substance, zone, patch, kap, power, ops):
    tiers, tiles = lax.axis_size("tier"), lax.axis_size("tile")
    s, lab, patch = warming[0], substance[0], patch[0]

    planes, heat, s, lab, h = begin(s, lab, patch, kap, power)
    swap_a, swap_b = pack_rows(s, lab, heat, zone, kap)
    pairs = [(i, i ^ 1) for i in range(tiles) if i ^ 1 < tiles]
    got_a = lax.ppermute(swap_a, "tile", pairs)
    pairs = [(i, ((i - 1) ^ 1) + 1) for i in range(1, tiles - 1 + tiles % 2)]
    got_b = lax.ppermute(swap_b, "tile", pairs)
    tables = make_tables(tiers, ops)
    h, g = faces(lab, kap, h)
    arrays = exchange(tiers, tiles, tables[0], zone, planes, h)
    edges, edge_zones, rims = edge_rows(swap_a, swap_b, got_a, got_b)
    h, g = more_faces(lab, kap, h, g, edges)
    if tiers == 4:
        edges = (edges, *(across(edges, bits, tiers) for bits in (1, 2, 3)))
    else:
        edges = (every(edges, tiers),)
    t = outer(s, h, g, rims)
    t, planes = bond(tiers, zone, tables, rims, heat, h, g, t, edge_zones, (*arrays, *edges))
    t = inside(s, h, g, rims, t, planes)
    arrays = exchange(tiers, tiles, tables[0], zone, planes, t)
    out = last_layers(t, h, g, rims)
    out = final_planes(tiers, zone, tables[0], arrays, out)
    return out[None]


def solution(mesh):
    in_specs = (
        P("tier", None, "tile", None),
        P("tier", None, "tile", None),
        P("tile", None),
        P("tier", "tile", None),
        P(),
        P("tier", None),
        P(),
    )
    out_specs = P("tier", None, "tile", None)
    return jax.shard_map(local, mesh=mesh, in_specs=in_specs, out_specs=out_specs, check_vma=False)
```

```python
import functools
import math

import jax
import jax.numpy as jnp
from jax import lax
from jax.experimental import pallas as pl
from jax.experimental.pallas import tpu as pltpu
from jax.sharding import PartitionSpec as P

STEPS = 2
step_dt = 0.04
half_dt = 0.5 * step_dt
LANES = 128
ROWS = 8
MIB = 1 << 20

VMEM = pl.BlockSpec(memory_space=pltpu.VMEM)
SMEM = pl.BlockSpec(memory_space=pltpu.SMEM)
ANY = pl.BlockSpec(memory_space=pl.ANY)
HBM = pl.BlockSpec(memory_space=pltpu.HBM)


def tile(r, c):
    return pl.ds(ROWS * r, ROWS), pl.ds(LANES * c, LANES)


def lane_ids():
    return lax.broadcasted_iota(jnp.int32, (ROWS, LANES), 1)


def row_ids():
    return lax.broadcasted_iota(jnp.int32, (ROWS, LANES), 0)


def choose(values, labels):
    values, bit = list(values), 1
    while len(values) > 1:
        odd = (labels & bit) != 0
        paired = [
            jnp.where(odd, values[i + 1], values[i]) if i + 1 < len(values) else values[i]
            for i in range(0, len(values), 2)
        ]
        values, bit = paired, 2 * bit
    return values[0]


def lookup(row, labels):
    return jnp.take_along_axis(row, labels, axis=1, mode="promise_in_bounds")


def splats(kap):
    return [jnp.full((ROWS, LANES), half_dt * kap[i], jnp.float32) for i in range(kap.shape[0])]


def stencil(R, W, get_s, get_h, get_z, halo, put, get_g=None, put_g=None):
    C, S = W // LANES, R // ROWS
    lane, row = lane_ids(), row_ids()
    first, last = lane == 0, lane == LANES - 1
    top, bottom = row == 0, row == ROWS - 1
    before = None
    for c in range(C):
        s = [get_s(r, c) for r in range(S)]
        h = [get_h(r, c) for r in range(S)]
        rs = [pltpu.roll(v, 1, 1) for v in s]
        rh = [pltpu.roll(v, 1, 1) for v in h] if get_g is None else None
        us = [pltpu.roll(v, 1, 0) for v in s]
        uh = [pltpu.roll(v, 1, 0) for v in h]
        if halo is not None:
            sa, ha, sb, hb = halo(c)
        acc, back, down = [], [], []
        for r in range(S):
            sl = jnp.where(first, 0.0 if c == 0 else before[0][r], rs[r])
            if get_g is None:
                g = h[r] + jnp.where(first, 0.0 if c == 0 else before[1][r], rh[r])
                if put_g is not None:
                    put_g(r, c, g)
            else:
                g = get_g(r, c)
            face = g * (sl - s[r])
            back.append(pltpu.roll(face, LANES - 1, 1))
            if r == 0:
                if halo is None:
                    su, hu = us[0], uh[0]
                else:
                    su, hu = jnp.where(top, sa, us[0]), jnp.where(top, ha, uh[0])
            else:
                su, hu = jnp.where(top, us[r - 1], us[r]), jnp.where(top, uh[r - 1], uh[r])
            upper = (h[r] + hu) * (su - s[r])
            down.append(pltpu.roll(upper, ROWS - 1, 0))
            acc.append((s[r] + get_z(r, c, s[r], h[r])) + (face + upper))
        for r in range(S):
            if r + 1 < S:
                lower = jnp.where(bottom, down[r + 1], down[r])
            elif halo is None:
                lower = down[r]
            else:
                lower = jnp.where(bottom, (h[r] + hb) * (s[r] - sb), down[r])
            acc[r] = acc[r] - lower
        if before is not None:
            for r in range(S):
                put(r, c - 1, before[3][r] - jnp.where(last, back[r], before[2][r]))
        before = (rs, rh, back, acc, s, h)
    for r in range(S):
        out = before[5][r] * before[4][r]
        put(r, C - 1, before[3][r] - jnp.where(last, out, before[2][r]))


def vertical(s, h, s_up, h_up, s_down, h_down):
    return (h + h_up) * (s_up - s) + (h + h_down) * (s_down - s)


def collect(row, pieces):
    value = None
    for q, (source_tile, source) in enumerate(pieces):
        moved = source_tile if q == source else pltpu.roll(source_tile, (q - source) % ROWS, 0)
        value = moved if value is None else jnp.where(row == q, moved, value)
    return value


def begin_kernel(
    s_hbm, lab_hbm, patch_hbm, kap_hbm, power_hbm,
    planes, heat, s_v, lab_v, h_out,
    patch, kap, power, sem,
):
    L, R, W = s_hbm.shape
    C = W // LANES
    small = [
        pltpu.make_async_copy(kap_hbm, kap, sem.at[0]),
        pltpu.make_async_copy(power_hbm, power, sem.at[1]),
        pltpu.make_async_copy(patch_hbm, patch, sem.at[2]),
    ]
    places = [pl.ds(0, 2), pl.ds(L - 2, 2), pl.ds(2, 1), pl.ds(L - 3, 1)]
    places += [(pl.ds(3, L - 6), pl.ds(row, ROWS)) for row in sorted({0, R - ROWS})]
    layers = [
        [
            pltpu.make_async_copy(s_hbm.at[at], s_v.at[at], sem.at[3 + 2 * k]),
            pltpu.make_async_copy(lab_hbm.at[at], lab_v.at[at], sem.at[4 + 2 * k]),
        ]
        for k, at in enumerate(places)
    ]
    layers = layers[:2] + [sum(layers[2:], [])]
    for copy in small + layers[0] + layers[1] + layers[2]:
        copy.start()
    for copy in small:
        copy.wait()
    values = splats(kap)
    heats = step_dt * jnp.broadcast_to(power[...], (ROWS, LANES))

    for c in range(C):
        for r in range(R // ROWS):
            heat[tile(r, c)] = lookup(heats, patch[tile(r, c)])
    for copy in layers[0]:
        copy.wait()

    def plane(p, _):
        own, near = p * (L - 1), 1 + p * (L - 3)
        heated = jnp.where(p == 0, 1.0, 0.0)

        @pl.when(p == 1)
        def _():
            for copy in layers[1]:
                copy.wait()

        def get_s(r, c):
            return s_v[(own,) + tile(r, c)]

        def get_h(r, c):
            value = choose(values, lab_v[(own,) + tile(r, c)])
            h_out[(own,) + tile(r, c)] = value
            return value

        def get_z(r, c, s, h):
            h_near = choose(values, lab_v[(near,) + tile(r, c)])
            h_out[(near,) + tile(r, c)] = h_near
            return (h + h_near) * (s_v[(near,) + tile(r, c)] - s) + heated * heat[tile(r, c)]

        def put(r, c, value):
            planes[(p,) + tile(r, c)] = value

        stencil(R, W, get_s, get_h, get_z, None, put)
        return 0

    lax.fori_loop(0, 2, plane, 0)
    for copy in layers[2]:
        copy.wait()


def begin(s, lab, patch, kap, power):
    _, R, W = s.shape
    f32, i32 = jnp.float32, jnp.int32
    args = [pltpu.with_memory_space_constraint(x, pltpu.HBM) for x in (s, lab, patch, kap, power)]
    return pl.pallas_call(
        begin_kernel,
        out_shape=(
            pltpu.VMEM((2, R, W), f32), pltpu.VMEM((R, W), f32), pltpu.VMEM(s.shape, f32), pltpu.VMEM(lab.shape, i32),
            pltpu.VMEM(s.shape, f32),
        ),
        in_specs=[HBM] * 5,
        out_specs=[VMEM] * 5,
        scratch_shapes=[
            pltpu.VMEM((R, W), i32),
            pltpu.SMEM(kap.shape, f32),
            pltpu.VMEM(power.shape, f32),
            pltpu.SemaphoreType.DMA((15,)),
        ],
        compiler_params=pltpu.CompilerParams(vmem_limit_bytes=16 * MIB),
        name="begin",
    )(*args)


def above_exists():
    return lax.axis_index("tile") > 0


def below_exists():
    return lax.axis_index("tile") < lax.axis_size("tile") - 1


def pack_kernel(
    s_hbm, lab_hbm, s_in, lab_in, heat, zone, kap, swap_a, swap_b, s, lab, rows_v, next_v, sem
):
    L, R, W = s.shape
    C = W // LANES
    copies = []
    if R > 2 * ROWS:
        at = pl.ds(3, L - 6), pl.ds(ROWS, R - 2 * ROWS)
        copies = [
            pltpu.make_async_copy(s_hbm.at[at], s.at[at], sem.at[0]),
            pltpu.make_async_copy(lab_hbm.at[at], lab.at[at], sem.at[1]),
        ]
    for copy in copies:
        copy.start()
    row = row_ids()
    values = splats(kap)
    group = math.gcd(C, 4)

    def body(first, _):
        for c in (group * first + n for n in range(group)):
            lanes = pl.ds(pl.multiple_of(c * LANES, LANES), LANES)
            for k, (start, at_edge, inwards) in enumerate(((0, 0, 1), (R - ROWS, ROWS - 1, ROWS - 2))):
                edge = pl.ds(start, ROWS)
                for base in range(0, L, ROWS):
                    for ref, at in ((s, 0), (lab, L)):
                        tiles = [ref[base + q, edge, lanes] for q in range(ROWS)]
                        for out, source in ((rows_v, at_edge), (next_v, inwards)):
                            packed = collect(row, [(x, source) for x in tiles])
                            if ref is lab:
                                packed = choose(values, packed)
                            out[k, pl.ds(at + base, ROWS), lanes] = packed
                zones = zone[edge, lanes].astype(jnp.float32)
                rows_v[k, pl.ds(3 * L, ROWS), lanes] = collect(row, [(zones, at_edge), (heat[edge, lanes], at_edge)])
        return 0

    lax.fori_loop(0, C // group, body, 0)

    def side(k, _):
        def at(base, r, c):
            return k, pl.ds(base + ROWS * r, ROWS), pl.ds(LANES * c, LANES)

        def get_s(r, c):
            return rows_v[at(0, r, c)]

        def get_h(r, c):
            return rows_v[at(L, r, c)]

        def get_z(r, c, s, h):
            flow = (h + next_v[at(L, r, c)]) * (next_v[at(0, r, c)] - s)
            if r == 0:
                flow = flow + jnp.where(row == 0, pltpu.roll(rows_v[at(3 * L, 0, c)], ROWS - 1, 0), 0.0)
            return flow

        def ends(c):
            last = L // ROWS - 1
            return get_s(0, c), get_h(0, c), get_s(last, c), get_h(last, c)

        def put(r, c, value):
            rows_v[at(2 * L, r, c)] = value

        stencil(L, W, get_s, get_h, get_z, ends, put)
        return 0

    lax.fori_loop(0, 2, side, 0)
    odd = lax.axis_index("tile") % 2

    for r in range(swap_a.shape[0] // ROWS):
        for c in range(C):
            swap_a[tile(r, c)] = rows_v[(1 - odd,) + tile(r, c)]
            swap_b[tile(r, c)] = rows_v[(odd,) + tile(r, c)]
    for copy in copies:
        copy.wait()


def pack_rows(s, lab, s_v, lab_v, heat, zone, kap):
    L, _, W = s.shape
    f32 = jnp.float32
    rows = 3 * L + ROWS
    s, lab = (pltpu.with_memory_space_constraint(x, pltpu.HBM) for x in (s, lab))
    return pl.pallas_call(
        pack_kernel,
        out_shape=(
            pltpu.VMEM((rows, W), f32),
            pltpu.VMEM((rows, W), f32),
            jax.ShapeDtypeStruct(s.shape, f32),
            jax.ShapeDtypeStruct(lab.shape, jnp.int32),
        ),
        in_specs=[HBM] * 2 + [VMEM] * 4 + [SMEM],
        out_specs=[VMEM] * 4,
        scratch_shapes=[
            pltpu.VMEM((2, rows, W), f32),
            pltpu.VMEM((2, 2 * L, W), f32),
            pltpu.SemaphoreType.DMA((2,)),
        ],
        input_output_aliases={2: 2, 3: 3},
        compiler_params=pltpu.CompilerParams(vmem_limit_bytes=24 * MIB),
        name="pack_rows",
    )(s, lab, s_v, lab_v, heat, zone, kap)


def edge_kernel(own_a, own_b, got_a, got_b, _, edges, zones, rims):
    rows, W = own_a.shape
    L = (rows - ROWS) // 3
    odd = lax.axis_index("tile") % 2 == 1
    for side, exists in enumerate((above_exists(), below_exists())):
        first_swap = odd if side == 0 else jnp.logical_not(odd)
        k_out, k_in = (0, 1) if side == 0 else (3, 2)

        def both_sides(at, n):
            at = pl.ds(at, n)
            other = jnp.where(exists, jnp.where(first_swap, got_a[at, :], got_b[at, :]), 0.0)
            return other, jnp.where(first_swap, own_a[at, :], own_b[at, :])

        for base in range(0, L, ROWS):
            part = pl.ds(base, ROWS)
            s_out, s_in = both_sides(base, ROWS)
            h_out, h_in = both_sides(L + base, ROWS)
            u_out, u_in = both_sides(2 * L + base, ROWS)
            face = (h_in + h_out) * (s_out - s_in)
            t_out, t_in = jnp.where(exists, u_out - face, 0.0), u_in + face
            rims[2 * side, part, :] = s_out
            rims[2 * side + 1, part, :] = h_out
            rims[4 + side, part, :] = t_out
            for i, l in ((0, 0), (1, L - 1)):
                if base <= l < base + ROWS:
                    edges[pl.ds(4 * i + k_out, 1), :] = t_out[l - base : l - base + 1]
                    edges[pl.ds(4 * i + k_in, 1), :] = t_in[l - base : l - base + 1]
        z_out, z_in = both_sides(3 * L, 1)
        for i in range(2):
            zones[pl.ds(4 * i + k_out, 1), :] = z_out
            zones[pl.ds(4 * i + k_in, 1), :] = z_in


def edge_rows(own_a, own_b, got_a, got_b, after):
    rows, W = own_a.shape
    f32 = jnp.float32
    return pl.pallas_call(
        edge_kernel,
        out_shape=(pltpu.VMEM((ROWS, W), f32), pltpu.VMEM((ROWS, W), f32), pltpu.VMEM((6, (rows - ROWS) // 3, W), f32)),
        in_specs=[VMEM] * 4 + [ANY],
        out_specs=[VMEM] * 3,
        compiler_params=pltpu.CompilerParams(vmem_limit_bytes=16 * MIB),
        name="edge_rows",
    )(own_a, own_b, got_a, got_b, after)


def pick(ref, base, l, lanes, row):
    at = base + (l // ROWS) * ROWS
    if not isinstance(l, int):
        at = pl.multiple_of(at, ROWS)
    return pltpu.roll(ref[pl.ds(at, ROWS), lanes], (row - l) % ROWS, 0)


def halo_rows(rims, state, lanes, l):
    end = ROWS - 1
    where = ((state[0], 0), (1, 0), (state[1], end), (3, end))
    return tuple(pick(rims.at[k], 0, l, lanes, row) for k, row in where)


def fill_faces(first, end, h_at, h_out, g_out):
    _, R, W = h_out.shape
    edge = lane_ids() == 0

    def body(l, _):
        before = [0.0] * (R // ROWS)
        for c in range(W // LANES):
            for r in range(R // ROWS):
                at = (l,) + tile(r, c)
                h = h_at(at, c)
                moved = pltpu.roll(h, 1, 1)
                h_out[at] = h
                g_out[at] = h + jnp.where(edge, before[r], moved)
                before[r] = moved
        return 0

    lax.fori_loop(first, end, body, 0)


def from_labels(lab, kap):
    values = splats(kap)
    table, lane = jnp.zeros((ROWS, LANES), jnp.float32), lane_ids()
    for k, value in enumerate(values):
        table = jnp.where(lane == k, value, table)
    return lambda at, c: lookup(table, lab[at]) if c % 4 == 0 else choose(values, lab[at])


def faces_kernel(lab, kap, h_in, h_out, g_out):
    L = lab.shape[0]

    def held(at, c):
        return h_out[at]

    getter = from_labels(lab, kap)
    for first, end in ((0, 2), (L - 2, L)):
        fill_faces(first, end, held, h_out, g_out)
    for l in (2, L - 3):
        fill_faces(l, l + 1, getter, h_out, g_out)


def faces(lab, kap, h):
    return pl.pallas_call(
        faces_kernel,
        out_shape=(jax.ShapeDtypeStruct(lab.shape, jnp.float32),) * 2,
        in_specs=[VMEM, SMEM, VMEM],
        out_specs=[VMEM] * 2,
        input_output_aliases={2: 0},
        compiler_params=pltpu.CompilerParams(vmem_limit_bytes=20 * MIB),
        name="faces",
    )(lab, kap, h)


def more_faces_kernel(lab, kap, h_in, g_in, _, h_out, g_out):
    fill_faces(3, lab.shape[0] - 3, from_labels(lab, kap), h_out, g_out)


def more_faces(lab, kap, h, g, after):
    return pl.pallas_call(
        more_faces_kernel,
        out_shape=(jax.ShapeDtypeStruct(lab.shape, jnp.float32),) * 2,
        in_specs=[VMEM, SMEM, VMEM, VMEM, ANY],
        out_specs=[VMEM] * 2,
        input_output_aliases={2: 0, 3: 1},
        compiler_params=pltpu.CompilerParams(vmem_limit_bytes=24 * MIB),
        name="more_faces",
    )(lab, kap, h, g, after)


def layer_step(l, s_ref, h_ref, g_ref, halo, put):
    _, R, W = s_ref.shape

    def get_s(r, c):
        return s_ref[(l,) + tile(r, c)]

    def get_h(r, c):
        return h_ref[(l,) + tile(r, c)]

    def get_g(r, c):
        return g_ref[(l,) + tile(r, c)]

    def get_z(r, c, s, h):
        a, b = (l - 1,) + tile(r, c), (l + 1,) + tile(r, c)
        return vertical(s, h, s_ref[a], h_ref[a], s_ref[b], h_ref[b])

    stencil(R, W, get_s, get_h, get_z, halo, put, get_g=get_g)


def first_step(l, s_ref, h_ref, g_ref, halo, t):
    def put(r, c, value):
        t[(l,) + tile(r, c)] = value

    layer_step(l, s_ref, h_ref, g_ref, halo, put)


def outer_kernel(s_ref, h_ref, g_ref, rims, t):
    L = s_ref.shape[0]

    def body(p, _):
        l = 1 + p * (L - 3)

        def halo(c):
            return halo_rows(rims, (0, 2), pl.ds(LANES * c, LANES), l)

        first_step(l, s_ref, h_ref, g_ref, halo, t)
        return 0

    lax.fori_loop(0, 2, body, 0)


def outer(s, h, g, rims):
    return pl.pallas_call(
        outer_kernel,
        out_shape=pltpu.VMEM(s.shape, jnp.float32),
        in_specs=[VMEM] * 4,
        out_specs=VMEM,
        compiler_params=pltpu.CompilerParams(vmem_limit_bytes=20 * MIB),
        name="outer",
    )(s, h, g, rims)


def inside_kernel(s_ref, h_ref, g_ref, rims, t_in, _, t):
    L = s_ref.shape[0]

    def body(l, _):
        def halo(c):
            return halo_rows(rims, (0, 2), pl.ds(LANES * c, LANES), l)

        first_step(l, s_ref, h_ref, g_ref, halo, t)
        return 0

    lax.fori_loop(2, L - 2, body, 0)


def inside(s, h, g, rims, t, after):
    return pl.pallas_call(
        inside_kernel,
        out_shape=jax.ShapeDtypeStruct(s.shape, jnp.float32),
        in_specs=[VMEM] * 5 + [ANY],
        out_specs=VMEM,
        input_output_aliases={4: 0},
        compiler_params=pltpu.CompilerParams(vmem_limit_bytes=24 * MIB),
        name="inside",
    )(s, h, g, rims, t, after)


def last_kernel(t_ref, h_ref, g_ref, rims, out, buf, sem):
    L, R, W = t_ref.shape

    def send(l):
        return pltpu.make_async_copy(buf.at[l], out.at[l], sem.at[l])

    def body(l, _):
        def put(r, c, value):
            buf[(l,) + tile(r, c)] = value

        def halo(c):
            return halo_rows(rims, (4, 5), pl.ds(LANES * c, LANES), l)

        layer_step(l, t_ref, h_ref, g_ref, halo, put)
        send(l).start()
        return 0

    lax.fori_loop(1, L - 1, body, 0)

    def drain(l, _):
        send(l).wait()
        return 0

    lax.fori_loop(1, L - 1, drain, 0)


def last_layers(t, h, g, rims):
    L = t.shape[0]
    return pl.pallas_call(
        last_kernel,
        out_shape=jax.ShapeDtypeStruct(t.shape, jnp.float32),
        in_specs=[VMEM] * 4,
        out_specs=HBM,
        scratch_shapes=[pltpu.VMEM(t.shape, jnp.float32), pltpu.SemaphoreType.DMA((L,))],
        compiler_params=pltpu.CompilerParams(vmem_limit_bytes=24 * MIB),
        name="last_layers",
    )(t, h, g, rims)


def near_of(side):
    me = lax.axis_index("tier")
    return (me ^ 1, me ^ 2) if side == 0 else (me ^ 2, me ^ 1)


def routes(tier, tile):
    odd = tile % 2
    return tier ^ (1 + odd), tier ^ (2 - odd)


def entries(tiers):
    me = lax.axis_index("tier")
    if tiers != 4:
        return [(2 * me + i, j) for i in range(2) for j in range(2 * tiers)]
    listed = []
    for side in range(2):
        near, target = near_of(side)
        columns = [2 * me, 2 * me + 1, 2 * near, 2 * near + 1]
        for who in (target, me):
            listed += [(2 * who + i, j) for i in range(2) for j in columns]
    return listed


def rim_entries(tiers):
    me = lax.axis_index("tier")
    return [me ^ q if tiers == 4 else q for q in range(tiers)]


def table_kernel(tiers, ops, table, rim_table):
    regions = ops.shape[0]
    for k, (i, j) in enumerate(entries(tiers)):
        for g in range(regions):
            table[k, g] = jnp.full((ROWS, LANES), ops[g, i, j], jnp.float32)
    lane, upper = lane_ids(), row_ids() < 4
    me = lax.axis_index("tier")
    for q, source in enumerate(rim_entries(tiers)):
        for k in range(2):
            value = jnp.zeros((ROWS, LANES), jnp.float32)
            for g in range(regions):
                a, b = ops[g, 2 * me, 2 * source + k], ops[g, 2 * me + 1, 2 * source + 1 - k]
                value = jnp.where(lane == g, jnp.where(upper, a, b), value)
            rim_table[2 * q + k] = value


def make_tables(tiers, ops):
    regions = ops.shape[0]
    f32 = jnp.float32
    count, rims = 32 if tiers == 4 else 4 * tiers, 2 * tiers
    return pl.pallas_call(
        functools.partial(table_kernel, tiers),
        out_shape=(pltpu.VMEM((count, regions, ROWS, LANES), f32), pltpu.VMEM((rims, ROWS, LANES), f32)),
        in_specs=[SMEM],
        out_specs=[VMEM, VMEM],
        compiler_params=pltpu.CompilerParams(vmem_limit_bytes=16 * MIB),
        name="make_tables",
    )(ops)


def product(table, at, zone, refs, partial, base, put):
    regions = table.shape[1]
    R, W = refs[0][0].shape[1:]
    S = R // ROWS

    def body(c, _):
        lanes = pl.ds(pl.multiple_of(c * LANES, LANES), LANES)
        whole = pl.ds(pl.multiple_of(base + c * LANES, LANES), LANES)
        for r0 in range(0, S, 2):
            rows = [pl.ds(ROWS * r, ROWS) for r in range(r0, min(S, r0 + 2))]
            zones = [zone[x, whole] for x in rows]
            for i in range(2):
                totals = [None] * len(rows)
                for j, (ref, index) in enumerate(refs):
                    values = [table[at + i * len(refs) + j, g] for g in range(regions)]
                    for k, x in enumerate(rows):
                        term = choose(values, zones[k]) * ref[index, x, lanes]
                        totals[k] = term if totals[k] is None else totals[k] + term
                for k, x in enumerate(rows):
                    for ref in partial:
                        totals[k] = totals[k] + ref[i, x, lanes]
                    put(i, x, lanes, whole, totals[k])
        return 0

    lax.fori_loop(0, W // LANES, body, 0)


def both(own, near):
    return [(own, 0), (own, 1), (near, 0), (near, 1)]


def put_in(out):
    def put(i, rows, lanes, whole, value):
        out[i, rows, lanes] = value

    return put


def way_of_tile():
    return lax.axis_index("tile") % 2


def combine_kernel(table, zone, own, near, _, out):
    product(table, 16 * way_of_tile(), zone, both(own, near), [], 0, put_in(out))


def combine(table, zone, own, near, after):
    return pl.pallas_call(
        combine_kernel,
        out_shape=pltpu.VMEM(own.shape, jnp.float32),
        in_specs=[VMEM] * 4 + [ANY],
        out_specs=VMEM,
        compiler_params=pltpu.CompilerParams(vmem_limit_bytes=16 * MIB),
        name="combine",
    )(table, zone, own, near, after)


def rim_product(rim_table, pairs, zones, lanes):
    zones = zones[:, lanes].astype(jnp.int32)
    value = None
    for at, planes in pairs:
        for k, x in enumerate((planes, pltpu.roll(planes, 4, 0))):
            term = lookup(rim_table[at + k], zones) * x
            value = term if value is None else value + term
    return value


def own_kernel(table, zone, own, near, _, base):
    product(table, 16 * way_of_tile() + 8, zone, both(own, near), [], 0, put_in(base))


def own_part(table, zone, own, near, after):
    return pl.pallas_call(
        own_kernel,
        out_shape=pltpu.VMEM(own.shape, jnp.float32),
        in_specs=[VMEM] * 4 + [ANY],
        out_specs=VMEM,
        compiler_params=pltpu.CompilerParams(vmem_limit_bytes=16 * MIB),
        name="own_part",
    )(table, zone, own, near, after)


def bond_kernel(tiers, zone, table, rim_table, rims, heat, h_ref, g_ref, t_in, *refs):
    pairs = tiers == 4
    (edge_zones, *arrays), (t, out, rim) = refs[:-3], refs[-3:]
    L, R, W = t.shape
    C = W // LANES
    row = row_ids()
    if pairs:
        base, part, *edges = arrays

        for i in range(2):
            for r in range(R // ROWS):
                for c in range(C):
                    t[(i * (L - 1),) + tile(r, c)] = base[(i,) + tile(r, c)] + part[(i,) + tile(r, c)]
    else:
        planes, edges = arrays

        def put(i, rows, lanes, whole, value):
            t[i * (L - 1), rows, lanes] = value

        product(table, 0, zone, [(planes, k) for k in range(2 * tiers)], [], 0, put)
    gone = ((row % 4 == 0) & jnp.logical_not(above_exists())) | ((row % 4 == 3) & jnp.logical_not(below_exists()))

    for c in range(C):
        lanes = pl.ds(c * LANES, LANES)
        tiles = [edges[q][:, lanes] if pairs else edges[q, :, lanes] for q in range(tiers)]
        value = rim_product(rim_table, [(2 * q, x) for q, x in enumerate(tiles)], edge_zones, lanes)
        value = jnp.where(gone, 0.0, value)
        rim[:, lanes] = value
        for i in range(2):
            t[i * (L - 1), pl.ds(0, 1), lanes] = value[4 * i + 1 : 4 * i + 2]
            t[i * (L - 1), pl.ds(R - 1, 1), lanes] = value[4 * i + 2 : 4 * i + 3]

    def plane(p, _):
        own, near = p * (L - 1), 1 + p * (L - 3)
        heated = jnp.where(p == 0, 1.0, 0.0)

        def get_s(r, c):
            return t[(own,) + tile(r, c)]

        def get_h(r, c):
            return h_ref[(own,) + tile(r, c)]

        def get_g(r, c):
            return g_ref[(own,) + tile(r, c)]

        def get_z(r, c, s, h):
            at = (near,) + tile(r, c)
            return (h + h_ref[at]) * (t[at] - s) + heated * heat[tile(r, c)]

        def halo(c):
            lanes = pl.ds(LANES * c, LANES)
            ha, hb = pick(rims.at[1], 0, own, lanes, 0), pick(rims.at[3], 0, own, lanes, ROWS - 1)
            return pltpu.roll(rim[:, lanes], (2 - p) * 4 % ROWS, 0), ha, pltpu.roll(rim[:, lanes], 4 - 4 * p, 0), hb

        def put_out(r, c, value):
            out[(p,) + tile(r, c)] = value

        stencil(R, W, get_s, get_h, get_z, halo, put_out, get_g=get_g)
        return 0

    lax.fori_loop(0, 2, plane, 0)


def bond(tiers, zone, tables, rims, heat, h, g, t, edge_zones, arrays):
    _, R, W = t.shape
    args = (zone, *tables, rims, heat, h, g, t, edge_zones, *arrays)
    f32 = jnp.float32
    return pl.pallas_call(
        functools.partial(bond_kernel, tiers),
        out_shape=(
            jax.ShapeDtypeStruct(t.shape, f32),
            jax.ShapeDtypeStruct((2, R, W), f32),
        ),
        in_specs=[VMEM] * len(args),
        out_specs=[VMEM] * 2,
        scratch_shapes=[pltpu.VMEM((ROWS, W), f32)],
        input_output_aliases={7: 0},
        compiler_params=pltpu.CompilerParams(vmem_limit_bytes=24 * MIB),
        name="bond",
    )(*args)


def final_kernel(tiers, zone, table, *refs):
    arrays, (_, out, buf, sem) = refs[:-4], refs[-4:]
    L, R, W = out.shape

    def put(i, rows, lanes, whole, value):
        buf[i, rows, lanes] = value

    if tiers != 4:
        product(table, 0, zone, [(arrays[0], k) for k in range(2 * tiers)], [], 0, put)
    copies = []
    for i in range(2):
        if tiers == 4:
            base, part = arrays
            for r in range(R // ROWS):
                for c in range(W // LANES):
                    buf[(i,) + tile(r, c)] = base[(i,) + tile(r, c)] + part[(i,) + tile(r, c)]
        copies.append(pltpu.make_async_copy(buf.at[i], out.at[i * (L - 1)], sem.at[i]))
        copies[i].start()
    for copy in copies:
        copy.wait()


def final_planes(tiers, zone, table, arrays, out):
    args = (zone, table, *arrays, out)
    _, R, W = out.shape
    return pl.pallas_call(
        functools.partial(final_kernel, tiers),
        out_shape=jax.ShapeDtypeStruct(out.shape, jnp.float32),
        in_specs=[VMEM] * (len(args) - 1) + [HBM],
        out_specs=HBM,
        scratch_shapes=[pltpu.VMEM((2, R, W), jnp.float32), pltpu.SemaphoreType.DMA((2,))],
        input_output_aliases={len(args) - 1: 0},
        compiler_params=pltpu.CompilerParams(vmem_limit_bytes=16 * MIB),
        name="final_planes",
    )(*args)


def across(value, bits, tiers):
    return lax.ppermute(value, "tier", [(i, i ^ bits) for i in range(tiers)])


def every(value, tiers):
    gathered = lax.all_gather(value, "tier", axis=0, tiled=False)
    return gathered.reshape((tiers * value.shape[0],) + value.shape[1:]) if value.ndim == 3 else gathered


def along(value, way, tiers, tiles):
    places = [(tier, tile) for tier in range(tiers) for tile in range(tiles)]
    pairs = [(tier * tiles + tile, routes(tier, tile)[way] * tiles + tile) for tier, tile in places]
    return lax.ppermute(value, ("tier", "tile"), pairs)


def exchange(tiers, tiles, table, zone, planes, after):
    if tiers != 4:
        return (every(planes, tiers),), planes
    near = along(planes, 0, tiers, tiles)
    total = combine(table, zone, planes, near, after)
    return (own_part(table, zone, planes, near, total), along(total, 1, tiers, tiles)), total


def local(warming, substance, zone, patch, kap, power, ops):
    tiers, tiles = lax.axis_size("tier"), lax.axis_size("tile")
    s, lab, patch = warming[0], substance[0], patch[0]

    planes, heat, s_v, lab_v, h = begin(s, lab, patch, kap, power)
    swap_a, swap_b, s, lab = pack_rows(s, lab, s_v, lab_v, heat, zone, kap)
    pairs = [(i, i ^ 1) for i in range(tiles) if i ^ 1 < tiles]
    got_a = lax.ppermute(swap_a, "tile", pairs)
    pairs = [(i, ((i - 1) ^ 1) + 1) for i in range(1, tiles - 1 + tiles % 2)]
    got_b = lax.ppermute(swap_b, "tile", pairs)
    tables = make_tables(tiers, ops)
    h, g = faces(lab, kap, h)
    arrays, _ = exchange(tiers, tiles, tables[0], zone, planes, h)
    edges, edge_zones, rims = edge_rows(swap_a, swap_b, got_a, got_b, h)
    h, g = more_faces(lab, kap, h, g, edges)
    if tiers == 4:
        edges = (edges, *(across(edges, bits, tiers) for bits in (1, 2, 3)))
    else:
        edges = (every(edges, tiers),)
    t = outer(s, h, g, rims)
    t, planes = bond(tiers, zone, tables, rims, heat, h, g, t, edge_zones, (*arrays, *edges))
    t = inside(s, h, g, rims, t, planes)
    arrays, _ = exchange(tiers, tiles, tables[0], zone, planes, t)
    out = last_layers(t, h, g, rims)
    out = final_planes(tiers, zone, tables[0], arrays, out)
    return out[None]


def solution(mesh):
    in_specs = (
        P("tier", None, "tile", None),
        P("tier", None, "tile", None),
        P("tile", None),
        P("tier", "tile", None),
        P(),
        P("tier", None),
        P(),
    )
    out_specs = P("tier", None, "tile", None)
    return jax.shard_map(local, mesh=mesh, in_specs=in_specs, out_specs=out_specs, check_vma=False)
```

```python
import functools
import math

import jax
import jax.numpy as jnp
from jax import lax
from jax.experimental import pallas as pl
from jax.experimental.pallas import tpu as pltpu
from jax.sharding import PartitionSpec as P

STEPS = 2
step_dt = 0.04
half_dt = 0.5 * step_dt
LANES = 128
ROWS = 8
MIB = 1 << 20

VMEM = pl.BlockSpec(memory_space=pltpu.VMEM)
SMEM = pl.BlockSpec(memory_space=pltpu.SMEM)
ANY = pl.BlockSpec(memory_space=pl.ANY)
HBM = pl.BlockSpec(memory_space=pltpu.HBM)


def tile(r, c):
    return pl.ds(ROWS * r, ROWS), pl.ds(LANES * c, LANES)


def lane_ids():
    return lax.broadcasted_iota(jnp.int32, (ROWS, LANES), 1)


def row_ids():
    return lax.broadcasted_iota(jnp.int32, (ROWS, LANES), 0)


def choose(values, labels):
    values, bit = list(values), 1
    while len(values) > 1:
        odd = (labels & bit) != 0
        paired = [
            jnp.where(odd, values[i + 1], values[i]) if i + 1 < len(values) else values[i]
            for i in range(0, len(values), 2)
        ]
        values, bit = paired, 2 * bit
    return values[0]


def lookup(row, labels):
    return jnp.take_along_axis(row, labels, axis=1, mode="promise_in_bounds")


def splats(kap):
    return [jnp.full((ROWS, LANES), half_dt * kap[i], jnp.float32) for i in range(kap.shape[0])]


def stencil(R, W, get_s, get_h, get_z, halo, put, get_g=None, put_g=None):
    C, S = W // LANES, R // ROWS
    lane, row = lane_ids(), row_ids()
    first, last = lane == 0, lane == LANES - 1
    top, bottom = row == 0, row == ROWS - 1
    before = None
    for c in range(C):
        s = [get_s(r, c) for r in range(S)]
        h = [get_h(r, c) for r in range(S)]
        rs = [pltpu.roll(v, 1, 1) for v in s]
        rh = [pltpu.roll(v, 1, 1) for v in h] if get_g is None else None
        us = [pltpu.roll(v, 1, 0) for v in s]
        uh = [pltpu.roll(v, 1, 0) for v in h]
        if halo is not None:
            sa, ha, sb, hb = halo(c)
        acc, back, down = [], [], []
        for r in range(S):
            sl = jnp.where(first, 0.0 if c == 0 else before[0][r], rs[r])
            if get_g is None:
                g = h[r] + jnp.where(first, 0.0 if c == 0 else before[1][r], rh[r])
                if put_g is not None:
                    put_g(r, c, g)
            else:
                g = get_g(r, c)
            face = g * (sl - s[r])
            back.append(pltpu.roll(face, LANES - 1, 1))
            if r == 0:
                if halo is None:
                    su, hu = us[0], uh[0]
                else:
                    su, hu = jnp.where(top, sa, us[0]), jnp.where(top, ha, uh[0])
            else:
                su, hu = jnp.where(top, us[r - 1], us[r]), jnp.where(top, uh[r - 1], uh[r])
            upper = (h[r] + hu) * (su - s[r])
            down.append(pltpu.roll(upper, ROWS - 1, 0))
            acc.append((s[r] + get_z(r, c, s[r], h[r])) + (face + upper))
        for r in range(S):
            if r + 1 < S:
                lower = jnp.where(bottom, down[r + 1], down[r])
            elif halo is None:
                lower = down[r]
            else:
                lower = jnp.where(bottom, (h[r] + hb) * (s[r] - sb), down[r])
            acc[r] = acc[r] - lower
        if before is not None:
            for r in range(S):
                put(r, c - 1, before[3][r] - jnp.where(last, back[r], before[2][r]))
        before = (rs, rh, back, acc, s, h)
    for r in range(S):
        out = before[5][r] * before[4][r]
        put(r, C - 1, before[3][r] - jnp.where(last, out, before[2][r]))


def vertical(s, h, s_up, h_up, s_down, h_down):
    return (h + h_up) * (s_up - s) + (h + h_down) * (s_down - s)


def collect(row, pieces):
    value = None
    for q, (source_tile, source) in enumerate(pieces):
        moved = source_tile if q == source else pltpu.roll(source_tile, (q - source) % ROWS, 0)
        value = moved if value is None else jnp.where(row == q, moved, value)
    return value


def begin_kernel(
    s_hbm, lab_hbm, patch_hbm, kap_hbm, power_hbm,
    planes, heat, s_v, lab_v, h_out,
    patch, kap, power, sem,
):
    L, R, W = s_hbm.shape
    C = W // LANES
    small = [
        pltpu.make_async_copy(kap_hbm, kap, sem.at[0]),
        pltpu.make_async_copy(power_hbm, power, sem.at[1]),
        pltpu.make_async_copy(patch_hbm, patch, sem.at[2]),
    ]
    places = [pl.ds(0, 2), pl.ds(L - 2, 2), pl.ds(2, 1), pl.ds(L - 3, 1)]
    places += [(pl.ds(3, L - 6), pl.ds(row, ROWS)) for row in sorted({0, R - ROWS})]
    layers = [
        [
            pltpu.make_async_copy(s_hbm.at[at], s_v.at[at], sem.at[3 + 2 * k]),
            pltpu.make_async_copy(lab_hbm.at[at], lab_v.at[at], sem.at[4 + 2 * k]),
        ]
        for k, at in enumerate(places)
    ]
    layers = layers[:2] + [sum(layers[2:], [])]
    for copy in small + layers[0] + layers[1] + layers[2]:
        copy.start()
    for copy in small:
        copy.wait()
    values = splats(kap)
    heats = step_dt * jnp.broadcast_to(power[...], (ROWS, LANES))

    for c in range(C):
        for r in range(R // ROWS):
            heat[tile(r, c)] = lookup(heats, patch[tile(r, c)])
    for copy in layers[0]:
        copy.wait()

    def plane(p, _):
        own, near = p * (L - 1), 1 + p * (L - 3)
        heated = jnp.where(p == 0, 1.0, 0.0)

        @pl.when(p == 1)
        def _():
            for copy in layers[1]:
                copy.wait()

        def get_s(r, c):
            return s_v[(own,) + tile(r, c)]

        def get_h(r, c):
            value = choose(values, lab_v[(own,) + tile(r, c)])
            h_out[(own,) + tile(r, c)] = value
            return value

        def get_z(r, c, s, h):
            h_near = choose(values, lab_v[(near,) + tile(r, c)])
            h_out[(near,) + tile(r, c)] = h_near
            return (h + h_near) * (s_v[(near,) + tile(r, c)] - s) + heated * heat[tile(r, c)]

        def put(r, c, value):
            planes[(p,) + tile(r, c)] = value

        stencil(R, W, get_s, get_h, get_z, None, put)
        return 0

    lax.fori_loop(0, 2, plane, 0)
    for copy in layers[2]:
        copy.wait()


def begin(s, lab, patch, kap, power):
    _, R, W = s.shape
    f32, i32 = jnp.float32, jnp.int32
    args = [pltpu.with_memory_space_constraint(x, pltpu.HBM) for x in (s, lab, patch, kap, power)]
    return pl.pallas_call(
        begin_kernel,
        out_shape=(
            pltpu.VMEM((2, R, W), f32), pltpu.VMEM((R, W), f32), pltpu.VMEM(s.shape, f32), pltpu.VMEM(lab.shape, i32),
            pltpu.VMEM(s.shape, f32),
        ),
        in_specs=[HBM] * 5,
        out_specs=[VMEM] * 5,
        scratch_shapes=[
            pltpu.VMEM((R, W), i32),
            pltpu.SMEM(kap.shape, f32),
            pltpu.VMEM(power.shape, f32),
            pltpu.SemaphoreType.DMA((15,)),
        ],
        compiler_params=pltpu.CompilerParams(vmem_limit_bytes=16 * MIB),
        name="begin",
    )(*args)


def above_exists():
    return lax.axis_index("tile") > 0


def below_exists():
    return lax.axis_index("tile") < lax.axis_size("tile") - 1


def pack_kernel(
    s_hbm, s_in, lab, heat, zone, kap, swap_a, swap_b, s, rows_v, next_v, sem
):
    L, R, W = s.shape
    C = W // LANES
    copies = []
    if R > 2 * ROWS:
        at = pl.ds(3, L - 6), pl.ds(ROWS, R - 2 * ROWS)
        copies = [pltpu.make_async_copy(s_hbm.at[at], s.at[at], sem)]
    for copy in copies:
        copy.start()
    row = row_ids()
    values = splats(kap)
    group = math.gcd(C, 4)

    def body(first, _):
        for c in (group * first + n for n in range(group)):
            lanes = pl.ds(pl.multiple_of(c * LANES, LANES), LANES)
            for k, (start, at_edge, inwards) in enumerate(((0, 0, 1), (R - ROWS, ROWS - 1, ROWS - 2))):
                edge = pl.ds(start, ROWS)
                for base in range(0, L, ROWS):
                    for ref, at in ((s, 0), (lab, L)):
                        tiles = [ref[base + q, edge, lanes] for q in range(ROWS)]
                        for out, source in ((rows_v, at_edge), (next_v, inwards)):
                            packed = collect(row, [(x, source) for x in tiles])
                            if ref is lab:
                                packed = choose(values, packed)
                            out[k, pl.ds(at + base, ROWS), lanes] = packed
                zones = zone[edge, lanes].astype(jnp.float32)
                rows_v[k, pl.ds(3 * L, ROWS), lanes] = collect(row, [(zones, at_edge), (heat[edge, lanes], at_edge)])
        return 0

    lax.fori_loop(0, C // group, body, 0)

    def side(k, _):
        def at(base, r, c):
            return k, pl.ds(base + ROWS * r, ROWS), pl.ds(LANES * c, LANES)

        def get_s(r, c):
            return rows_v[at(0, r, c)]

        def get_h(r, c):
            return rows_v[at(L, r, c)]

        def get_z(r, c, s, h):
            flow = (h + next_v[at(L, r, c)]) * (next_v[at(0, r, c)] - s)
            if r == 0:
                flow = flow + jnp.where(row == 0, pltpu.roll(rows_v[at(3 * L, 0, c)], ROWS - 1, 0), 0.0)
            return flow

        def ends(c):
            last = L // ROWS - 1
            return get_s(0, c), get_h(0, c), get_s(last, c), get_h(last, c)

        def put(r, c, value):
            rows_v[at(2 * L, r, c)] = value

        stencil(L, W, get_s, get_h, get_z, ends, put)
        return 0

    lax.fori_loop(0, 2, side, 0)
    odd = lax.axis_index("tile") % 2

    for r in range(swap_a.shape[0] // ROWS):
        for c in range(C):
            swap_a[tile(r, c)] = rows_v[(1 - odd,) + tile(r, c)]
            swap_b[tile(r, c)] = rows_v[(odd,) + tile(r, c)]
    for copy in copies:
        copy.wait()


def pack_rows(s, s_v, lab_v, heat, zone, kap):
    L, _, W = s.shape
    f32 = jnp.float32
    rows = 3 * L + ROWS
    s = pltpu.with_memory_space_constraint(s, pltpu.HBM)
    return pl.pallas_call(
        pack_kernel,
        out_shape=(
            pltpu.VMEM((rows, W), f32),
            pltpu.VMEM((rows, W), f32),
            jax.ShapeDtypeStruct(s.shape, f32),
        ),
        in_specs=[HBM] + [VMEM] * 4 + [SMEM],
        out_specs=[VMEM] * 3,
        scratch_shapes=[
            pltpu.VMEM((2, rows, W), f32),
            pltpu.VMEM((2, 2 * L, W), f32),
            pltpu.SemaphoreType.DMA,
        ],
        input_output_aliases={1: 2},
        compiler_params=pltpu.CompilerParams(vmem_limit_bytes=24 * MIB),
        name="pack_rows",
    )(s, s_v, lab_v, heat, zone, kap)


def edge_kernel(own_a, own_b, got_a, got_b, _, edges, zones, rims):
    rows, W = own_a.shape
    L = (rows - ROWS) // 3
    odd = lax.axis_index("tile") % 2 == 1
    for side, exists in enumerate((above_exists(), below_exists())):
        first_swap = odd if side == 0 else jnp.logical_not(odd)
        k_out, k_in = (0, 1) if side == 0 else (3, 2)

        def both_sides(at, n):
            at = pl.ds(at, n)
            other = jnp.where(exists, jnp.where(first_swap, got_a[at, :], got_b[at, :]), 0.0)
            return other, jnp.where(first_swap, own_a[at, :], own_b[at, :])

        for base in range(0, L, ROWS):
            part = pl.ds(base, ROWS)
            s_out, s_in = both_sides(base, ROWS)
            h_out, h_in = both_sides(L + base, ROWS)
            u_out, u_in = both_sides(2 * L + base, ROWS)
            face = (h_in + h_out) * (s_out - s_in)
            t_out, t_in = jnp.where(exists, u_out - face, 0.0), u_in + face
            rims[2 * side, part, :] = s_out
            rims[2 * side + 1, part, :] = h_out
            rims[4 + side, part, :] = t_out
            for i, l in ((0, 0), (1, L - 1)):
                if base <= l < base + ROWS:
                    edges[pl.ds(4 * i + k_out, 1), :] = t_out[l - base : l - base + 1]
                    edges[pl.ds(4 * i + k_in, 1), :] = t_in[l - base : l - base + 1]
        z_out, z_in = both_sides(3 * L, 1)
        for i in range(2):
            zones[pl.ds(4 * i + k_out, 1), :] = z_out
            zones[pl.ds(4 * i + k_in, 1), :] = z_in


def edge_rows(own_a, own_b, got_a, got_b, after):
    rows, W = own_a.shape
    f32 = jnp.float32
    return pl.pallas_call(
        edge_kernel,
        out_shape=(pltpu.VMEM((ROWS, W), f32), pltpu.VMEM((ROWS, W), f32), pltpu.VMEM((6, (rows - ROWS) // 3, W), f32)),
        in_specs=[VMEM] * 4 + [ANY],
        out_specs=[VMEM] * 3,
        compiler_params=pltpu.CompilerParams(vmem_limit_bytes=16 * MIB),
        name="edge_rows",
    )(own_a, own_b, got_a, got_b, after)


def pick(ref, base, l, lanes, row):
    at = base + (l // ROWS) * ROWS
    if not isinstance(l, int):
        at = pl.multiple_of(at, ROWS)
    return pltpu.roll(ref[pl.ds(at, ROWS), lanes], (row - l) % ROWS, 0)


def halo_rows(rims, state, lanes, l):
    end = ROWS - 1
    where = ((state[0], 0), (1, 0), (state[1], end), (3, end))
    return tuple(pick(rims.at[k], 0, l, lanes, row) for k, row in where)


def fill_faces(first, end, h_at, h_out, g_out):
    _, R, W = h_out.shape
    edge = lane_ids() == 0

    def body(l, _):
        before = [0.0] * (R // ROWS)
        for c in range(W // LANES):
            for r in range(R // ROWS):
                at = (l,) + tile(r, c)
                h = h_at(at, c)
                moved = pltpu.roll(h, 1, 1)
                h_out[at] = h
                g_out[at] = h + jnp.where(edge, before[r], moved)
                before[r] = moved
        return 0

    lax.fori_loop(first, end, body, 0)


def from_labels(lab, kap):
    values = splats(kap)
    table, lane = jnp.zeros((ROWS, LANES), jnp.float32), lane_ids()
    for k, value in enumerate(values):
        table = jnp.where(lane == k, value, table)
    return lambda at, c: lookup(table, lab[at]) if c % 4 == 0 else choose(values, lab[at])


def faces_kernel(lab_hbm, kap, h_in, lab_in, _, h_out, g_out, lab, sem):
    L, R, _ = lab.shape
    copies = []
    if R > 2 * ROWS:
        at = pl.ds(3, L - 6), pl.ds(ROWS, R - 2 * ROWS)
        copies = [pltpu.make_async_copy(lab_hbm.at[at], lab.at[at], sem)]
    for copy in copies:
        copy.start()

    def held(at, c):
        return h_out[at]

    getter = from_labels(lab, kap)
    for first, end in ((0, 2), (L - 2, L)):
        fill_faces(first, end, held, h_out, g_out)
    for l in (2, L - 3):
        fill_faces(l, l + 1, getter, h_out, g_out)
    for copy in copies:
        copy.wait()


def faces(lab, kap, h, lab_v, after):
    lab = pltpu.with_memory_space_constraint(lab, pltpu.HBM)
    f32 = jnp.float32
    return pl.pallas_call(
        faces_kernel,
        out_shape=(jax.ShapeDtypeStruct(lab.shape, f32),) * 2 + (jax.ShapeDtypeStruct(lab.shape, jnp.int32),),
        in_specs=[HBM, SMEM, VMEM, VMEM, ANY],
        out_specs=[VMEM] * 3,
        scratch_shapes=[pltpu.SemaphoreType.DMA],
        input_output_aliases={2: 0, 3: 2},
        compiler_params=pltpu.CompilerParams(vmem_limit_bytes=24 * MIB),
        name="faces",
    )(lab, kap, h, lab_v, after)


def more_faces_kernel(lab, kap, h_in, g_in, _, h_out, g_out):
    fill_faces(3, lab.shape[0] - 3, from_labels(lab, kap), h_out, g_out)


def more_faces(lab, kap, h, g, after):
    return pl.pallas_call(
        more_faces_kernel,
        out_shape=(jax.ShapeDtypeStruct(lab.shape, jnp.float32),) * 2,
        in_specs=[VMEM, SMEM, VMEM, VMEM, ANY],
        out_specs=[VMEM] * 2,
        input_output_aliases={2: 0, 3: 1},
        compiler_params=pltpu.CompilerParams(vmem_limit_bytes=24 * MIB),
        name="more_faces",
    )(lab, kap, h, g, after)


def layer_step(l, s_ref, h_ref, g_ref, halo, put):
    _, R, W = s_ref.shape

    def get_s(r, c):
        return s_ref[(l,) + tile(r, c)]

    def get_h(r, c):
        return h_ref[(l,) + tile(r, c)]

    def get_g(r, c):
        return g_ref[(l,) + tile(r, c)]

    def get_z(r, c, s, h):
        a, b = (l - 1,) + tile(r, c), (l + 1,) + tile(r, c)
        return vertical(s, h, s_ref[a], h_ref[a], s_ref[b], h_ref[b])

    stencil(R, W, get_s, get_h, get_z, halo, put, get_g=get_g)


def first_step(l, s_ref, h_ref, g_ref, halo, t):
    def put(r, c, value):
        t[(l,) + tile(r, c)] = value

    layer_step(l, s_ref, h_ref, g_ref, halo, put)


def outer_kernel(s_ref, h_ref, g_ref, rims, t):
    L = s_ref.shape[0]

    def body(p, _):
        l = 1 + p * (L - 3)

        def halo(c):
            return halo_rows(rims, (0, 2), pl.ds(LANES * c, LANES), l)

        first_step(l, s_ref, h_ref, g_ref, halo, t)
        return 0

    lax.fori_loop(0, 2, body, 0)


def outer(s, h, g, rims):
    return pl.pallas_call(
        outer_kernel,
        out_shape=pltpu.VMEM(s.shape, jnp.float32),
        in_specs=[VMEM] * 4,
        out_specs=VMEM,
        compiler_params=pltpu.CompilerParams(vmem_limit_bytes=20 * MIB),
        name="outer",
    )(s, h, g, rims)


def inside_kernel(s_ref, h_ref, g_ref, rims, t_in, _, t):
    L = s_ref.shape[0]

    def body(l, _):
        def halo(c):
            return halo_rows(rims, (0, 2), pl.ds(LANES * c, LANES), l)

        first_step(l, s_ref, h_ref, g_ref, halo, t)
        return 0

    lax.fori_loop(2, L - 2, body, 0)


def inside(s, h, g, rims, t, after):
    return pl.pallas_call(
        inside_kernel,
        out_shape=jax.ShapeDtypeStruct(s.shape, jnp.float32),
        in_specs=[VMEM] * 5 + [ANY],
        out_specs=VMEM,
        input_output_aliases={4: 0},
        compiler_params=pltpu.CompilerParams(vmem_limit_bytes=24 * MIB),
        name="inside",
    )(s, h, g, rims, t, after)


def last_kernel(t_ref, h_ref, g_ref, rims, out, buf, sem):
    L, R, W = t_ref.shape

    def send(l):
        return pltpu.make_async_copy(buf.at[l], out.at[l], sem.at[l])

    def body(l, _):
        def put(r, c, value):
            buf[(l,) + tile(r, c)] = value

        def halo(c):
            return halo_rows(rims, (4, 5), pl.ds(LANES * c, LANES), l)

        layer_step(l, t_ref, h_ref, g_ref, halo, put)
        send(l).start()
        return 0

    lax.fori_loop(1, L - 1, body, 0)

    def drain(l, _):
        send(l).wait()
        return 0

    lax.fori_loop(1, L - 1, drain, 0)


def last_layers(t, h, g, rims):
    L = t.shape[0]
    return pl.pallas_call(
        last_kernel,
        out_shape=jax.ShapeDtypeStruct(t.shape, jnp.float32),
        in_specs=[VMEM] * 4,
        out_specs=HBM,
        scratch_shapes=[pltpu.VMEM(t.shape, jnp.float32), pltpu.SemaphoreType.DMA((L,))],
        compiler_params=pltpu.CompilerParams(vmem_limit_bytes=24 * MIB),
        name="last_layers",
    )(t, h, g, rims)


def near_of(side):
    me = lax.axis_index("tier")
    return (me ^ 1, me ^ 2) if side == 0 else (me ^ 2, me ^ 1)


def routes(tier, tile):
    odd = tile % 2
    return tier ^ (1 + odd), tier ^ (2 - odd)


def entries(tiers):
    me = lax.axis_index("tier")
    if tiers != 4:
        return [(2 * me + i, j) for i in range(2) for j in range(2 * tiers)]
    listed = []
    for side in range(2):
        near, target = near_of(side)
        columns = [2 * me, 2 * me + 1, 2 * near, 2 * near + 1]
        for who in (target, me):
            listed += [(2 * who + i, j) for i in range(2) for j in columns]
    return listed


def rim_entries(tiers):
    me = lax.axis_index("tier")
    return [me ^ q if tiers == 4 else q for q in range(tiers)]


def table_kernel(tiers, ops, table, rim_table):
    regions = ops.shape[0]
    for k, (i, j) in enumerate(entries(tiers)):
        for g in range(regions):
            table[k, g] = jnp.full((ROWS, LANES), ops[g, i, j], jnp.float32)
    lane, upper = lane_ids(), row_ids() < 4
    me = lax.axis_index("tier")
    for q, source in enumerate(rim_entries(tiers)):
        for k in range(2):
            value = jnp.zeros((ROWS, LANES), jnp.float32)
            for g in range(regions):
                a, b = ops[g, 2 * me, 2 * source + k], ops[g, 2 * me + 1, 2 * source + 1 - k]
                value = jnp.where(lane == g, jnp.where(upper, a, b), value)
            rim_table[2 * q + k] = value


def make_tables(tiers, ops):
    regions = ops.shape[0]
    f32 = jnp.float32
    count, rims = 32 if tiers == 4 else 4 * tiers, 2 * tiers
    return pl.pallas_call(
        functools.partial(table_kernel, tiers),
        out_shape=(pltpu.VMEM((count, regions, ROWS, LANES), f32), pltpu.VMEM((rims, ROWS, LANES), f32)),
        in_specs=[SMEM],
        out_specs=[VMEM, VMEM],
        compiler_params=pltpu.CompilerParams(vmem_limit_bytes=16 * MIB),
        name="make_tables",
    )(ops)


def product(table, at, zone, refs, partial, base, put):
    regions = table.shape[1]
    R, W = refs[0][0].shape[1:]
    S = R // ROWS

    def body(c, _):
        lanes = pl.ds(pl.multiple_of(c * LANES, LANES), LANES)
        whole = pl.ds(pl.multiple_of(base + c * LANES, LANES), LANES)
        for r0 in range(0, S, 2):
            rows = [pl.ds(ROWS * r, ROWS) for r in range(r0, min(S, r0 + 2))]
            zones = [zone[x, whole] for x in rows]
            for i in range(2):
                totals = [None] * len(rows)
                for j, (ref, index) in enumerate(refs):
                    values = [table[at + i * len(refs) + j, g] for g in range(regions)]
                    for k, x in enumerate(rows):
                        term = choose(values, zones[k]) * ref[index, x, lanes]
                        totals[k] = term if totals[k] is None else totals[k] + term
                for k, x in enumerate(rows):
                    for ref in partial:
                        totals[k] = totals[k] + ref[i, x, lanes]
                    put(i, x, lanes, whole, totals[k])
        return 0

    lax.fori_loop(0, W // LANES, body, 0)


def both(own, near):
    return [(own, 0), (own, 1), (near, 0), (near, 1)]


def put_in(out):
    def put(i, rows, lanes, whole, value):
        out[i, rows, lanes] = value

    return put


def way_of_tile():
    return lax.axis_index("tile") % 2


def combine_kernel(table, zone, own, near, _, out):
    product(table, 16 * way_of_tile(), zone, both(own, near), [], 0, put_in(out))


def combine(table, zone, own, near, after):
    return pl.pallas_call(
        combine_kernel,
        out_shape=pltpu.VMEM(own.shape, jnp.float32),
        in_specs=[VMEM] * 4 + [ANY],
        out_specs=VMEM,
        compiler_params=pltpu.CompilerParams(vmem_limit_bytes=16 * MIB),
        name="combine",
    )(table, zone, own, near, after)


def rim_product(rim_table, pairs, zones, lanes):
    zones = zones[:, lanes].astype(jnp.int32)
    value = None
    for at, planes in pairs:
        for k, x in enumerate((planes, pltpu.roll(planes, 4, 0))):
            term = lookup(rim_table[at + k], zones) * x
            value = term if value is None else value + term
    return value


def own_kernel(table, zone, own, near, _, base):
    product(table, 16 * way_of_tile() + 8, zone, both(own, near), [], 0, put_in(base))


def own_part(table, zone, own, near, after):
    return pl.pallas_call(
        own_kernel,
        out_shape=pltpu.VMEM(own.shape, jnp.float32),
        in_specs=[VMEM] * 4 + [ANY],
        out_specs=VMEM,
        compiler_params=pltpu.CompilerParams(vmem_limit_bytes=16 * MIB),
        name="own_part",
    )(table, zone, own, near, after)


def bond_kernel(tiers, zone, table, rim_table, rims, heat, h_ref, g_ref, t_in, *refs):
    pairs = tiers == 4
    (edge_zones, *arrays), (t, out, rim) = refs[:-3], refs[-3:]
    L, R, W = t.shape
    C = W // LANES
    row = row_ids()
    if pairs:
        base, part, *edges = arrays

        for i in range(2):
            for r in range(R // ROWS):
                for c in range(C):
                    t[(i * (L - 1),) + tile(r, c)] = base[(i,) + tile(r, c)] + part[(i,) + tile(r, c)]
    else:
        planes, edges = arrays

        def put(i, rows, lanes, whole, value):
            t[i * (L - 1), rows, lanes] = value

        product(table, 0, zone, [(planes, k) for k in range(2 * tiers)], [], 0, put)
    gone = ((row % 4 == 0) & jnp.logical_not(above_exists())) | ((row % 4 == 3) & jnp.logical_not(below_exists()))

    for c in range(C):
        lanes = pl.ds(c * LANES, LANES)
        tiles = [edges[q][:, lanes] if pairs else edges[q, :, lanes] for q in range(tiers)]
        value = rim_product(rim_table, [(2 * q, x) for q, x in enumerate(tiles)], edge_zones, lanes)
        value = jnp.where(gone, 0.0, value)
        rim[:, lanes] = value
        for i in range(2):
            t[i * (L - 1), pl.ds(0, 1), lanes] = value[4 * i + 1 : 4 * i + 2]
            t[i * (L - 1), pl.ds(R - 1, 1), lanes] = value[4 * i + 2 : 4 * i + 3]

    def plane(p, _):
        own, near = p * (L - 1), 1 + p * (L - 3)
        heated = jnp.where(p == 0, 1.0, 0.0)

        def get_s(r, c):
            return t[(own,) + tile(r, c)]

        def get_h(r, c):
            return h_ref[(own,) + tile(r, c)]

        def get_g(r, c):
            return g_ref[(own,) + tile(r, c)]

        def get_z(r, c, s, h):
            at = (near,) + tile(r, c)
            return (h + h_ref[at]) * (t[at] - s) + heated * heat[tile(r, c)]

        def halo(c):
            lanes = pl.ds(LANES * c, LANES)
            ha, hb = pick(rims.at[1], 0, own, lanes, 0), pick(rims.at[3], 0, own, lanes, ROWS - 1)
            return pltpu.roll(rim[:, lanes], (2 - p) * 4 % ROWS, 0), ha, pltpu.roll(rim[:, lanes], 4 - 4 * p, 0), hb

        def put_out(r, c, value):
            out[(p,) + tile(r, c)] = value

        stencil(R, W, get_s, get_h, get_z, halo, put_out, get_g=get_g)
        return 0

    lax.fori_loop(0, 2, plane, 0)


def bond(tiers, zone, tables, rims, heat, h, g, t, edge_zones, arrays):
    _, R, W = t.shape
    args = (zone, *tables, rims, heat, h, g, t, edge_zones, *arrays)
    f32 = jnp.float32
    return pl.pallas_call(
        functools.partial(bond_kernel, tiers),
        out_shape=(
            jax.ShapeDtypeStruct(t.shape, f32),
            jax.ShapeDtypeStruct((2, R, W), f32),
        ),
        in_specs=[VMEM] * len(args),
        out_specs=[VMEM] * 2,
        scratch_shapes=[pltpu.VMEM((ROWS, W), f32)],
        input_output_aliases={7: 0},
        compiler_params=pltpu.CompilerParams(vmem_limit_bytes=24 * MIB),
        name="bond",
    )(*args)


def final_kernel(tiers, zone, table, *refs):
    arrays, (_, out, buf, sem) = refs[:-4], refs[-4:]
    L, R, W = out.shape

    def put(i, rows, lanes, whole, value):
        buf[i, rows, lanes] = value

    if tiers != 4:
        product(table, 0, zone, [(arrays[0], k) for k in range(2 * tiers)], [], 0, put)
    copies = []
    for i in range(2):
        if tiers == 4:
            base, part = arrays
            for r in range(R // ROWS):
                for c in range(W // LANES):
                    buf[(i,) + tile(r, c)] = base[(i,) + tile(r, c)] + part[(i,) + tile(r, c)]
        copies.append(pltpu.make_async_copy(buf.at[i], out.at[i * (L - 1)], sem.at[i]))
        copies[i].start()
    for copy in copies:
        copy.wait()


def final_planes(tiers, zone, table, arrays, out):
    args = (zone, table, *arrays, out)
    _, R, W = out.shape
    return pl.pallas_call(
        functools.partial(final_kernel, tiers),
        out_shape=jax.ShapeDtypeStruct(out.shape, jnp.float32),
        in_specs=[VMEM] * (len(args) - 1) + [HBM],
        out_specs=HBM,
        scratch_shapes=[pltpu.VMEM((2, R, W), jnp.float32), pltpu.SemaphoreType.DMA((2,))],
        input_output_aliases={len(args) - 1: 0},
        compiler_params=pltpu.CompilerParams(vmem_limit_bytes=16 * MIB),
        name="final_planes",
    )(*args)


def across(value, bits, tiers):
    return lax.ppermute(value, "tier", [(i, i ^ bits) for i in range(tiers)])


def every(value, tiers):
    gathered = lax.all_gather(value, "tier", axis=0, tiled=False)
    return gathered.reshape((tiers * value.shape[0],) + value.shape[1:]) if value.ndim == 3 else gathered


def along(value, way, tiers, tiles):
    places = [(tier, tile) for tier in range(tiers) for tile in range(tiles)]
    pairs = [(tier * tiles + tile, routes(tier, tile)[way] * tiles + tile) for tier, tile in places]
    return lax.ppermute(value, ("tier", "tile"), pairs)


def exchange(tiers, tiles, table, zone, planes, after):
    if tiers != 4:
        return (every(planes, tiers),), planes
    near = along(planes, 0, tiers, tiles)
    total = combine(table, zone, planes, near, after)
    return (own_part(table, zone, planes, near, total), along(total, 1, tiers, tiles)), total


def local(warming, substance, zone, patch, kap, power, ops):
    tiers, tiles = lax.axis_size("tier"), lax.axis_size("tile")
    s, lab, patch = warming[0], substance[0], patch[0]

    planes, heat, s_v, lab_v, h = begin(s, lab, patch, kap, power)
    swap_a, swap_b, s = pack_rows(s, s_v, lab_v, heat, zone, kap)
    pairs = [(i, i ^ 1) for i in range(tiles) if i ^ 1 < tiles]
    got_a = lax.ppermute(swap_a, "tile", pairs)
    pairs = [(i, ((i - 1) ^ 1) + 1) for i in range(1, tiles - 1 + tiles % 2)]
    got_b = lax.ppermute(swap_b, "tile", pairs)
    tables = make_tables(tiers, ops)
    h, g, lab = faces(lab, kap, h, lab_v, swap_a)
    arrays, _ = exchange(tiers, tiles, tables[0], zone, planes, h)
    edges, edge_zones, rims = edge_rows(swap_a, swap_b, got_a, got_b, h)
    h, g = more_faces(lab, kap, h, g, edges)
    if tiers == 4:
        edges = (edges, *(across(edges, bits, tiers) for bits in (1, 2, 3)))
    else:
        edges = (every(edges, tiers),)
    t = outer(s, h, g, rims)
    t, planes = bond(tiers, zone, tables, rims, heat, h, g, t, edge_zones, (*arrays, *edges))
    t = inside(s, h, g, rims, t, planes)
    arrays, _ = exchange(tiers, tiles, tables[0], zone, planes, t)
    out = last_layers(t, h, g, rims)
    out = final_planes(tiers, zone, tables[0], arrays, out)
    return out[None]


def solution(mesh):
    in_specs = (
        P("tier", None, "tile", None),
        P("tier", None, "tile", None),
        P("tile", None),
        P("tier", "tile", None),
        P(),
        P("tier", None),
        P(),
    )
    out_specs = P("tier", None, "tile", None)
    return jax.shard_map(local, mesh=mesh, in_specs=in_specs, out_specs=out_specs, check_vma=False)
```

```python
import functools
import math

import jax
import jax.numpy as jnp
from jax import lax
from jax.experimental import pallas as pl
from jax.experimental.pallas import tpu as pltpu
from jax.sharding import PartitionSpec as P

STEPS = 2
step_dt = 0.04
half_dt = 0.5 * step_dt
LANES = 128
ROWS = 8
MIB = 1 << 20

VMEM = pl.BlockSpec(memory_space=pltpu.VMEM)
SMEM = pl.BlockSpec(memory_space=pltpu.SMEM)
ANY = pl.BlockSpec(memory_space=pl.ANY)
HBM = pl.BlockSpec(memory_space=pltpu.HBM)


def tile(r, c):
    return pl.ds(ROWS * r, ROWS), pl.ds(LANES * c, LANES)


def lane_ids():
    return lax.broadcasted_iota(jnp.int32, (ROWS, LANES), 1)


def row_ids():
    return lax.broadcasted_iota(jnp.int32, (ROWS, LANES), 0)


def choose(values, labels):
    values, bit = list(values), 1
    while len(values) > 1:
        odd = (labels & bit) != 0
        paired = [
            jnp.where(odd, values[i + 1], values[i]) if i + 1 < len(values) else values[i]
            for i in range(0, len(values), 2)
        ]
        values, bit = paired, 2 * bit
    return values[0]


def lookup(row, labels):
    return jnp.take_along_axis(row, labels, axis=1, mode="promise_in_bounds")


def splats(kap):
    return [jnp.full((ROWS, LANES), half_dt * kap[i], jnp.float32) for i in range(kap.shape[0])]


def stencil(R, W, get_s, get_h, get_z, halo, put, get_g=None, put_g=None):
    C, S = W // LANES, R // ROWS
    lane, row = lane_ids(), row_ids()
    first, last = lane == 0, lane == LANES - 1
    top, bottom = row == 0, row == ROWS - 1
    before = None
    for c in range(C):
        s = [get_s(r, c) for r in range(S)]
        h = [get_h(r, c) for r in range(S)]
        rs = [pltpu.roll(v, 1, 1) for v in s]
        rh = [pltpu.roll(v, 1, 1) for v in h] if get_g is None else None
        us = [pltpu.roll(v, 1, 0) for v in s]
        uh = [pltpu.roll(v, 1, 0) for v in h]
        if halo is not None:
            sa, ha, sb, hb = halo(c)
        acc, back, down = [], [], []
        for r in range(S):
            sl = jnp.where(first, 0.0 if c == 0 else before[0][r], rs[r])
            if get_g is None:
                g = h[r] + jnp.where(first, 0.0 if c == 0 else before[1][r], rh[r])
                if put_g is not None:
                    put_g(r, c, g)
            else:
                g = get_g(r, c)
            face = g * (sl - s[r])
            back.append(pltpu.roll(face, LANES - 1, 1))
            if r == 0:
                if halo is None:
                    su, hu = us[0], uh[0]
                else:
                    su, hu = jnp.where(top, sa, us[0]), jnp.where(top, ha, uh[0])
            else:
                su, hu = jnp.where(top, us[r - 1], us[r]), jnp.where(top, uh[r - 1], uh[r])
            upper = (h[r] + hu) * (su - s[r])
            down.append(pltpu.roll(upper, ROWS - 1, 0))
            acc.append((s[r] + get_z(r, c, s[r], h[r])) + (face + upper))
        for r in range(S):
            if r + 1 < S:
                lower = jnp.where(bottom, down[r + 1], down[r])
            elif halo is None:
                lower = down[r]
            else:
                lower = jnp.where(bottom, (h[r] + hb) * (s[r] - sb), down[r])
            acc[r] = acc[r] - lower
        if before is not None:
            for r in range(S):
                put(r, c - 1, before[3][r] - jnp.where(last, back[r], before[2][r]))
        before = (rs, rh, back, acc, s, h)
    for r in range(S):
        out = before[5][r] * before[4][r]
        put(r, C - 1, before[3][r] - jnp.where(last, out, before[2][r]))


def vertical(s, h, s_up, h_up, s_down, h_down):
    return (h + h_up) * (s_up - s) + (h + h_down) * (s_down - s)


def collect(row, pieces):
    value = None
    for q, (source_tile, source) in enumerate(pieces):
        moved = source_tile if q == source else pltpu.roll(source_tile, (q - source) % ROWS, 0)
        value = moved if value is None else jnp.where(row == q, moved, value)
    return value


def begin_kernel(
    s_hbm, lab_hbm, patch_hbm, kap_hbm, power_hbm,
    planes, heat, s_v, lab_v, h_out,
    patch, kap, power, sem,
):
    L, R, W = s_hbm.shape
    C = W // LANES
    small = [
        pltpu.make_async_copy(kap_hbm, kap, sem.at[0]),
        pltpu.make_async_copy(power_hbm, power, sem.at[1]),
        pltpu.make_async_copy(patch_hbm, patch, sem.at[2]),
    ]
    places = [pl.ds(0, 2), pl.ds(L - 2, 2), pl.ds(2, 1), pl.ds(L - 3, 1)]
    places += [(pl.ds(3, L - 6), pl.ds(row, ROWS)) for row in sorted({0, R - ROWS})]
    layers = [
        [
            pltpu.make_async_copy(s_hbm.at[at], s_v.at[at], sem.at[3 + 2 * k]),
            pltpu.make_async_copy(lab_hbm.at[at], lab_v.at[at], sem.at[4 + 2 * k]),
        ]
        for k, at in enumerate(places)
    ]
    layers = layers[:2] + [sum(layers[2:], [])]
    for copy in small + layers[0] + layers[1] + layers[2]:
        copy.start()
    for copy in small:
        copy.wait()
    values = splats(kap)
    heats = step_dt * jnp.broadcast_to(power[...], (ROWS, LANES))

    for c in range(C):
        for r in range(R // ROWS):
            heat[tile(r, c)] = lookup(heats, patch[tile(r, c)])
    for copy in layers[0]:
        copy.wait()

    def plane(p, _):
        own, near = p * (L - 1), 1 + p * (L - 3)
        heated = jnp.where(p == 0, 1.0, 0.0)

        @pl.when(p == 1)
        def _():
            for copy in layers[1]:
                copy.wait()

        def get_s(r, c):
            return s_v[(own,) + tile(r, c)]

        def get_h(r, c):
            value = choose(values, lab_v[(own,) + tile(r, c)])
            h_out[(own,) + tile(r, c)] = value
            return value

        def get_z(r, c, s, h):
            h_near = choose(values, lab_v[(near,) + tile(r, c)])
            h_out[(near,) + tile(r, c)] = h_near
            return (h + h_near) * (s_v[(near,) + tile(r, c)] - s) + heated * heat[tile(r, c)]

        def put(r, c, value):
            planes[(p,) + tile(r, c)] = value

        stencil(R, W, get_s, get_h, get_z, None, put)
        return 0

    lax.fori_loop(0, 2, plane, 0)
    for copy in layers[2]:
        copy.wait()


def begin(s, lab, patch, kap, power):
    _, R, W = s.shape
    f32, i32 = jnp.float32, jnp.int32
    args = [pltpu.with_memory_space_constraint(x, pltpu.HBM) for x in (s, lab, patch, kap, power)]
    return pl.pallas_call(
        begin_kernel,
        out_shape=(
            pltpu.VMEM((2, R, W), f32), pltpu.VMEM((R, W), f32), pltpu.VMEM(s.shape, f32), pltpu.VMEM(lab.shape, i32),
            pltpu.VMEM(s.shape, f32),
        ),
        in_specs=[HBM] * 5,
        out_specs=[VMEM] * 5,
        scratch_shapes=[
            pltpu.VMEM((R, W), i32),
            pltpu.SMEM(kap.shape, f32),
            pltpu.VMEM(power.shape, f32),
            pltpu.SemaphoreType.DMA((15,)),
        ],
        compiler_params=pltpu.CompilerParams(vmem_limit_bytes=16 * MIB),
        name="begin",
    )(*args)


def above_exists():
    return lax.axis_index("tile") > 0


def below_exists():
    return lax.axis_index("tile") < lax.axis_size("tile") - 1


def pack_kernel(
    s_hbm, s_in, lab, heat, zone, kap, swap_a, swap_b, s, rows_v, next_v, sem
):
    L, R, W = s.shape
    C = W // LANES
    copies = []
    if R > 2 * ROWS:
        at = pl.ds(3, L - 6), pl.ds(ROWS, R - 2 * ROWS)
        copies = [pltpu.make_async_copy(s_hbm.at[at], s.at[at], sem)]
    for copy in copies:
        copy.start()
    row = row_ids()
    values = splats(kap)
    group = math.gcd(C, 4)

    def body(first, _):
        for c in (group * first + n for n in range(group)):
            lanes = pl.ds(pl.multiple_of(c * LANES, LANES), LANES)
            for k, (start, at_edge, inwards) in enumerate(((0, 0, 1), (R - ROWS, ROWS - 1, ROWS - 2))):
                edge = pl.ds(start, ROWS)
                for base in range(0, L, ROWS):
                    for ref, at in ((s, 0), (lab, L)):
                        tiles = [ref[base + q, edge, lanes] for q in range(ROWS)]
                        for out, source in ((rows_v, at_edge), (next_v, inwards)):
                            packed = collect(row, [(x, source) for x in tiles])
                            if ref is lab:
                                packed = choose(values, packed)
                            out[k, pl.ds(at + base, ROWS), lanes] = packed
                zones = zone[edge, lanes].astype(jnp.float32)
                rows_v[k, pl.ds(3 * L, ROWS), lanes] = collect(row, [(zones, at_edge), (heat[edge, lanes], at_edge)])
        return 0

    lax.fori_loop(0, C // group, body, 0)

    def side(k, _):
        def at(base, r, c):
            return k, pl.ds(base + ROWS * r, ROWS), pl.ds(LANES * c, LANES)

        def get_s(r, c):
            return rows_v[at(0, r, c)]

        def get_h(r, c):
            return rows_v[at(L, r, c)]

        def get_z(r, c, s, h):
            flow = (h + next_v[at(L, r, c)]) * (next_v[at(0, r, c)] - s)
            if r == 0:
                flow = flow + jnp.where(row == 0, pltpu.roll(rows_v[at(3 * L, 0, c)], ROWS - 1, 0), 0.0)
            return flow

        def ends(c):
            last = L // ROWS - 1
            return get_s(0, c), get_h(0, c), get_s(last, c), get_h(last, c)

        def put(r, c, value):
            rows_v[at(2 * L, r, c)] = value

        stencil(L, W, get_s, get_h, get_z, ends, put)
        return 0

    lax.fori_loop(0, 2, side, 0)
    odd = lax.axis_index("tile") % 2

    for r in range(swap_a.shape[0] // ROWS):
        for c in range(C):
            swap_a[tile(r, c)] = rows_v[(1 - odd,) + tile(r, c)]
            swap_b[tile(r, c)] = rows_v[(odd,) + tile(r, c)]
    for copy in copies:
        copy.wait()


def pack_rows(s, s_v, lab_v, heat, zone, kap):
    L, _, W = s.shape
    f32 = jnp.float32
    rows = 3 * L + ROWS
    s = pltpu.with_memory_space_constraint(s, pltpu.HBM)
    return pl.pallas_call(
        pack_kernel,
        out_shape=(
            pltpu.VMEM((rows, W), f32),
            pltpu.VMEM((rows, W), f32),
            jax.ShapeDtypeStruct(s.shape, f32),
        ),
        in_specs=[HBM] + [VMEM] * 4 + [SMEM],
        out_specs=[VMEM] * 3,
        scratch_shapes=[
            pltpu.VMEM((2, rows, W), f32),
            pltpu.VMEM((2, 2 * L, W), f32),
            pltpu.SemaphoreType.DMA,
        ],
        input_output_aliases={1: 2},
        compiler_params=pltpu.CompilerParams(vmem_limit_bytes=24 * MIB),
        name="pack_rows",
    )(s, s_v, lab_v, heat, zone, kap)


def edge_kernel(own_a, own_b, got_a, got_b, _, edges, zones, rims):
    rows, W = own_a.shape
    L = (rows - ROWS) // 3
    odd = lax.axis_index("tile") % 2 == 1
    for side, exists in enumerate((above_exists(), below_exists())):
        first_swap = odd if side == 0 else jnp.logical_not(odd)
        k_out, k_in = (0, 1) if side == 0 else (3, 2)

        def both_sides(at, n):
            at = pl.ds(at, n)
            other = jnp.where(exists, jnp.where(first_swap, got_a[at, :], got_b[at, :]), 0.0)
            return other, jnp.where(first_swap, own_a[at, :], own_b[at, :])

        for base in range(0, L, ROWS):
            part = pl.ds(base, ROWS)
            s_out, s_in = both_sides(base, ROWS)
            h_out, h_in = both_sides(L + base, ROWS)
            u_out, u_in = both_sides(2 * L + base, ROWS)
            face = (h_in + h_out) * (s_out - s_in)
            t_out, t_in = jnp.where(exists, u_out - face, 0.0), u_in + face
            rims[2 * side, part, :] = s_out
            rims[2 * side + 1, part, :] = h_out
            rims[4 + side, part, :] = t_out
            for i, l in ((0, 0), (1, L - 1)):
                if base <= l < base + ROWS:
                    edges[pl.ds(4 * i + k_out, 1), :] = t_out[l - base : l - base + 1]
                    edges[pl.ds(4 * i + k_in, 1), :] = t_in[l - base : l - base + 1]
        z_out, z_in = both_sides(3 * L, 1)
        for i in range(2):
            zones[pl.ds(4 * i + k_out, 1), :] = z_out
            zones[pl.ds(4 * i + k_in, 1), :] = z_in


def edge_rows(own_a, own_b, got_a, got_b, after):
    rows, W = own_a.shape
    f32 = jnp.float32
    return pl.pallas_call(
        edge_kernel,
        out_shape=(pltpu.VMEM((ROWS, W), f32), pltpu.VMEM((ROWS, W), f32), pltpu.VMEM((6, (rows - ROWS) // 3, W), f32)),
        in_specs=[VMEM] * 4 + [ANY],
        out_specs=[VMEM] * 3,
        compiler_params=pltpu.CompilerParams(vmem_limit_bytes=16 * MIB),
        name="edge_rows",
    )(own_a, own_b, got_a, got_b, after)


def pick(ref, base, l, lanes, row):
    at = base + (l // ROWS) * ROWS
    if not isinstance(l, int):
        at = pl.multiple_of(at, ROWS)
    return pltpu.roll(ref[pl.ds(at, ROWS), lanes], (row - l) % ROWS, 0)


def halo_rows(rims, state, lanes, l):
    end = ROWS - 1
    where = ((state[0], 0), (1, 0), (state[1], end), (3, end))
    return tuple(pick(rims.at[k], 0, l, lanes, row) for k, row in where)


def fill_faces(first, end, h_at, h_out, g_out):
    _, R, W = h_out.shape
    edge = lane_ids() == 0

    def body(l, _):
        before = [0.0] * (R // ROWS)
        for c in range(W // LANES):
            for r in range(R // ROWS):
                at = (l,) + tile(r, c)
                h = h_at(at, c)
                moved = pltpu.roll(h, 1, 1)
                h_out[at] = h
                g_out[at] = h + jnp.where(edge, before[r], moved)
                before[r] = moved
        return 0

    lax.fori_loop(first, end, body, 0)


def from_labels(lab, kap):
    values = splats(kap)
    table, lane = jnp.zeros((ROWS, LANES), jnp.float32), lane_ids()
    for k, value in enumerate(values):
        table = jnp.where(lane == k, value, table)
    return lambda at, c: lookup(table, lab[at]) if c % 4 == 0 else choose(values, lab[at])


def faces_kernel(lab_hbm, kap, h_in, lab_in, _, h_out, g_out, lab, sem):
    L, R, _ = lab.shape
    copies = []
    if R > 2 * ROWS:
        at = pl.ds(3, L - 6), pl.ds(ROWS, R - 2 * ROWS)
        copies = [pltpu.make_async_copy(lab_hbm.at[at], lab.at[at], sem)]
    for copy in copies:
        copy.start()

    def held(at, c):
        return h_out[at]

    getter = from_labels(lab, kap)
    for first, end in ((0, 2), (L - 2, L)):
        fill_faces(first, end, held, h_out, g_out)
    for l in (2, L - 3):
        fill_faces(l, l + 1, getter, h_out, g_out)
    for copy in copies:
        copy.wait()


def faces(lab, kap, h, lab_v, after):
    lab = pltpu.with_memory_space_constraint(lab, pltpu.HBM)
    f32 = jnp.float32
    return pl.pallas_call(
        faces_kernel,
        out_shape=(jax.ShapeDtypeStruct(lab.shape, f32),) * 2 + (jax.ShapeDtypeStruct(lab.shape, jnp.int32),),
        in_specs=[HBM, SMEM, VMEM, VMEM, ANY],
        out_specs=[VMEM] * 3,
        scratch_shapes=[pltpu.SemaphoreType.DMA],
        input_output_aliases={2: 0, 3: 2},
        compiler_params=pltpu.CompilerParams(vmem_limit_bytes=24 * MIB),
        name="faces",
    )(lab, kap, h, lab_v, after)


def more_faces_kernel(lab, kap, h_in, g_in, _, h_out, g_out):
    fill_faces(3, lab.shape[0] - 3, from_labels(lab, kap), h_out, g_out)


def more_faces(lab, kap, h, g, after):
    return pl.pallas_call(
        more_faces_kernel,
        out_shape=(jax.ShapeDtypeStruct(lab.shape, jnp.float32),) * 2,
        in_specs=[VMEM, SMEM, VMEM, VMEM, ANY],
        out_specs=[VMEM] * 2,
        input_output_aliases={2: 0, 3: 1},
        compiler_params=pltpu.CompilerParams(vmem_limit_bytes=24 * MIB),
        name="more_faces",
    )(lab, kap, h, g, after)


def layer_step(l, s_ref, h_ref, g_ref, halo, put):
    _, R, W = s_ref.shape

    def get_s(r, c):
        return s_ref[(l,) + tile(r, c)]

    def get_h(r, c):
        return h_ref[(l,) + tile(r, c)]

    def get_g(r, c):
        return g_ref[(l,) + tile(r, c)]

    def get_z(r, c, s, h):
        a, b = (l - 1,) + tile(r, c), (l + 1,) + tile(r, c)
        return vertical(s, h, s_ref[a], h_ref[a], s_ref[b], h_ref[b])

    stencil(R, W, get_s, get_h, get_z, halo, put, get_g=get_g)


def first_step(l, s_ref, h_ref, g_ref, halo, t):
    def put(r, c, value):
        t[(l,) + tile(r, c)] = value

    layer_step(l, s_ref, h_ref, g_ref, halo, put)


def outer_kernel(s_ref, h_ref, g_ref, rims, t):
    L = s_ref.shape[0]

    def body(p, _):
        l = 1 + p * (L - 3)

        def halo(c):
            return halo_rows(rims, (0, 2), pl.ds(LANES * c, LANES), l)

        first_step(l, s_ref, h_ref, g_ref, halo, t)
        return 0

    lax.fori_loop(0, 2, body, 0)


def outer(s, h, g, rims):
    return pl.pallas_call(
        outer_kernel,
        out_shape=pltpu.VMEM(s.shape, jnp.float32),
        in_specs=[VMEM] * 4,
        out_specs=VMEM,
        compiler_params=pltpu.CompilerParams(vmem_limit_bytes=20 * MIB),
        name="outer",
    )(s, h, g, rims)


def inside_kernel(s_ref, h_ref, g_ref, rims, t_in, _, t):
    L = s_ref.shape[0]

    def body(l, _):
        def halo(c):
            return halo_rows(rims, (0, 2), pl.ds(LANES * c, LANES), l)

        first_step(l, s_ref, h_ref, g_ref, halo, t)
        return 0

    lax.fori_loop(2, L - 2, body, 0)


def inside(s, h, g, rims, t, after):
    return pl.pallas_call(
        inside_kernel,
        out_shape=jax.ShapeDtypeStruct(s.shape, jnp.float32),
        in_specs=[VMEM] * 5 + [ANY],
        out_specs=VMEM,
        input_output_aliases={4: 0},
        compiler_params=pltpu.CompilerParams(vmem_limit_bytes=24 * MIB),
        name="inside",
    )(s, h, g, rims, t, after)


def last_kernel(t_ref, h_ref, g_ref, rims, out, buf, sem):
    L, R, W = t_ref.shape

    def send(l):
        return pltpu.make_async_copy(buf.at[l], out.at[l], sem.at[l])

    def body(l, _):
        def put(r, c, value):
            buf[(l,) + tile(r, c)] = value

        def halo(c):
            return halo_rows(rims, (4, 5), pl.ds(LANES * c, LANES), l)

        layer_step(l, t_ref, h_ref, g_ref, halo, put)
        send(l).start()
        return 0

    lax.fori_loop(1, L - 1, body, 0)

    def drain(l, _):
        send(l).wait()
        return 0

    lax.fori_loop(1, L - 1, drain, 0)


def last_layers(t, h, g, rims):
    L = t.shape[0]
    return pl.pallas_call(
        last_kernel,
        out_shape=jax.ShapeDtypeStruct(t.shape, jnp.float32),
        in_specs=[VMEM] * 4,
        out_specs=HBM,
        scratch_shapes=[pltpu.VMEM(t.shape, jnp.float32), pltpu.SemaphoreType.DMA((L,))],
        compiler_params=pltpu.CompilerParams(vmem_limit_bytes=24 * MIB),
        name="last_layers",
    )(t, h, g, rims)


def near_of(side):
    me = lax.axis_index("tier")
    return (me ^ 1, me ^ 2) if side == 0 else (me ^ 2, me ^ 1)


def routes(tier, tile):
    odd = tile % 2
    return tier ^ (1 + odd), tier ^ (2 - odd)


def entries(tiers):
    me = lax.axis_index("tier")
    if tiers != 4:
        return [(2 * me + i, j) for i in range(2) for j in range(2 * tiers)]
    listed = []
    for side in range(2):
        near, target = near_of(side)
        columns = [2 * me, 2 * me + 1, 2 * near, 2 * near + 1]
        for who in (target, me):
            listed += [(2 * who + i, j) for i in range(2) for j in columns]
    return listed


def rim_entries(tiers):
    me = lax.axis_index("tier")
    return [me ^ q if tiers == 4 else q for q in range(tiers)]


def table_kernel(tiers, ops, table, rim_table):
    regions = ops.shape[0]
    for k, (i, j) in enumerate(entries(tiers)):
        for g in range(regions):
            table[k, g] = jnp.full((ROWS, LANES), ops[g, i, j], jnp.float32)
    lane, upper = lane_ids(), row_ids() < 4
    me = lax.axis_index("tier")
    for q, source in enumerate(rim_entries(tiers)):
        for k in range(2):
            value = jnp.zeros((ROWS, LANES), jnp.float32)
            for g in range(regions):
                a, b = ops[g, 2 * me, 2 * source + k], ops[g, 2 * me + 1, 2 * source + 1 - k]
                value = jnp.where(lane == g, jnp.where(upper, a, b), value)
            rim_table[2 * q + k] = value


def make_tables(tiers, ops):
    regions = ops.shape[0]
    f32 = jnp.float32
    count, rims = 32 if tiers == 4 else 4 * tiers, 2 * tiers
    return pl.pallas_call(
        functools.partial(table_kernel, tiers),
        out_shape=(pltpu.VMEM((count, regions, ROWS, LANES), f32), pltpu.VMEM((rims, ROWS, LANES), f32)),
        in_specs=[SMEM],
        out_specs=[VMEM, VMEM],
        compiler_params=pltpu.CompilerParams(vmem_limit_bytes=16 * MIB),
        name="make_tables",
    )(ops)


def product(table, at, zone, refs, partial, base, put):
    regions = table.shape[1]
    R, W = refs[0][0].shape[1:]
    S = R // ROWS

    group = math.gcd(W // LANES, 2)

    def column(c):
        lanes = pl.ds(pl.multiple_of(c * LANES, LANES), LANES)
        whole = pl.ds(pl.multiple_of(base + c * LANES, LANES), LANES)
        for r0 in range(0, S, 2):
            rows = [pl.ds(ROWS * r, ROWS) for r in range(r0, min(S, r0 + 2))]
            zones = [zone[x, whole] for x in rows]
            for i in range(2):
                totals = [None] * len(rows)
                for j, (ref, index) in enumerate(refs):
                    values = [table[at + i * len(refs) + j, g] for g in range(regions)]
                    for k, x in enumerate(rows):
                        term = choose(values, zones[k]) * ref[index, x, lanes]
                        totals[k] = term if totals[k] is None else totals[k] + term
                for k, x in enumerate(rows):
                    for ref in partial:
                        totals[k] = totals[k] + ref[i, x, lanes]
                    put(i, x, lanes, whole, totals[k])

    def body(first, _):
        for n in range(group):
            column(group * first + n)
        return 0

    lax.fori_loop(0, W // LANES // group, body, 0)


def both(own, near):
    return [(own, 0), (own, 1), (near, 0), (near, 1)]


def put_in(out):
    def put(i, rows, lanes, whole, value):
        out[i, rows, lanes] = value

    return put


def way_of_tile():
    return lax.axis_index("tile") % 2


def combine_kernel(table, zone, own, near, _, out):
    product(table, 16 * way_of_tile(), zone, both(own, near), [], 0, put_in(out))


def combine(table, zone, own, near, after):
    return pl.pallas_call(
        combine_kernel,
        out_shape=pltpu.VMEM(own.shape, jnp.float32),
        in_specs=[VMEM] * 4 + [ANY],
        out_specs=VMEM,
        compiler_params=pltpu.CompilerParams(vmem_limit_bytes=16 * MIB),
        name="combine",
    )(table, zone, own, near, after)


def rim_product(rim_table, pairs, zones, lanes):
    zones = zones[:, lanes].astype(jnp.int32)
    value = None
    for at, planes in pairs:
        for k, x in enumerate((planes, pltpu.roll(planes, 4, 0))):
            term = lookup(rim_table[at + k], zones) * x
            value = term if value is None else value + term
    return value


def own_kernel(table, zone, own, near, _, base):
    product(table, 16 * way_of_tile() + 8, zone, both(own, near), [], 0, put_in(base))


def own_part(table, zone, own, near, after):
    return pl.pallas_call(
        own_kernel,
        out_shape=pltpu.VMEM(own.shape, jnp.float32),
        in_specs=[VMEM] * 4 + [ANY],
        out_specs=VMEM,
        compiler_params=pltpu.CompilerParams(vmem_limit_bytes=16 * MIB),
        name="own_part",
    )(table, zone, own, near, after)


def bond_kernel(tiers, zone, table, rim_table, rims, heat, h_ref, g_ref, t_in, *refs):
    pairs = tiers == 4
    (edge_zones, *arrays), (t, out, rim) = refs[:-3], refs[-3:]
    L, R, W = t.shape
    C = W // LANES
    row = row_ids()
    if pairs:
        base, part, *edges = arrays

        for i in range(2):
            for r in range(R // ROWS):
                for c in range(C):
                    t[(i * (L - 1),) + tile(r, c)] = base[(i,) + tile(r, c)] + part[(i,) + tile(r, c)]
    else:
        planes, edges = arrays

        def put(i, rows, lanes, whole, value):
            t[i * (L - 1), rows, lanes] = value

        product(table, 0, zone, [(planes, k) for k in range(2 * tiers)], [], 0, put)
    gone = ((row % 4 == 0) & jnp.logical_not(above_exists())) | ((row % 4 == 3) & jnp.logical_not(below_exists()))

    for c in range(C):
        lanes = pl.ds(c * LANES, LANES)
        tiles = [edges[q][:, lanes] if pairs else edges[q, :, lanes] for q in range(tiers)]
        value = rim_product(rim_table, [(2 * q, x) for q, x in enumerate(tiles)], edge_zones, lanes)
        value = jnp.where(gone, 0.0, value)
        rim[:, lanes] = value
        for i in range(2):
            t[i * (L - 1), pl.ds(0, 1), lanes] = value[4 * i + 1 : 4 * i + 2]
            t[i * (L - 1), pl.ds(R - 1, 1), lanes] = value[4 * i + 2 : 4 * i + 3]

    def plane(p, _):
        own, near = p * (L - 1), 1 + p * (L - 3)
        heated = jnp.where(p == 0, 1.0, 0.0)

        def get_s(r, c):
            return t[(own,) + tile(r, c)]

        def get_h(r, c):
            return h_ref[(own,) + tile(r, c)]

        def get_g(r, c):
            return g_ref[(own,) + tile(r, c)]

        def get_z(r, c, s, h):
            at = (near,) + tile(r, c)
            return (h + h_ref[at]) * (t[at] - s) + heated * heat[tile(r, c)]

        def halo(c):
            lanes = pl.ds(LANES * c, LANES)
            ha, hb = pick(rims.at[1], 0, own, lanes, 0), pick(rims.at[3], 0, own, lanes, ROWS - 1)
            return pltpu.roll(rim[:, lanes], (2 - p) * 4 % ROWS, 0), ha, pltpu.roll(rim[:, lanes], 4 - 4 * p, 0), hb

        def put_out(r, c, value):
            out[(p,) + tile(r, c)] = value

        stencil(R, W, get_s, get_h, get_z, halo, put_out, get_g=get_g)
        return 0

    lax.fori_loop(0, 2, plane, 0)


def bond(tiers, zone, tables, rims, heat, h, g, t, edge_zones, arrays):
    _, R, W = t.shape
    args = (zone, *tables, rims, heat, h, g, t, edge_zones, *arrays)
    f32 = jnp.float32
    return pl.pallas_call(
        functools.partial(bond_kernel, tiers),
        out_shape=(
            jax.ShapeDtypeStruct(t.shape, f32),
            jax.ShapeDtypeStruct((2, R, W), f32),
        ),
        in_specs=[VMEM] * len(args),
        out_specs=[VMEM] * 2,
        scratch_shapes=[pltpu.VMEM((ROWS, W), f32)],
        input_output_aliases={7: 0},
        compiler_params=pltpu.CompilerParams(vmem_limit_bytes=24 * MIB),
        name="bond",
    )(*args)


def final_kernel(tiers, zone, table, *refs):
    arrays, (_, out, buf, sem) = refs[:-4], refs[-4:]
    L, R, W = out.shape

    def put(i, rows, lanes, whole, value):
        buf[i, rows, lanes] = value

    if tiers != 4:
        product(table, 0, zone, [(arrays[0], k) for k in range(2 * tiers)], [], 0, put)
    copies = []
    for i in range(2):
        if tiers == 4:
            base, part = arrays
            for r in range(R // ROWS):
                for c in range(W // LANES):
                    buf[(i,) + tile(r, c)] = base[(i,) + tile(r, c)] + part[(i,) + tile(r, c)]
        copies.append(pltpu.make_async_copy(buf.at[i], out.at[i * (L - 1)], sem.at[i]))
        copies[i].start()
    for copy in copies:
        copy.wait()


def final_planes(tiers, zone, table, arrays, out):
    args = (zone, table, *arrays, out)
    _, R, W = out.shape
    return pl.pallas_call(
        functools.partial(final_kernel, tiers),
        out_shape=jax.ShapeDtypeStruct(out.shape, jnp.float32),
        in_specs=[VMEM] * (len(args) - 1) + [HBM],
        out_specs=HBM,
        scratch_shapes=[pltpu.VMEM((2, R, W), jnp.float32), pltpu.SemaphoreType.DMA((2,))],
        input_output_aliases={len(args) - 1: 0},
        compiler_params=pltpu.CompilerParams(vmem_limit_bytes=16 * MIB),
        name="final_planes",
    )(*args)


def across(value, bits, tiers):
    return lax.ppermute(value, "tier", [(i, i ^ bits) for i in range(tiers)])


def every(value, tiers):
    gathered = lax.all_gather(value, "tier", axis=0, tiled=False)
    return gathered.reshape((tiers * value.shape[0],) + value.shape[1:]) if value.ndim == 3 else gathered


def along(value, way, tiers, tiles):
    places = [(tier, tile) for tier in range(tiers) for tile in range(tiles)]
    pairs = [(tier * tiles + tile, routes(tier, tile)[way] * tiles + tile) for tier, tile in places]
    return lax.ppermute(value, ("tier", "tile"), pairs)


def exchange(tiers, tiles, table, zone, planes, after):
    if tiers != 4:
        return (every(planes, tiers),), planes
    near = along(planes, 0, tiers, tiles)
    total = combine(table, zone, planes, near, after)
    return (own_part(table, zone, planes, near, total), along(total, 1, tiers, tiles)), total


def local(warming, substance, zone, patch, kap, power, ops):
    tiers, tiles = lax.axis_size("tier"), lax.axis_size("tile")
    s, lab, patch = warming[0], substance[0], patch[0]

    planes, heat, s_v, lab_v, h = begin(s, lab, patch, kap, power)
    swap_a, swap_b, s = pack_rows(s, s_v, lab_v, heat, zone, kap)
    pairs = [(i, i ^ 1) for i in range(tiles) if i ^ 1 < tiles]
    got_a = lax.ppermute(swap_a, "tile", pairs)
    pairs = [(i, ((i - 1) ^ 1) + 1) for i in range(1, tiles - 1 + tiles % 2)]
    got_b = lax.ppermute(swap_b, "tile", pairs)
    tables = make_tables(tiers, ops)
    h, g, lab = faces(lab, kap, h, lab_v, swap_a)
    arrays, _ = exchange(tiers, tiles, tables[0], zone, planes, h)
    edges, edge_zones, rims = edge_rows(swap_a, swap_b, got_a, got_b, h)
    h, g = more_faces(lab, kap, h, g, edges)
    if tiers == 4:
        edges = (edges, *(across(edges, bits, tiers) for bits in (1, 2, 3)))
    else:
        edges = (every(edges, tiers),)
    t = outer(s, h, g, rims)
    t, planes = bond(tiers, zone, tables, rims, heat, h, g, t, edge_zones, (*arrays, *edges))
    t = inside(s, h, g, rims, t, planes)
    arrays, _ = exchange(tiers, tiles, tables[0], zone, planes, t)
    out = last_layers(t, h, g, rims)
    out = final_planes(tiers, zone, tables[0], arrays, out)
    return out[None]


def solution(mesh):
    in_specs = (
        P("tier", None, "tile", None),
        P("tier", None, "tile", None),
        P("tile", None),
        P("tier", "tile", None),
        P(),
        P("tier", None),
        P(),
    )
    out_specs = P("tier", None, "tile", None)
    return jax.shard_map(local, mesh=mesh, in_specs=in_specs, out_specs=out_specs, check_vma=False)
```
